32 devices in a mesh: dp: 4 (over y, x), sp: 8 (over z, core).
Axes of the slice: x: 2, y: 2, z: 4, core: 2. Of those that a mesh axis runs over, the one named last changes fastest.
Arguments:
- block_input: bfloat16 [4, 1024, 2048], P('dp', 'sp'), may hold values from -6 to 6
- segments: int32 [4, 1024], P('dp', 'sp'), may hold values from 0 to 4, as said below
- out_grad: bfloat16 [4, 1024, 2048], P('dp', 'sp'), may hold values from -6 to 6
- ln1_gain: bfloat16 [2048], P(('dp', 'sp')), may hold values from 0.5 to 1.5
- ln1_bias: bfloat16 [2048], P(('dp', 'sp')), may hold values from -1 to 1
- w_qkv: bfloat16 [2048, 6144], P(('dp', 'sp')), may hold values from -0.1875 to 0.1875
- b_qkv: bfloat16 [6144], P(('dp', 'sp')), may hold values from -1 to 1
- w_attn_out: bfloat16 [2048, 2048], P(('dp', 'sp')), may hold values from -0.5 to 0.5
- b_attn_out: bfloat16 [2048], P(('dp', 'sp')), may hold values from -1 to 1
- ln2_gain: bfloat16 [2048], P(('dp', 'sp')), may hold values from 0.5 to 1.5
- ln2_bias: bfloat16 [2048], P(('dp', 'sp')), may hold values from -1 to 1
- w_up: bfloat16 [2048, 8192], P(('dp', 'sp')), may hold values from -0.125 to 0.125
- b_up: bfloat16 [8192], P(('dp', 'sp')), may hold values from -1.5 to 1.5
- w_down: bfloat16 [8192, 2048], P(('dp', 'sp')), may hold values from -0.0625 to 0.0625
- b_down: bfloat16 [2048], P(('dp', 'sp')), may hold values from -1 to 1
Outputs:
- block_output: float32 [4, 1024, 2048], P('dp', 'sp')
- input_grad: float32 [4, 1024, 2048], P('dp', 'sp')
- grad_ln1_gain: float32 [2048], P(('dp', 'sp'))
- grad_ln1_bias: float32 [2048], P(('dp', 'sp'))
- grad_w_qkv: float32 [2048, 6144], P(('dp', 'sp'))
- grad_b_qkv: float32 [6144], P(('dp', 'sp'))
- grad_w_attn_out: float32 [2048, 2048], P(('dp', 'sp'))
- grad_b_attn_out: float32 [2048], P(('dp', 'sp'))
- grad_ln2_gain: float32 [2048], P(('dp', 'sp'))
- grad_ln2_bias: float32 [2048], P(('dp', 'sp'))
- grad_w_up: float32 [2048, 8192], P(('dp', 'sp'))
- grad_b_up: float32 [8192], P(('dp', 'sp'))
- grad_w_down: float32 [8192, 2048], P(('dp', 'sp'))
- grad_b_down: float32 [2048], P(('dp', 'sp'))
The draws below stay inside these ranges and needn't reach their ends.
Inputs may be any that keep to these rules, and one draw needn't show every extreme that they name: `segments`: segment numbers never fall along a sequence. In each sequence one document begins within the first 128 tokens and ends within the last 128 tokens; two shorter documents come before it and two after it.
All inputs are finite; a program needn't handle non-finite values.
Results may differ from the reference program's by a relative error of at most 0.012.
Values may be sent and summed in bfloat16 or wider, within the bound.
No kernel may reach another device: no remote copies, remote signals or barrier semaphores. Data moves between devices by JAX's collectives and lax.ppermute only.
A program may use at most 704 MiB of HBM per device.

```python
import math
import jax
import jax.numpy as jnp
from jax import lax

D = 2048
HEADS = 8
HEAD = 256
ROT = 64
FF = 8192
TOK_DEV = 128
SEQS = 4
LENGTH = 1024


def draw_segments(key, part):
    key = jax.random.fold_in(key, 11)
    key_list = jax.random.split(key, 4)
    half_tok = TOK_DEV // 2
    first_cut = jax.random.randint(key_list[0], (SEQS, 1), 1, half_tok + 1)
    second_cut = jax.random.randint(key_list[1], (SEQS, 1), half_tok + 1, TOK_DEV)
    third_cut = LENGTH - TOK_DEV + jax.random.randint(key_list[2], (SEQS, 1), 1, half_tok)
    fourth_cut = LENGTH - jax.random.randint(key_list[3], (SEQS, 1), 1, half_tok)
    positions = jnp.arange(LENGTH, dtype=jnp.int32)[None, :]
    result = (positions >= first_cut).astype(jnp.int32) + (positions >= second_cut).astype(jnp.int32)
    result = result + (positions >= third_cut).astype(jnp.int32) + (positions >= fourth_cut).astype(jnp.int32)
    return result.astype(jnp.int32)


def levels(key, extent, cuts, low, high):
    gain = 1.0
    for axis_at, blocks in cuts:
        steps = jax.random.uniform(jax.random.fold_in(jax.random.fold_in(key, 6), axis_at), (blocks,), jnp.float32, low / len(cuts), high / len(cuts))
        gain = gain * jnp.repeat(jnp.exp(steps), extent[axis_at] // blocks).reshape((-1,) + (1,) * (len(extent) - 1 - axis_at))
    return gain


def scatter_about(stream_key, dims, scale, reach, cuts=(), kind=jnp.bfloat16):
    entries = scale * jax.random.normal(stream_key, dims, jnp.float32)
    if cuts:
        entries = entries * levels(stream_key, dims, cuts, -0.22, 0.18)
    return jnp.clip(entries, -reach, reach).astype(kind)


def setup_inputs(seed: int = 0) -> dict:
    keys = jax.random.split(jax.random.key(seed), 16)
    return {
        "block_input": scatter_about(keys[0], (SEQS, LENGTH, D), 1.0, 6.0, ((0, 4), (1, 8))),
        "segments": draw_segments(jax.random.fold_in(keys[15], 71), 0),
        "out_grad": scatter_about(keys[2], (SEQS, LENGTH, D), 1.0, 6.0, ((0, 4), (1, 8))),
        "ln1_gain": jnp.clip(1.0 + 0.1 * jax.random.normal(keys[3], (D,), jnp.float32), 0.5, 1.5).astype(jnp.bfloat16),
        "ln1_bias": scatter_about(keys[4], (D,), 0.2, 1.0, ((0, 32),)),
        "w_qkv": scatter_about(keys[5], (D, 3 * D), (D // 2) ** -0.5, 0.1875, ((0, 32),)),
        "b_qkv": scatter_about(keys[6], (3 * D,), 0.2, 1.0, ((0, 32),)),
        "w_attn_out": scatter_about(keys[7], (D, D), (D // 16) ** -0.5, 0.5, ((0, 32),)),
        "b_attn_out": scatter_about(keys[8], (D,), 0.2, 1.0, ((0, 32),)),
        "ln2_gain": jnp.clip(1.0 + 0.1 * jax.random.normal(keys[9], (D,), jnp.float32), 0.5, 1.5).astype(jnp.bfloat16),
        "ln2_bias": scatter_about(keys[10], (D,), 0.2, 1.0, ((0, 32),)),
        "w_up": scatter_about(keys[11], (D, FF), D ** -0.5, 0.125, ((0, 32),)),
        "b_up": scatter_about(keys[12], (FF,), 0.3, 1.5, ((0, 32),)),
        "w_down": scatter_about(keys[13], (FF, D), FF ** -0.5, 0.0625, ((0, 32),)),
        "b_down": scatter_about(keys[14], (D,), 0.2, 1.0, ((0, 32),)),
    }


@jax.custom_vjp
def low(v):
    return lax.optimization_barrier(v.astype(jnp.bfloat16)).astype(jnp.float32)

@jax.custom_vjp
def low_back(v):
    return v

def low_keep(v):
    return (low(v), None)

def low_pass(kept, grad):
    return (grad,)

def back_keep(v):
    return (v, None)

def back_low(kept, grad):
    return (low(grad),)
low.defvjp(low_keep, low_pass)
low_back.defvjp(back_keep, back_low)
precise = lax.Precision.HIGHEST

def matmul(left, right):
    return jnp.dot(left, right, preferred_element_type=jnp.float32, precision=precise)

def norm_layer(values, gain_vec, shift_vec):
    center = values - lax.optimization_barrier(jnp.mean(values, axis=-1, keepdims=True))
    spread = lax.optimization_barrier(jnp.mean(center * center, axis=-1, keepdims=True))
    return center * lax.rsqrt(spread + 1e-05) * gain_vec + shift_vec

def rotary_tables(positions):
    inverse_freq = 10000.0 ** (-jnp.arange(0, ROT, 2).astype(jnp.float32) / ROT)
    angles = positions[:, None] * inverse_freq[None, :]
    angles = jnp.concatenate([angles, angles], axis=1)
    return (jnp.cos(angles), jnp.sin(angles))

def rotate(values, cosine, sine):
    half_rot = ROT // 2
    rot_part = values[..., :ROT]
    turned = jnp.concatenate([-rot_part[..., half_rot:], rot_part[..., :half_rot]], axis=-1)
    rotated = rot_part * cosine[:, None, :] + turned * sine[:, None, :]
    return jnp.concatenate([rotated, values[..., ROT:]], axis=-1)

def attend_rows(queries, key_rows, value_rows, seg_row):
    length = queries.shape[0]
    block_rows = math.gcd(length, 512)
    score_scale = 1.0 / math.sqrt(HEAD)
    key_pos = jnp.arange(length).astype(jnp.int32)

    def one_block(block_index):
        first_row = (block_index * block_rows).astype(jnp.int32)
        query_blk = lax.dynamic_slice_in_dim(queries, first_row, block_rows, 0)
        query_seg = lax.dynamic_slice_in_dim(seg_row, first_row, block_rows, 0)
        query_pos = first_row + jnp.arange(block_rows).astype(jnp.int32)
        scores = low_back(jnp.einsum('qhd,khd->hqk', query_blk, key_rows, precision=precise) * score_scale)
        allowed = (query_seg[:, None] == seg_row[None, :]) & (key_pos[None, :] <= query_pos[:, None])
        masked = jnp.where(allowed[None], scores, -1e+30)
        top_score = lax.optimization_barrier(jnp.max(masked, axis=-1, keepdims=True))
        weights = jnp.exp(masked - top_score)
        weight_sum = lax.optimization_barrier(jnp.sum(weights, axis=-1))
        mixed = jnp.einsum('hqk,khd->qhd', low(weights), value_rows, precision=precise)
        return mixed / jnp.transpose(weight_sum)[:, :, None]
    blocks = lax.map(jax.checkpoint(one_block), jnp.arange(length // block_rows))
    return blocks.reshape(length, HEADS * HEAD)

def layer_rows(inputs, seg_row, ln1_gain, ln1_bias, w_qkv, b_qkv, w_attn_out, b_attn_out, ln2_gain, ln2_bias, w_up, b_up, w_down, b_down):
    length = inputs.shape[0]
    first_in = low(norm_layer(inputs, ln1_gain, ln1_bias))
    joined = low_back(matmul(first_in, w_qkv) + b_qkv)
    cosine, sine = rotary_tables(jnp.arange(length).astype(jnp.float32))
    split_heads = joined.reshape(length, 3, HEADS, HEAD)
    queries = low(rotate(split_heads[:, 0], cosine, sine))
    key_rows = low(rotate(split_heads[:, 1], cosine, sine))
    value_rows = low(split_heads[:, 2])
    context = low(low_back(attend_rows(queries, key_rows, value_rows, seg_row)))
    attn_branch = matmul(context, w_attn_out) + b_attn_out
    second_in = low(norm_layer(inputs, ln2_gain, ln2_bias))
    hidden = low_back(matmul(second_in, w_up) + b_up)
    active = low(jax.nn.gelu(hidden, approximate=False))
    mlp_branch = matmul(active, w_down) + b_down
    return inputs + attn_branch + mlp_branch

def reference(block_input, segments, out_grad, ln1_gain, ln1_bias, w_qkv, b_qkv, w_attn_out, b_attn_out, ln2_gain, ln2_bias, w_up, b_up, w_down, b_down):
    params = (ln1_gain.astype(jnp.float32), ln1_bias.astype(jnp.float32), w_qkv.astype(jnp.float32), b_qkv.astype(jnp.float32), w_attn_out.astype(jnp.float32), b_attn_out.astype(jnp.float32), ln2_gain.astype(jnp.float32), ln2_bias.astype(jnp.float32), w_up.astype(jnp.float32), b_up.astype(jnp.float32), w_down.astype(jnp.float32), b_down.astype(jnp.float32))
    zeros = jax.tree.map(lambda param: jnp.zeros(param.shape, jnp.float32), params)

    def per_sequence(totals, sequence):
        inputs, seg_row, cotangent = sequence

        def forward(values, *weights):
            return layer_rows(values, seg_row, *weights)
        result, pullback = jax.vjp(forward, inputs.astype(jnp.float32), *params)
        gradients = pullback(cotangent.astype(jnp.float32))
        totals = jax.tree.map(lambda total, update: total + update, totals, tuple(gradients[1:]))
        return (totals, (result, gradients[0]))
    totals, (result, input_grad) = lax.scan(per_sequence, zeros, (block_input, segments, out_grad))
    return (result, input_grad, totals[0], totals[1], totals[2], totals[3], totals[4], totals[5], totals[6], totals[7], totals[8], totals[9], totals[10], totals[11])
```

```python
import math

import jax
import jax.numpy as jnp
from jax import lax
from jax.sharding import PartitionSpec as P

HEADS = 8
HEAD = 256
ROT = 64
BF16 = jnp.bfloat16
F32 = jnp.float32


def normalize(values):
    center = values - jnp.mean(values, axis=-1, keepdims=True)
    spread = jnp.mean(center * center, axis=-1, keepdims=True)
    scale = lax.rsqrt(spread + 1e-05)
    return center * scale, scale


def rotary_tables(positions):
    inverse_freq = 10000.0 ** (-jnp.arange(0, ROT, 2).astype(F32) / ROT)
    angles = positions[:, None] * inverse_freq[None, :]
    angles = jnp.concatenate([angles, angles], axis=1)
    return (jnp.cos(angles), jnp.sin(angles))


def rotate(values, cosine, sine):
    half_rot = ROT // 2
    rot_part = values[..., :ROT]
    turned = jnp.concatenate([-rot_part[..., half_rot:], rot_part[..., :half_rot]], axis=-1)
    rotated = rot_part * cosine + turned * sine
    return jnp.concatenate([rotated, values[..., ROT:]], axis=-1)


def pick(array, index, axis=0):
    return lax.dynamic_index_in_dim(array, index, axis, keepdims=False)


def put(array, piece, index):
    return lax.dynamic_update_slice_in_dim(array, piece[None], index, 0)


def swap(extent, mask):
    return [(i, i ^ mask) for i in range(extent)]


class LineGrid:
    def __init__(self):
        self.dp = lax.axis_index("dp")
        self.sp = lax.axis_index("sp")
        self.line = self.sp // 2
        self.core = self.sp % 2
        self.part = 0

    def gather_dp(self, block):
        half = block.shape[0] // 2
        along_x = lax.ppermute(block, "dp", swap(4, 1))
        along_y = lax.ppermute(block, "dp", swap(4, 2))
        far_one = lax.ppermute(along_y[:half], "dp", swap(4, 1))
        far_two = lax.ppermute(along_x[half:], "dp", swap(4, 2))
        far = jnp.concatenate([far_one, far_two], axis=0)
        out = jnp.zeros((4,) + block.shape, block.dtype)
        for mask, piece in enumerate((block, along_x, along_y, far)):
            out = put(out, piece, self.dp ^ mask)
        return out

    def reduce_dp(self, terms):
        half = terms.shape[1] // 2
        own, to_x, to_y, to_far = (pick(terms, self.dp ^ mask) for mask in range(4))
        far_x = lax.ppermute(to_far[:half], "dp", swap(4, 1))
        far_y = lax.ppermute(to_far[half:], "dp", swap(4, 2))
        top_x = lax.ppermute(to_x[:half], "dp", swap(4, 1))
        low_y = lax.ppermute(to_y[half:], "dp", swap(4, 2))
        top_y = lax.ppermute(
            (to_y[:half].astype(F32) + far_x.astype(F32)).astype(BF16), "dp", swap(4, 2)
        )
        low_x = lax.ppermute(
            (to_x[half:].astype(F32) + far_y.astype(F32)).astype(BF16), "dp", swap(4, 1)
        )
        others = jnp.concatenate(
            [top_x.astype(F32) + top_y.astype(F32), low_x.astype(F32) + low_y.astype(F32)], axis=0
        )
        return own.astype(F32) + others

    def gather_sp(self, block):
        right = [(i, i + 2) for i in range(6)]
        left = [(i + 2, i) for i in range(6)]
        from_left, from_right = [block], [block]
        for step in range(3):
            from_left.append(lax.ppermute(from_left[-1], "sp", right[2 * step :]))
            from_right.append(lax.ppermute(from_right[-1], "sp", left[: 6 - 2 * step]))
        mine = put(jnp.zeros((4,) + block.shape, block.dtype), block, self.line)
        for step in range(1, 4):
            piece = jnp.where(self.line >= step, from_left[step], from_right[4 - step])
            mine = put(mine, piece, (self.line - step) % 4)
        other = lax.ppermute(mine, "sp", swap(8, 1))
        pair = jnp.stack(
            [jnp.where(self.core == 0, mine, other), jnp.where(self.core == 0, other, mine)], axis=1
        )
        return pair.reshape((8 * block.shape[0],) + block.shape[1:])

    def reduce_sp(self, terms):
        rows = terms.shape[0] // 8
        pairs = terms.reshape((4, 2, rows) + terms.shape[1:])
        other = lax.ppermute(pick(pairs, 1 - self.core, 1), "sp", swap(8, 1))
        mine = (pick(pairs, self.core, 1).astype(F32) + other.astype(F32)).astype(BF16)
        right = [(i, i + 2) for i in range(6)]
        left = [(i + 2, i) for i in range(6)]
        going_right = going_left = None
        for step in range(1, 4):
            for_right = pick(mine, jnp.minimum(self.line + 4 - step, 3))
            for_left = pick(mine, jnp.maximum(self.line - 4 + step, 0))
            if step > 1:
                for_right = (for_right.astype(F32) + going_right.astype(F32)).astype(BF16)
                for_left = (for_left.astype(F32) + going_left.astype(F32)).astype(BF16)
            going_right = lax.ppermute(for_right, "sp", right[: 2 * step])
            going_left = lax.ppermute(for_left, "sp", left[6 - 2 * step :])
        return pick(mine, self.line).astype(F32) + going_right.astype(F32) + going_left.astype(F32)

    def exchange_sp(self, blocks):
        pairs = blocks.reshape((4, 2) + blocks.shape[1:])
        keep = pick(pairs, self.core, 1)
        other = lax.ppermute(pick(pairs, 1 - self.core, 1), "sp", swap(8, 1))
        out = jnp.stack(
            [jnp.where(self.core == 0, keep, other), jnp.where(self.core == 0, other, keep)], axis=1
        )
        moved = [
            lax.ppermute(pick(out, self.line ^ step), "sp", swap(8, 2 * step))
            for step in range(1, 4)
        ]
        for step in range(1, 4):
            out = put(out, moved[step - 1], self.line ^ step)
        return out.reshape(blocks.shape)

    def exchange_four(self, blocks):
        place = self.sp % 4
        moved = [
            lax.ppermute(pick(blocks, place ^ step), "sp", swap(8, step)) for step in range(1, 4)
        ]
        for step in range(1, 4):
            blocks = put(blocks, moved[step - 1], place ^ step)
        return blocks

    def gather_small(self, vector):
        out = jnp.zeros((8, 4) + vector.shape, vector.dtype)
        other = lax.ppermute(vector, "sp", swap(8, 1))
        pair = jnp.stack(
            [jnp.where(self.core == 0, vector, other), jnp.where(self.core == 0, other, vector)]
        )
        out = put(jnp.zeros((4,) + pair.shape, pair.dtype), pair, self.line)
        for step in range(1, 4):
            out = put(out, lax.ppermute(pair, "sp", swap(8, 2 * step)), self.line ^ step)
        whole = put(jnp.zeros((4,) + out.shape, out.dtype), out, self.dp)
        for step in range(1, 4):
            whole = put(whole, lax.ppermute(out, "dp", swap(4, step)), self.dp ^ step)
        return whole.reshape((32,) + vector.shape)

    def reduce_small(self, terms):
        blocks = terms.reshape((4, 8) + terms.shape[1:])
        total = pick(blocks, self.dp)
        for step in range(1, 4):
            total = total + lax.ppermute(pick(blocks, self.dp ^ step), "dp", swap(4, step))
        pairs = total.reshape((4, 2) + terms.shape[1:])
        pair = pick(pairs, self.core, 1) + lax.ppermute(
            pick(pairs, 1 - self.core, 1), "sp", swap(8, 1)
        )
        total = pick(pair, self.line)
        for step in range(1, 4):
            total = total + lax.ppermute(pick(pair, self.line ^ step), "sp", swap(8, 2 * step))
        return total

    def gather_out(self, block):
        return self.exchange_four(self.gather_dp(block)).reshape(HEAD, block.shape[1])

    def reduce_out(self, terms):
        return self.reduce_dp(self.exchange_four(terms.reshape(4, HEAD // 4, terms.shape[1])))

    def whole_keys(self, block):
        return block

    def reduce_keys(self, terms):
        return terms


class AnyGrid:
    def __init__(self):
        self.dp = lax.axis_index("dp")
        self.sp = lax.axis_index("sp")
        self.dps = lax.axis_size("dp")
        self.sps = lax.axis_size("sp")
        self.parts = self.sps // HEADS
        self.part = self.sp // HEADS
        self.team = [
            [part * HEADS + rank for rank in range(HEADS)] for part in range(self.parts)
        ]
        self.peers = [
            [part * HEADS + rank for part in range(self.parts)] for rank in range(HEADS)
        ]

    def gather_dp(self, block):
        block = lax.all_gather(block, "sp", axis=0, axis_index_groups=self.peers)
        block = lax.all_gather(block, "dp", axis=0)
        return block.reshape((self.dps * self.parts,) + block.shape[2:])

    def reduce_dp(self, terms):
        block = terms.reshape((self.dps, self.parts) + terms.shape[1:])
        block = lax.psum_scatter(block, "dp", scatter_dimension=0)
        return lax.psum_scatter(
            block, "sp", scatter_dimension=0, axis_index_groups=self.peers
        ).astype(F32)

    def gather_sp(self, block):
        return lax.all_gather(block, "sp", axis=0, tiled=True, axis_index_groups=self.team)

    def reduce_sp(self, terms):
        return lax.psum_scatter(
            terms, "sp", scatter_dimension=0, tiled=True, axis_index_groups=self.team
        ).astype(F32)

    def exchange_sp(self, blocks):
        return lax.all_to_all(
            blocks, "sp", split_axis=0, concat_axis=0, tiled=True, axis_index_groups=self.team
        )

    def gather_small(self, vector):
        return lax.all_gather(vector, ("dp", "sp"), axis=0)

    def reduce_small(self, terms):
        return lax.psum_scatter(terms, ("dp", "sp"), scatter_dimension=0)

    def gather_out(self, block):
        whole = lax.all_gather(block, ("dp", "sp"), axis=0, tiled=True)
        return lax.dynamic_slice_in_dim(whole, head_of(self.sp % HEADS) * HEAD, HEAD, 0)

    def reduce_out(self, terms):
        whole = jnp.zeros((HEADS * HEAD, terms.shape[1]), terms.dtype)
        whole = lax.dynamic_update_slice_in_dim(whole, terms, head_of(self.sp % HEADS) * HEAD, 0)
        return lax.psum_scatter(
            whole, ("dp", "sp"), scatter_dimension=0, tiled=True
        ).astype(F32)

    def whole_keys(self, block):
        return lax.all_gather(block, "sp", axis=0, tiled=True, axis_index_groups=self.peers)

    def reduce_keys(self, terms):
        return lax.psum_scatter(
            terms, "sp", scatter_dimension=0, tiled=True, axis_index_groups=self.peers
        )


def head_of(rank):
    return 2 * (rank % 4) + rank // 4


HEAD_ORDER = [2 * (rank % 4) + rank // 4 for rank in range(HEADS)]
RANK_ORDER = [HEAD_ORDER.index(head) for head in range(HEADS)]


def dot(left, right, contract):
    return lax.dot_general(
        left, right, (((contract[0],), (contract[1],)), ((), ())), preferred_element_type=F32
    )


def shards(
    block_input,
    segments,
    out_grad,
    ln1_gain,
    ln1_bias,
    w_qkv,
    b_qkv,
    w_attn_out,
    b_attn_out,
    ln2_gain,
    ln2_bias,
    w_up,
    b_up,
    w_down,
    b_down,
):
    dps, sps = lax.axis_size("dp"), lax.axis_size("sp")
    devices = dps * sps
    grid = LineGrid() if (dps, sps) == (4, 8) else AnyGrid()
    groups = devices // HEADS
    x_own = block_input[0]
    g_own = out_grad[0]
    tokens, width = x_own.shape
    rows = w_qkv.shape[0]
    cols_up = b_up.shape[0]
    cols_qkv = b_qkv.shape[0]
    length = tokens * HEADS
    scale = 1.0 / math.sqrt(HEAD)

    packed = jnp.concatenate(
        [
            ln1_gain,
            ln1_bias,
            ln2_gain,
            ln2_bias,
            b_attn_out,
            b_down,
            b_qkv,
            b_up,
            segments[0].astype(BF16),
        ]
    )
    small = grid.gather_small(packed)
    vectors = [
        small[:, k * rows : (k + 1) * rows].reshape(width).astype(F32) for k in range(6)
    ]
    gain_one, shift_one, gain_two, shift_two, bias_out, bias_down = vectors
    at = 6 * rows
    rank = grid.sp % HEADS
    bias_qkv = small[:, at : at + cols_qkv].reshape(3, HEADS, HEAD)
    bias_qkv = pick(bias_qkv, head_of(rank), 1).astype(F32).reshape(3 * HEAD)
    at += cols_qkv
    bias_up = small[:, at : at + cols_up].reshape(groups, HEADS, cols_up)
    bias_up = pick(bias_up, rank, 1).astype(F32).reshape(groups * cols_up)
    at += cols_up
    seg_all = pick(small[:, at:].reshape(dps, sps * tokens), grid.dp)
    seg_mine = lax.dynamic_slice_in_dim(seg_all, grid.part * length, length, 0)

    x_all = grid.gather_sp(x_own)
    up_blocks = w_up.reshape(rows, groups, HEADS, cols_up).transpose(2, 0, 1, 3)
    up_blocks = up_blocks.reshape(HEADS, rows, groups * cols_up)
    up_rows = grid.exchange_sp(up_blocks).reshape(HEADS * rows, groups * cols_up)
    weight_down = grid.gather_dp(w_down).reshape(groups * cols_up, width)
    weight_up = grid.gather_dp(up_rows).reshape(width, groups * cols_up)
    qkv_blocks = w_qkv.reshape(rows, 3, HEADS, HEAD)
    qkv_blocks = jnp.stack([qkv_blocks[:, :, head] for head in HEAD_ORDER])
    qkv_blocks = qkv_blocks.reshape(HEADS, rows, 3 * HEAD)
    qkv_rows = grid.exchange_sp(qkv_blocks).reshape(HEADS * rows, 3 * HEAD)
    weight_qkv = grid.gather_dp(qkv_rows).reshape(width, 3 * HEAD)
    weight_out = grid.gather_out(w_attn_out)
    g_all = grid.gather_sp(g_own)

    normed, _ = normalize(x_all.astype(F32))
    first_in = (normed * gain_one + shift_one).astype(BF16)
    second_in = (normed * gain_two + shift_two).astype(BF16)

    hidden = dot(second_in, weight_up, (1, 0)) + bias_up
    active_wide, gelu_pull = jax.vjp(lambda v: jax.nn.gelu(v, approximate=False), hidden)
    active = active_wide.astype(BF16)
    d_active = dot(g_all, weight_down, (1, 1))
    d_hidden = gelu_pull(d_active)[0].astype(BF16)
    term_down = dot(active, g_all, (0, 0)).astype(BF16)
    term_up = dot(second_in, d_hidden, (0, 0)).astype(BF16)

    joined = dot(first_in, weight_qkv, (1, 0)) + bias_qkv
    position = grid.part * length + jnp.arange(length, dtype=jnp.int32)
    cosine, sine = rotary_tables(position.astype(F32))
    queries = rotate(joined[:, :HEAD], cosine, sine).astype(BF16)
    key_rows = grid.whole_keys(rotate(joined[:, HEAD : 2 * HEAD], cosine, sine).astype(BF16))
    value_rows = grid.whole_keys(joined[:, 2 * HEAD :].astype(BF16))
    key_position = jnp.arange(key_rows.shape[0], dtype=jnp.int32)
    allowed = (seg_mine[:, None] == seg_all[None, :]) & (
        key_position[None, :] <= position[:, None]
    )
    scores = jnp.where(allowed, dot(queries, key_rows, (1, 1)) * scale, -1e30)
    top = jnp.max(scores, axis=-1, keepdims=True)
    weights = jnp.where(allowed, jnp.exp(scores - top), 0.0)
    weight_sum = jnp.sum(weights, axis=-1, keepdims=True)
    log_sum = top + jnp.log(weight_sum)
    context = dot(weights.astype(BF16), value_rows, (1, 0)) / weight_sum
    context_low = context.astype(BF16)

    out_terms = dot(context_low, weight_out, (1, 0)) + dot(active, weight_down, (1, 0))
    out_sum = grid.reduce_sp(out_terms.astype(BF16))
    block_output = (x_own.astype(F32) + out_sum + (bias_out + bias_down))[None]

    d_context = dot(g_all, weight_out, (1, 1)).astype(BF16)
    row_delta = jnp.sum(d_context.astype(F32) * context, axis=-1, keepdims=True)
    probs = jnp.where(allowed, jnp.exp(scores - log_sum), 0.0)
    d_probs = dot(d_context, value_rows, (1, 1))
    d_scores = (probs * (d_probs - row_delta)).astype(BF16)
    d_queries = dot(d_scores, key_rows, (1, 0)) * scale
    d_keys = grid.reduce_keys(dot(d_scores, queries, (0, 0)) * scale)
    d_values = grid.reduce_keys(dot(probs.astype(BF16), d_context, (0, 0)))
    d_joined = jnp.concatenate(
        [rotate(d_queries, cosine, -sine), rotate(d_keys, cosine, -sine), d_values], axis=1
    ).astype(BF16)

    d_first = dot(d_joined, weight_qkv, (1, 1))
    d_second = dot(d_hidden, weight_up, (1, 1))
    u_terms = d_first * gain_one + d_second * gain_two
    u_sum = grid.reduce_sp(u_terms.astype(BF16))
    normed_own, scale_own = normalize(x_own.astype(F32))
    u_mean = jnp.mean(u_sum, axis=-1, keepdims=True)
    u_along = jnp.mean(u_sum * normed_own, axis=-1, keepdims=True)
    input_grad = (g_own.astype(F32) + (u_sum - u_mean - normed_own * u_along) * scale_own)[None]

    term_qkv = dot(first_in, d_joined, (0, 0)).astype(BF16)
    term_out = dot(context_low, g_all, (0, 0)).astype(BF16)
    grad_down = grid.reduce_dp(term_down.reshape(groups, cols_up, width))
    up_sum = grid.reduce_dp(term_up.reshape(groups, HEADS * rows, groups * cols_up))
    up_back = grid.exchange_sp(up_sum.astype(BF16).reshape(HEADS, rows, groups * cols_up))
    grad_up = (
        up_back.astype(F32)
        .reshape(HEADS, rows, groups, cols_up)
        .transpose(1, 2, 0, 3)
        .reshape(rows, devices * cols_up)
    )
    grad_out = grid.reduce_out(term_out)
    qkv_sum = grid.reduce_dp(term_qkv.reshape(groups, HEADS * rows, 3 * HEAD))
    qkv_back = grid.exchange_sp(qkv_sum.astype(BF16).reshape(HEADS, rows, 3, HEAD)).astype(F32)
    grad_qkv = jnp.stack([qkv_back[place] for place in RANK_ORDER], axis=2)
    grad_qkv = grad_qkv.reshape(rows, 3 * HEADS * HEAD)

    sum_qkv = jnp.zeros((3, HEADS, HEAD), F32)
    sum_qkv = lax.dynamic_update_slice(
        sum_qkv,
        jnp.sum(d_joined.astype(F32), axis=0).reshape(3, 1, HEAD),
        (0, head_of(rank), 0),
    )
    sum_up = jnp.zeros((groups, HEADS, cols_up), F32)
    sum_up = lax.dynamic_update_slice(
        sum_up,
        jnp.sum(d_hidden.astype(F32), axis=0).reshape(groups, 1, cols_up),
        (0, rank, 0),
    )
    totals = [
        jnp.sum(d_first * normed, axis=0),
        jnp.sum(d_first, axis=0),
        jnp.sum(d_second * normed, axis=0),
        jnp.sum(d_second, axis=0),
        jnp.sum(g_own.astype(F32), axis=0),
        sum_qkv,
        sum_up,
    ]
    totals = jnp.concatenate([total.reshape(devices, -1) for total in totals], axis=1)
    owned = grid.reduce_small(totals)
    parts = [owned[k * rows : (k + 1) * rows] for k in range(5)]
    grad_g1, grad_s1, grad_g2, grad_s2, grad_bout = parts
    grad_bqkv = owned[5 * rows : 5 * rows + cols_qkv]
    grad_bup = owned[5 * rows + cols_qkv :]
    return (
        block_output,
        input_grad,
        grad_g1,
        grad_s1,
        grad_qkv,
        grad_bqkv,
        grad_out,
        grad_bout,
        grad_g2,
        grad_s2,
        grad_up,
        grad_bup,
        grad_down,
        grad_bout,
    )


def solution(mesh):
    tokens = P("dp", "sp", None)
    split = P(("dp", "sp"))
    matrix = P(("dp", "sp"), None)
    return jax.shard_map(
        shards,
        mesh=mesh,
        in_specs=(
            tokens,
            P("dp", "sp"),
            tokens,
            split,
            split,
            matrix,
            split,
            matrix,
            split,
            split,
            split,
            matrix,
            split,
            matrix,
            split,
        ),
        out_specs=(
            tokens,
            tokens,
            split,
            split,
            matrix,
            split,
            matrix,
            split,
            split,
            split,
            matrix,
            split,
            matrix,
            split,
        ),
        check_vma=False,
    )
```

```python
import functools
import math

import jax
import jax.numpy as jnp
from jax import lax
from jax.experimental import pallas as pl
from jax.experimental.pallas import tpu as pltpu
from jax.sharding import PartitionSpec as P

HEADS = 8
HEAD = 256
ROT = 64
TILE = 256
BF16 = jnp.bfloat16
F32 = jnp.float32

def normalize(values):
    center = values - jnp.mean(values, axis=-1, keepdims=True)
    spread = jnp.mean(center * center, axis=-1, keepdims=True)
    scale = lax.rsqrt(spread + 1e-05)
    return center * scale, scale


def rotary_tables(positions):
    inverse_freq = 10000.0 ** (-jnp.arange(0, ROT, 2).astype(F32) / ROT)
    angles = positions[:, None] * inverse_freq[None, :]
    angles = jnp.concatenate([angles, angles], axis=1)
    return (jnp.cos(angles), jnp.sin(angles))


def rotate(values, cosine, sine):
    half_rot = ROT // 2
    rot_part = values[..., :ROT]
    turned = jnp.concatenate([-rot_part[..., half_rot:], rot_part[..., :half_rot]], axis=-1)
    rotated = rot_part * cosine + turned * sine
    return jnp.concatenate([rotated, values[..., ROT:]], axis=-1)


def pick(array, index, axis=0):
    return lax.dynamic_index_in_dim(array, index, axis, keepdims=False)


def put(array, piece, index):
    return lax.dynamic_update_slice_in_dim(array, piece[None], index, 0)


def swap(extent, mask):
    return [(i, i ^ mask) for i in range(extent)]


class AnyGrid:
    def __init__(self):
        self.dp = lax.axis_index("dp")
        self.sp = lax.axis_index("sp")
        self.dps = lax.axis_size("dp")
        self.sps = lax.axis_size("sp")
        self.parts = self.sps // HEADS
        self.part = self.sp // HEADS
        self.team = [
            [part * HEADS + rank for rank in range(HEADS)] for part in range(self.parts)
        ]
        self.peers = [
            [part * HEADS + rank for part in range(self.parts)] for rank in range(HEADS)
        ]

    def gather_dp(self, block):
        block = lax.all_gather(block, "sp", axis=0, axis_index_groups=self.peers)
        block = lax.all_gather(block, "dp", axis=0)
        return block.reshape((self.dps * self.parts,) + block.shape[2:])

    def reduce_dp(self, terms):
        block = terms.reshape((self.dps, self.parts) + terms.shape[1:])
        block = lax.psum_scatter(block, "dp", scatter_dimension=0)
        return lax.psum_scatter(
            block, "sp", scatter_dimension=0, axis_index_groups=self.peers
        ).astype(F32)

    def gather_sp(self, block):
        return lax.all_gather(block, "sp", axis=0, tiled=True, axis_index_groups=self.team)

    def reduce_sp(self, terms):
        return lax.psum_scatter(
            terms, "sp", scatter_dimension=0, tiled=True, axis_index_groups=self.team
        ).astype(F32)

    def exchange_sp(self, blocks):
        return lax.all_to_all(
            blocks, "sp", split_axis=0, concat_axis=0, tiled=True, axis_index_groups=self.team
        )

    def gather_small(self, vector):
        return lax.all_gather(vector, ("dp", "sp"), axis=0)

    def reduce_small(self, terms):
        return lax.psum_scatter(terms, ("dp", "sp"), scatter_dimension=0)

    def gather_out(self, block):
        whole = lax.all_gather(block, ("dp", "sp"), axis=0, tiled=True)
        return lax.dynamic_slice_in_dim(whole, head_of(self.sp % HEADS) * HEAD, HEAD, 0)

    def reduce_out(self, terms):
        whole = jnp.zeros((HEADS * HEAD, terms.shape[1]), terms.dtype)
        whole = lax.dynamic_update_slice_in_dim(whole, terms, head_of(self.sp % HEADS) * HEAD, 0)
        return lax.psum_scatter(
            whole, ("dp", "sp"), scatter_dimension=0, tiled=True
        ).astype(F32)

    def whole_keys(self, block):
        return lax.all_gather(block, "sp", axis=0, tiled=True, axis_index_groups=self.peers)

    def reduce_keys(self, terms):
        return lax.psum_scatter(
            terms, "sp", scatter_dimension=0, tiled=True, axis_index_groups=self.peers
        )


def head_of(rank):
    return 2 * (rank % 4) + rank // 4


HEAD_ORDER = [2 * (rank % 4) + rank // 4 for rank in range(HEADS)]
RANK_ORDER = [HEAD_ORDER.index(head) for head in range(HEADS)]


def dot(left, right, contract):
    return lax.dot_general(
        left, right, (((contract[0],), (contract[1],)), ((), ())), preferred_element_type=F32
    )


def any_shards(
    block_input,
    segments,
    out_grad,
    ln1_gain,
    ln1_bias,
    w_qkv,
    b_qkv,
    w_attn_out,
    b_attn_out,
    ln2_gain,
    ln2_bias,
    w_up,
    b_up,
    w_down,
    b_down,
):
    dps, sps = lax.axis_size("dp"), lax.axis_size("sp")
    devices = dps * sps
    grid = AnyGrid()
    groups = devices // HEADS
    x_own = block_input[0]
    g_own = out_grad[0]
    tokens, width = x_own.shape
    rows = w_qkv.shape[0]
    cols_up = b_up.shape[0]
    cols_qkv = b_qkv.shape[0]
    length = tokens * HEADS
    scale = 1.0 / math.sqrt(HEAD)

    packed = jnp.concatenate(
        [
            ln1_gain,
            ln1_bias,
            ln2_gain,
            ln2_bias,
            b_attn_out,
            b_down,
            b_qkv,
            b_up,
            segments[0].astype(BF16),
        ]
    )
    small = grid.gather_small(packed)
    vectors = [
        small[:, k * rows : (k + 1) * rows].reshape(width).astype(F32) for k in range(6)
    ]
    gain_one, shift_one, gain_two, shift_two, bias_out, bias_down = vectors
    at = 6 * rows
    rank = grid.sp % HEADS
    bias_qkv = small[:, at : at + cols_qkv].reshape(3, HEADS, HEAD)
    bias_qkv = pick(bias_qkv, head_of(rank), 1).astype(F32).reshape(3 * HEAD)
    at += cols_qkv
    bias_up = small[:, at : at + cols_up].reshape(groups, HEADS, cols_up)
    bias_up = pick(bias_up, rank, 1).astype(F32).reshape(groups * cols_up)
    at += cols_up
    seg_all = pick(small[:, at:].reshape(dps, sps * tokens), grid.dp)
    seg_mine = lax.dynamic_slice_in_dim(seg_all, grid.part * length, length, 0)

    x_all = grid.gather_sp(x_own)
    up_blocks = w_up.reshape(rows, groups, HEADS, cols_up).transpose(2, 0, 1, 3)
    up_blocks = up_blocks.reshape(HEADS, rows, groups * cols_up)
    up_rows = grid.exchange_sp(up_blocks).reshape(HEADS * rows, groups * cols_up)
    weight_down = grid.gather_dp(w_down).reshape(groups * cols_up, width)
    weight_up = grid.gather_dp(up_rows).reshape(width, groups * cols_up)
    qkv_blocks = w_qkv.reshape(rows, 3, HEADS, HEAD)
    qkv_blocks = jnp.stack([qkv_blocks[:, :, head] for head in HEAD_ORDER])
    qkv_blocks = qkv_blocks.reshape(HEADS, rows, 3 * HEAD)
    qkv_rows = grid.exchange_sp(qkv_blocks).reshape(HEADS * rows, 3 * HEAD)
    weight_qkv = grid.gather_dp(qkv_rows).reshape(width, 3 * HEAD)
    weight_out = grid.gather_out(w_attn_out)
    g_all = grid.gather_sp(g_own)

    normed, _ = normalize(x_all.astype(F32))
    first_in = (normed * gain_one + shift_one).astype(BF16)
    second_in = (normed * gain_two + shift_two).astype(BF16)

    hidden = dot(second_in, weight_up, (1, 0)) + bias_up
    active_wide, gelu_pull = jax.vjp(lambda v: jax.nn.gelu(v, approximate=False), hidden)
    active = active_wide.astype(BF16)
    d_active = dot(g_all, weight_down, (1, 1))
    d_hidden = gelu_pull(d_active)[0].astype(BF16)
    term_down = dot(active, g_all, (0, 0)).astype(BF16)
    term_up = dot(second_in, d_hidden, (0, 0)).astype(BF16)

    joined = dot(first_in, weight_qkv, (1, 0)) + bias_qkv
    position = grid.part * length + jnp.arange(length, dtype=jnp.int32)
    cosine, sine = rotary_tables(position.astype(F32))
    queries = rotate(joined[:, :HEAD], cosine, sine).astype(BF16)
    key_rows = grid.whole_keys(rotate(joined[:, HEAD : 2 * HEAD], cosine, sine).astype(BF16))
    value_rows = grid.whole_keys(joined[:, 2 * HEAD :].astype(BF16))
    key_position = jnp.arange(key_rows.shape[0], dtype=jnp.int32)
    allowed = (seg_mine[:, None] == seg_all[None, :]) & (
        key_position[None, :] <= position[:, None]
    )
    scores = jnp.where(allowed, dot(queries, key_rows, (1, 1)) * scale, -1e30)
    top = jnp.max(scores, axis=-1, keepdims=True)
    weights = jnp.where(allowed, jnp.exp(scores - top), 0.0)
    weight_sum = jnp.sum(weights, axis=-1, keepdims=True)
    log_sum = top + jnp.log(weight_sum)
    context = dot(weights.astype(BF16), value_rows, (1, 0)) / weight_sum
    context_low = context.astype(BF16)

    out_terms = dot(context_low, weight_out, (1, 0)) + dot(active, weight_down, (1, 0))
    out_sum = grid.reduce_sp(out_terms.astype(BF16))
    block_output = (x_own.astype(F32) + out_sum + (bias_out + bias_down))[None]

    d_context = dot(g_all, weight_out, (1, 1)).astype(BF16)
    row_delta = jnp.sum(d_context.astype(F32) * context, axis=-1, keepdims=True)
    probs = jnp.where(allowed, jnp.exp(scores - log_sum), 0.0)
    d_probs = dot(d_context, value_rows, (1, 1))
    d_scores = (probs * (d_probs - row_delta)).astype(BF16)
    d_queries = dot(d_scores, key_rows, (1, 0)) * scale
    d_keys = grid.reduce_keys(dot(d_scores, queries, (0, 0)) * scale)
    d_values = grid.reduce_keys(dot(probs.astype(BF16), d_context, (0, 0)))
    d_joined = jnp.concatenate(
        [rotate(d_queries, cosine, -sine), rotate(d_keys, cosine, -sine), d_values], axis=1
    ).astype(BF16)

    d_first = dot(d_joined, weight_qkv, (1, 1))
    d_second = dot(d_hidden, weight_up, (1, 1))
    u_terms = d_first * gain_one + d_second * gain_two
    u_sum = grid.reduce_sp(u_terms.astype(BF16))
    normed_own, scale_own = normalize(x_own.astype(F32))
    u_mean = jnp.mean(u_sum, axis=-1, keepdims=True)
    u_along = jnp.mean(u_sum * normed_own, axis=-1, keepdims=True)
    input_grad = (g_own.astype(F32) + (u_sum - u_mean - normed_own * u_along) * scale_own)[None]

    term_qkv = dot(first_in, d_joined, (0, 0)).astype(BF16)
    term_out = dot(context_low, g_all, (0, 0)).astype(BF16)
    grad_down = grid.reduce_dp(term_down.reshape(groups, cols_up, width))
    up_sum = grid.reduce_dp(term_up.reshape(groups, HEADS * rows, groups * cols_up))
    up_back = grid.exchange_sp(up_sum.astype(BF16).reshape(HEADS, rows, groups * cols_up))
    grad_up = (
        up_back.astype(F32)
        .reshape(HEADS, rows, groups, cols_up)
        .transpose(1, 2, 0, 3)
        .reshape(rows, devices * cols_up)
    )
    grad_out = grid.reduce_out(term_out)
    qkv_sum = grid.reduce_dp(term_qkv.reshape(groups, HEADS * rows, 3 * HEAD))
    qkv_back = grid.exchange_sp(qkv_sum.astype(BF16).reshape(HEADS, rows, 3, HEAD)).astype(F32)
    grad_qkv = jnp.stack([qkv_back[place] for place in RANK_ORDER], axis=2)
    grad_qkv = grad_qkv.reshape(rows, 3 * HEADS * HEAD)

    sum_qkv = jnp.zeros((3, HEADS, HEAD), F32)
    sum_qkv = lax.dynamic_update_slice(
        sum_qkv,
        jnp.sum(d_joined.astype(F32), axis=0).reshape(3, 1, HEAD),
        (0, head_of(rank), 0),
    )
    sum_up = jnp.zeros((groups, HEADS, cols_up), F32)
    sum_up = lax.dynamic_update_slice(
        sum_up,
        jnp.sum(d_hidden.astype(F32), axis=0).reshape(groups, 1, cols_up),
        (0, rank, 0),
    )
    totals = [
        jnp.sum(d_first * normed, axis=0),
        jnp.sum(d_first, axis=0),
        jnp.sum(d_second * normed, axis=0),
        jnp.sum(d_second, axis=0),
        jnp.sum(g_own.astype(F32), axis=0),
        sum_qkv,
        sum_up,
    ]
    totals = jnp.concatenate([total.reshape(devices, -1) for total in totals], axis=1)
    owned = grid.reduce_small(totals)
    parts = [owned[k * rows : (k + 1) * rows] for k in range(5)]
    grad_g1, grad_s1, grad_g2, grad_s2, grad_bout = parts
    grad_bqkv = owned[5 * rows : 5 * rows + cols_qkv]
    grad_bup = owned[5 * rows + cols_qkv :]
    return (
        block_output,
        input_grad,
        grad_g1,
        grad_s1,
        grad_qkv,
        grad_bqkv,
        grad_out,
        grad_bout,
        grad_g2,
        grad_s2,
        grad_up,
        grad_bup,
        grad_down,
        grad_bout,
    )


def fill(dp, full, pieces, rows, take=None):
    own, along_x, along_y, far_one, far_two = pieces
    take = rows if take is None else take
    def at(mask, shift=0):
        return pl.multiple_of((dp ^ mask) * take + shift, 16)
    full[pl.ds(at(0), take), :] = own[0:take, :]
    full[pl.ds(at(1), take), :] = along_x[0:take, :]
    full[pl.ds(at(2), take), :] = along_y[0:take, :]
    cut = far_one.shape[0]
    full[pl.ds(at(3), cut), :] = far_one[...]
    full[pl.ds(at(3, cut), take - cut), :] = far_two[0 : take - cut, :]

def whole(shape):
    return pl.BlockSpec(shape, lambda *_: (0,) * len(shape), pipeline_mode=pl.Buffered(1))

def tile(cols):
    return pl.BlockSpec((TILE, cols), lambda i, *_: (i, 0))

def run(body, name, dp, inputs, specs, outs, out_specs, scratch, grid, flops=0, vmem=56):
    bytes_accessed = sum(a.size * a.dtype.itemsize for a in inputs) + sum(math.prod(o.shape) * o.dtype.itemsize for o in outs)
    return pl.pallas_call(
        body, name=name,
        grid_spec=pltpu.PrefetchScalarGridSpec(num_scalar_prefetch=1, grid=grid, in_specs=specs, out_specs=out_specs, scratch_shapes=scratch),
        out_shape=outs,
        compiler_params=pltpu.CompilerParams(vmem_limit_bytes=vmem * 2**20, dimension_semantics=("arbitrary",) * len(grid)),
        cost_estimate=pl.CostEstimate(flops=flops, bytes_accessed=bytes_accessed, transcendentals=0),
    )(dp.reshape(1), *inputs)

def shape(dims, kind):
    return jax.ShapeDtypeStruct(dims, kind)

def norm_tile(x):
    v = x.astype(F32)
    center = v - jnp.mean(v, axis=-1, keepdims=True)
    scale = lax.rsqrt(jnp.mean(center * center, axis=-1, keepdims=True) + 1e-05)
    return center * scale, scale

def norms_body(dp, x, vec, first, second):
    normed, _ = norm_tile(x[...])
    first[...] = (normed * vec[0:1, :] + vec[1:2, :]).astype(BF16)
    second[...] = (normed * vec[2:3, :] + vec[3:4, :]).astype(BF16)

def norms(dp, x, vec):
    n, w = x.shape
    return run(norms_body, "norms", dp, [x, vec], [tile(w), whole(vec.shape)], [shape((n, w), BF16)] * 2, [tile(w)] * 2, [], (n // TILE,))

def turn(v, cos, s1, s2):
    left = v[:, :128]
    out = left * cos + pltpu.roll(left, 96, 1) * s1 + pltpu.roll(left, 32, 1) * s2
    return jnp.concatenate([out, v[:, 128:]], axis=1)

def qkv_body(dp, first, w0, wx, wy, w1, w2, bias, cos, s1, s2, q, k, v, full):
    @pl.when(pl.program_id(0) == 0)
    def _():
        fill(dp[0], full, (w0, wx, wy, w1, w2), w0.shape[0])
    joined = dot(first[...], full[...], (1, 0)) + bias[...]
    q[...] = turn(joined[:, :HEAD], cos[...], s1[...], s2[...]).astype(BF16)
    k[...] = turn(joined[:, HEAD:2 * HEAD], cos[...], s1[...], s2[...]).astype(BF16)
    v[...] = joined[:, 2 * HEAD:].astype(BF16)

def qkv(dp, first, pieces, bias, tables):
    n, w = first.shape
    return run(qkv_body, "qkv", dp, [first, *pieces, bias, *tables],
        [tile(w)] + [whole(p.shape) for p in pieces] + [whole(bias.shape)] + [tile(128)] * 3,
        [shape((n, HEAD), BF16)] * 3, [tile(HEAD)] * 3, [pltpu.VMEM((w, 3 * HEAD), BF16)], (n // TILE,), flops=2 * n * w * 3 * HEAD)

def mlp_body(dp, second, g, u0, ux, uy, u1, u2, d0, dx, dy, d1, d2, bias, active, d_hidden, sums, full_up, full_down):
    step = pl.program_id(0)
    @pl.when(step == 0)
    def _():
        fill(dp[0], full_up, (u0, ux, uy, u1, u2), u0.shape[0])
        fill(dp[0], full_down, (d0, dx, dy, d1, d2), None, full_down.shape[0] // 4)
        sums[...] = jnp.zeros_like(sums)
    hidden = dot(second[...], full_up[...], (1, 0)) + bias[...]
    d_active = dot(g[...], full_down[...], (1, 1))
    half_cdf = 0.5 + 0.5 * lax.erf(hidden * (1.0 / math.sqrt(2.0)))
    active[...] = (hidden * half_cdf).astype(BF16)
    slope = half_cdf + hidden * (jnp.exp(-0.5 * hidden * hidden) * (1.0 / math.sqrt(2.0 * math.pi)))
    low = (slope * d_active).astype(BF16)
    d_hidden[...] = low
    sums[...] += jnp.sum(low.astype(F32), axis=0, keepdims=True)

def mlp(dp, second, g, up, down, bias):
    n, w = second.shape
    h = up[0].shape[1]
    return run(mlp_body, "mlp", dp, [second, g, *up, *down, bias],
        [tile(w)] * 2 + [whole(p.shape) for p in (*up, *down, bias)],
        [shape((n, h), BF16)] * 2 + [shape((1, h), F32)], [tile(h)] * 2 + [whole((1, h))],
        [pltpu.VMEM((w, h), BF16), pltpu.VMEM((h, w), BF16)], (n // TILE,), flops=4 * n * w * h)

def attend_body(dp, q, k, v, g, w_out, seg_q, seg_k, cos, s1, s2, kcos, ks1, ks2, ctx, dq, dk, dv, sums, dk_acc, dv_acc):
    step = pl.program_id(0)
    count = k.shape[0] // TILE
    scale = 1.0 / math.sqrt(HEAD)
    @pl.when(step == 0)
    def _():
        sums[...] = jnp.zeros_like(sums)
        dk_acc[...] = jnp.zeros_like(dk_acc)
        dv_acc[...] = jnp.zeros_like(dv_acc)
    d_ctx = dot(g[...], w_out[...], (1, 1)).astype(BF16)
    def block(index):
        reach = (index + 1) * TILE
        keys, values = k[0:reach, :], v[0:reach, :]
        scores = dot(q[...], keys, (1, 1)) * scale
        row = index * TILE + lax.broadcasted_iota(jnp.int32, (TILE, reach), 0)
        col = lax.broadcasted_iota(jnp.int32, (TILE, reach), 1)
        allowed = (seg_q[...] == seg_k[:, 0:reach]) & (col <= row)
        scores = jnp.where(allowed, scores, -1e30)
        top = jnp.max(scores, axis=1, keepdims=True)
        weights = jnp.where(allowed, jnp.exp(scores - top), 0.0)
        inverse = 1.0 / jnp.sum(weights, axis=1, keepdims=True)
        context = dot(weights.astype(BF16), values, (1, 0)) * inverse
        ctx[...] = context.astype(BF16)
        delta = jnp.sum(d_ctx.astype(F32) * context, axis=1, keepdims=True)
        probs = weights * inverse
        d_probs = dot(d_ctx, values, (1, 1))
        d_scores = (probs * (d_probs - delta)).astype(BF16)
        d_q = dot(d_scores, keys, (1, 0)) * scale
        low = turn(d_q, cos[...], -s1[...], -s2[...]).astype(BF16)
        dq[...] = low
        sums[:, 0:HEAD] += jnp.sum(low.astype(F32), axis=0, keepdims=True)
        dk_acc[0:reach, :] += dot(d_scores, q[...], (0, 0))
        dv_acc[0:reach, :] += dot(probs.astype(BF16), d_ctx, (0, 0))
    for index in range(count):
        @pl.when(step == index)
        def _(index=index):
            block(index)
    @pl.when(step == count - 1)
    def _():
        low_k = turn(dk_acc[...] * scale, kcos[...], -ks1[...], -ks2[...]).astype(BF16)
        low_v = dv_acc[...].astype(BF16)
        dk[...] = low_k
        dv[...] = low_v
        sums[:, HEAD:2 * HEAD] = jnp.sum(low_k.astype(F32), axis=0, keepdims=True)
        sums[:, 2 * HEAD:] = jnp.sum(low_v.astype(F32), axis=0, keepdims=True)

def attend(dp, q, k, v, g, w_out, seg_col, seg_row, tables):
    n = q.shape[0]; w = g.shape[1]
    return run(attend_body, "attend", dp, [q, k, v, g, w_out, seg_col, seg_row, *tables, *tables],
        [tile(HEAD), whole(k.shape), whole(v.shape), tile(w), whole(w_out.shape), tile(1), whole(seg_row.shape)] + [tile(128)] * 3 + [whole((n, 128))] * 3,
        [shape((n, HEAD), BF16)] * 4 + [shape((1, 3 * HEAD), F32)],
        [tile(HEAD)] * 2 + [whole((n, HEAD))] * 2 + [whole((1, 3 * HEAD))],
        [pltpu.VMEM((n, HEAD), F32)] * 2, (n // TILE,), flops=2 * n * w * HEAD + 7 * n * n * HEAD)

def output_body(dp, ctx, active, w_out, d0, dx, dy, d1, d2, out, full):
    @pl.when(pl.program_id(0) == 0)
    def _():
        fill(dp[0], full, (d0, dx, dy, d1, d2), None, full.shape[0] // 4)
    out[...] = (dot(ctx[...], w_out[...], (1, 0)) + dot(active[...], full[...], (1, 0))).astype(BF16)

def output(dp, ctx, active, w_out, down):
    n, h = active.shape; w = w_out.shape[1]
    return run(output_body, "output", dp, [ctx, active, w_out, *down],
        [tile(HEAD), tile(h), whole(w_out.shape)] + [whole(p.shape) for p in down],
        [shape((n, w), BF16)], [tile(w)], [pltpu.VMEM((h, w), BF16)], (n // TILE,), flops=2 * n * w * (h + HEAD))[0]

def inward_body(dp, x, dq, dk, dv, d_hidden, w0, wx, wy, w1, w2, u0, ux, uy, u1, u2, vec, u, sums, full_qkv, full_up):
    @pl.when(pl.program_id(0) == 0)
    def _():
        fill(dp[0], full_qkv, (w0, wx, wy, w1, w2), w0.shape[0])
        fill(dp[0], full_up, (u0, ux, uy, u1, u2), u0.shape[0])
        sums[...] = jnp.zeros_like(sums)
    normed, _ = norm_tile(x[...])
    d_joined = jnp.concatenate([dq[...], dk[...], dv[...]], axis=1)
    d_first = dot(d_joined, full_qkv[...], (1, 1))
    d_second = dot(d_hidden[...], full_up[...], (1, 1))
    u[...] = (d_first * vec[0:1, :] + d_second * vec[2:3, :]).astype(BF16)
    sums[0:1, :] += jnp.sum(d_first * normed, axis=0, keepdims=True)
    sums[1:2, :] += jnp.sum(d_first, axis=0, keepdims=True)
    sums[2:3, :] += jnp.sum(d_second * normed, axis=0, keepdims=True)
    sums[3:4, :] += jnp.sum(d_second, axis=0, keepdims=True)

def inward(dp, x, dq, dk, dv, d_hidden, wq, up, vec):
    n, w = x.shape; h = d_hidden.shape[1]
    return run(inward_body, "inward", dp, [x, dq, dk, dv, d_hidden, *wq, *up, vec],
        [tile(w)] + [tile(HEAD)] * 3 + [tile(h)] + [whole(p.shape) for p in (*wq, *up, vec)],
        [shape((n, w), BF16), shape((4, w), F32)], [tile(w), whole((4, w))],
        [pltpu.VMEM((w, 3 * HEAD), BF16), pltpu.VMEM((w, h), BF16)], (n // TILE,), flops=2 * n * w * (h + 3 * HEAD))

ORDER = (3, 1, 2, 0)
def terms_body(count, dp, left, *refs):
    rights, outs = refs[:count], refs[count:]
    step = pl.program_id(0)
    right = rights[0][...] if count == 1 else jnp.concatenate([r[...] for r in rights], axis=1)
    for place in range(4):
        @pl.when(step == place)
        def _(place=place):
            term = dot(left[...], right, (0, 0)).astype(BF16)
            if place == 3:
                outs[6][...] = term
            else:
                half = term.shape[0] // 2
                outs[2 * place][...] = term[:half]
                outs[2 * place + 1][...] = term[half:]

def order_mask(step):
    return jnp.where(step == 0, 3, jnp.where(step == 3, 0, step))

def terms(dp, left, rights, name):
    n, w = left.shape; rows = w // 4; cols = sum(r.shape[1] for r in rights)
    outs = [shape((rows // 2, cols), BF16)] * 6 + [shape((rows, cols), BF16)]
    return run(functools.partial(terms_body, len(rights)), name, dp, [left, *rights],
        [pl.BlockSpec((n, rows), lambda i, d: (0, d[0] ^ order_mask(i)))] + [whole(r.shape) for r in rights],
        outs, [whole(o.shape) for o in outs], [], (4,), flops=2 * n * w * cols)


def up_blocks_body(source, out):
    for rank in range(HEADS):
        for group in range(4):
            at = (group * HEADS + rank) * 256
            out[rank, :, group * 256 : group * 256 + 256] = source[:, at : at + 256]


def qkv_blocks_body(source, out):
    for rank in range(HEADS):
        for part in range(3):
            at = (part * HEADS + HEAD_ORDER[rank]) * HEAD
            out[rank, :, part * HEAD : part * HEAD + HEAD] = source[:, at : at + HEAD]


def up_rows_body(source, out):
    for rank in range(HEADS):
        for group in range(4):
            at = (group * HEADS + rank) * 256
            out[:, at : at + 256] = source[rank, :, group * 256 : group * 256 + 256].astype(F32)


def qkv_rows_body(source, out):
    for rank in range(HEADS):
        for part in range(3):
            at = (part * HEADS + HEAD_ORDER[rank]) * HEAD
            out[:, at : at + HEAD] = source[rank, :, part * HEAD : part * HEAD + HEAD].astype(F32)


def repack(body, name, source, out):
    return pl.pallas_call(
        body,
        name=name,
        out_shape=out,
        compiler_params=pltpu.CompilerParams(vmem_limit_bytes=16 * 2**20),
        cost_estimate=pl.CostEstimate(
            flops=0,
            bytes_accessed=source.size * source.dtype.itemsize * 3,
            transcendentals=0,
        ),
    )(source)


def over_x(block):
    return lax.ppermute(block, "dp", swap(4, 1))


def over_y(block):
    return lax.ppermute(block, "dp", swap(4, 2))


def gather_pieces(block, cut):
    along_x = over_x(block)
    along_y = over_y(block)
    return (block, along_x, along_y, over_x(along_y[:cut]), over_y(along_x[cut:]))


def reduce_pieces(pieces):
    far_top, far_low, x_top, x_low, y_top, y_low, own = pieces
    half = far_top.shape[0]
    far_x = over_x(far_top)
    far_y = over_y(far_low)
    got_x_top = over_x(x_top)
    got_y_low = over_y(y_low)
    got_y_top = over_y((y_top.astype(F32) + far_x.astype(F32)).astype(BF16))
    got_x_low = over_x((x_low.astype(F32) + far_y.astype(F32)).astype(BF16))
    top = own[:half].astype(F32) + got_x_top.astype(F32) + got_y_top.astype(F32)
    low = own[half:].astype(F32) + got_x_low.astype(F32) + got_y_low.astype(F32)
    return top, low


def rotary_lanes(length):
    position = jnp.arange(length, dtype=jnp.int32).astype(F32)
    cosine, sine = rotary_tables(position)
    blank = jnp.zeros((length, 32), F32)
    rest = jnp.zeros((length, 64), F32)
    cos = jnp.concatenate([cosine, jnp.ones((length, 64), F32)], axis=1)
    first = jnp.concatenate([-sine[:, :32], blank, rest], axis=1)
    second = jnp.concatenate([blank, sine[:, 32:], rest], axis=1)
    return cos, first, second


def line_shards(
    block_input,
    segments,
    out_grad,
    ln1_gain,
    ln1_bias,
    w_qkv,
    b_qkv,
    w_attn_out,
    b_attn_out,
    ln2_gain,
    ln2_bias,
    w_up,
    b_up,
    w_down,
    b_down,
):
    dp, sp = lax.axis_index("dp"), lax.axis_index("sp")
    dp = dp.astype(jnp.int32)
    x_own = block_input[0]
    g_own = out_grad[0]
    tokens, width = x_own.shape
    length = tokens * HEADS
    rows = w_qkv.shape[0]
    everywhere = ("dp", "sp")
    head = head_of(sp)

    x_all = lax.all_gather(x_own, "sp", axis=0, tiled=True)
    down = gather_pieces(jnp.concatenate([w_down, w_attn_out], axis=0), w_down.shape[0] // 2)
    up_blocks = repack(
        up_blocks_body, "up_blocks", w_up, jax.ShapeDtypeStruct((HEADS, rows, 1024), BF16)
    )
    up_rows = lax.all_to_all(up_blocks, "sp", 0, 0, tiled=True).reshape(HEADS * rows, 1024)
    packed = jnp.concatenate(
        [
            jnp.stack([ln1_gain, ln1_bias, ln2_gain, ln2_bias, b_attn_out, b_down]),
            b_qkv.reshape(3, 64),
            b_up.reshape(4, 64),
            segments[0].astype(BF16).reshape(2, 64),
        ]
    )
    small = lax.all_to_all(
        jnp.broadcast_to(packed[None], (32,) + packed.shape), everywhere, 0, 0, tiled=True
    )
    up = gather_pieces(up_rows, HEADS * rows // 2)
    qkv_blocks = repack(
        qkv_blocks_body, "qkv_blocks", w_qkv, jax.ShapeDtypeStruct((HEADS, rows, 768), BF16)
    )
    qkv_rows = lax.all_to_all(qkv_blocks, "sp", 0, 0, tiled=True).reshape(HEADS * rows, 768)
    w_in = gather_pieces(qkv_rows, HEADS * rows // 2)
    g_all = lax.all_gather(g_own, "sp", axis=0, tiled=True)
    cut = w_down.shape[0] // 2
    out_parts = [piece[2 * cut :] for piece in down[:3]] + [down[4][cut:]]
    out_rows = jnp.zeros((4, rows, width), BF16)
    for mask, piece in enumerate(out_parts):
        out_rows = put(out_rows, piece, dp ^ mask)
    fours = [[0, 1, 2, 3], [4, 5, 6, 7]]
    w_out = lax.all_to_all(
        out_rows, "sp", 0, 0, tiled=True, axis_index_groups=fours
    ).reshape(HEAD, width)

    vectors = small[:, :6].transpose(1, 0, 2).reshape(6, width).astype(F32)
    norm_vec = vectors[:4]
    bias_qkv = pick(small[:, 6:9].reshape(3, HEADS, HEAD), head, 1).astype(F32).reshape(1, 768)
    bias_up = pick(small[:, 9:13].reshape(4, HEADS, 256), sp, 1).astype(F32).reshape(1, 1024)
    seg = pick(small[:, 13:].reshape(4, length), dp).astype(F32)
    tables = rotary_lanes(length)

    first_in, second_in = norms(dp, x_all, norm_vec)
    active, d_hidden, up_sums = mlp(dp, second_in, g_all, up, down, bias_up)
    down_terms = terms(dp, active, [g_all], "down_terms")
    up_terms = terms(dp, second_in, [d_hidden], "up_terms")
    queries, key_rows, value_rows = qkv(dp, first_in, w_in, bias_qkv, tables)
    context, d_q, d_k, d_v, qkv_sums = attend(
        dp,
        queries,
        key_rows,
        value_rows,
        g_all,
        w_out,
        seg.reshape(length, 1),
        seg.reshape(1, length),
        tables,
    )
    out_terms = output(dp, context, active, w_out, down)
    out_sum = lax.psum_scatter(out_terms, "sp", scatter_dimension=0, tiled=True)
    u_terms, norm_sums = inward(dp, x_all, d_q, d_k, d_v, d_hidden, w_in, up, norm_vec)
    u_sum = lax.psum_scatter(u_terms, "sp", scatter_dimension=0, tiled=True)
    qkv_terms = terms(dp, first_in, [d_q, d_k, d_v], "qkv_terms")
    attn_terms = dot(context, g_all, (0, 0)).astype(BF16).reshape(4, HEAD // 4, width)
    attn_terms = lax.all_to_all(
        attn_terms, "sp", 0, 0, tiled=True, axis_index_groups=fours
    )

    grad_down = jnp.concatenate(reduce_pieces(down_terms), axis=0)
    up_sum = jnp.concatenate([half.astype(BF16) for half in reduce_pieces(up_terms)], axis=0)
    up_back = lax.all_to_all(up_sum.reshape(HEADS, rows, 1024), "sp", 0, 0, tiled=True)
    grad_up = repack(
        up_rows_body, "up_rows", up_back, jax.ShapeDtypeStruct((rows, HEADS * 1024), F32)
    )
    own, to_x, to_y, to_far = (pick(attn_terms, dp ^ mask) for mask in range(4))
    part = rows // 2
    grad_out = jnp.concatenate(
        reduce_pieces(
            (
                to_far[:part],
                to_far[part:],
                to_x[:part],
                to_x[part:],
                to_y[:part],
                to_y[part:],
                own,
            )
        ),
        axis=0,
    )
    qkv_sum = jnp.concatenate([half.astype(BF16) for half in reduce_pieces(qkv_terms)], axis=0)
    qkv_back = lax.all_to_all(qkv_sum.reshape(HEADS, rows, 768), "sp", 0, 0, tiled=True)
    grad_qkv = repack(
        qkv_rows_body, "qkv_rows", qkv_back, jax.ShapeDtypeStruct((rows, HEADS * 768), F32)
    )

    x_wide = x_own.astype(F32)
    block_output = (x_wide + out_sum.astype(F32) + (vectors[4] + vectors[5]))[None]
    u_wide = u_sum.astype(F32)
    normed, scale = normalize(x_wide)
    u_mean = jnp.mean(u_wide, axis=-1, keepdims=True)
    u_along = jnp.mean(u_wide * normed, axis=-1, keepdims=True)
    input_grad = (g_own.astype(F32) + (u_wide - u_mean - normed * u_along) * scale)[None]

    sum_qkv = lax.dynamic_update_slice(
        jnp.zeros((3, HEADS, HEAD), F32), qkv_sums.reshape(3, 1, HEAD), (0, head, 0)
    )
    sum_up = lax.dynamic_update_slice(
        jnp.zeros((4, HEADS, 256), F32), up_sums.reshape(4, 1, 256), (0, sp, 0)
    )
    sum_out = jnp.sum(g_own.astype(F32), axis=0)
    totals = jnp.concatenate(
        [
            norm_sums.reshape(4, 32, 64).transpose(1, 0, 2).reshape(32, 256),
            sum_out.reshape(32, 64),
            sum_qkv.reshape(32, 192),
            sum_up.reshape(32, 256),
        ],
        axis=1,
    )
    owned = jnp.sum(lax.all_to_all(totals, everywhere, 0, 0, tiled=True), axis=0)
    grad_g1, grad_s1, grad_g2, grad_s2, grad_bout = (
        owned[k * rows : (k + 1) * rows] for k in range(5)
    )
    return (
        block_output,
        input_grad,
        grad_g1,
        grad_s1,
        grad_qkv,
        owned[320:512],
        grad_out,
        grad_bout,
        grad_g2,
        grad_s2,
        grad_up,
        owned[512:],
        grad_down,
        grad_bout,
    )


def shards(*arrays):
    if (lax.axis_size("dp"), lax.axis_size("sp")) == (4, 8):
        return line_shards(*arrays)
    return any_shards(*arrays)


def solution(mesh):
    tokens = P("dp", "sp", None)
    split = P(("dp", "sp"))
    matrix = P(("dp", "sp"), None)
    return jax.shard_map(
        shards,
        mesh=mesh,
        in_specs=(
            tokens,
            P("dp", "sp"),
            tokens,
            split,
            split,
            matrix,
            split,
            matrix,
            split,
            split,
            split,
            matrix,
            split,
            matrix,
            split,
        ),
        out_specs=(
            tokens,
            tokens,
            split,
            split,
            matrix,
            split,
            matrix,
            split,
            split,
            split,
            matrix,
            split,
            matrix,
            split,
        ),
        check_vma=False,
    )
```

```python
import functools
import math

import jax
import jax.numpy as jnp
from jax import lax
from jax.experimental import pallas as pl
from jax.experimental.pallas import tpu as pltpu
from jax.sharding import PartitionSpec as P

HEADS = 8
HEAD = 256
ROT = 64
TILE = 256
BF16 = jnp.bfloat16
F32 = jnp.float32

def normalize(values):
    center = values - jnp.mean(values, axis=-1, keepdims=True)
    spread = jnp.mean(center * center, axis=-1, keepdims=True)
    scale = lax.rsqrt(spread + 1e-05)
    return center * scale, scale


def rotary_tables(positions):
    inverse_freq = 10000.0 ** (-jnp.arange(0, ROT, 2).astype(F32) / ROT)
    angles = positions[:, None] * inverse_freq[None, :]
    angles = jnp.concatenate([angles, angles], axis=1)
    return (jnp.cos(angles), jnp.sin(angles))


def rotate(values, cosine, sine):
    half_rot = ROT // 2
    rot_part = values[..., :ROT]
    turned = jnp.concatenate([-rot_part[..., half_rot:], rot_part[..., :half_rot]], axis=-1)
    rotated = rot_part * cosine + turned * sine
    return jnp.concatenate([rotated, values[..., ROT:]], axis=-1)


def pick(array, index, axis=0):
    return lax.dynamic_index_in_dim(array, index, axis, keepdims=False)


def put(array, piece, index):
    return lax.dynamic_update_slice_in_dim(array, piece[None], index, 0)


def swap(extent, mask):
    return [(i, i ^ mask) for i in range(extent)]


class AnyGrid:
    def __init__(self):
        self.dp = lax.axis_index("dp")
        self.sp = lax.axis_index("sp")
        self.dps = lax.axis_size("dp")
        self.sps = lax.axis_size("sp")
        self.parts = self.sps // HEADS
        self.part = self.sp // HEADS
        self.team = [
            [part * HEADS + rank for rank in range(HEADS)] for part in range(self.parts)
        ]
        self.peers = [
            [part * HEADS + rank for part in range(self.parts)] for rank in range(HEADS)
        ]

    def gather_dp(self, block):
        block = lax.all_gather(block, "sp", axis=0, axis_index_groups=self.peers)
        block = lax.all_gather(block, "dp", axis=0)
        return block.reshape((self.dps * self.parts,) + block.shape[2:])

    def reduce_dp(self, terms):
        block = terms.reshape((self.dps, self.parts) + terms.shape[1:])
        block = lax.psum_scatter(block, "dp", scatter_dimension=0)
        return lax.psum_scatter(
            block, "sp", scatter_dimension=0, axis_index_groups=self.peers
        ).astype(F32)

    def gather_sp(self, block):
        return lax.all_gather(block, "sp", axis=0, tiled=True, axis_index_groups=self.team)

    def reduce_sp(self, terms):
        return lax.psum_scatter(
            terms, "sp", scatter_dimension=0, tiled=True, axis_index_groups=self.team
        ).astype(F32)

    def exchange_sp(self, blocks):
        return lax.all_to_all(
            blocks, "sp", split_axis=0, concat_axis=0, tiled=True, axis_index_groups=self.team
        )

    def gather_small(self, vector):
        return lax.all_gather(vector, ("dp", "sp"), axis=0)

    def reduce_small(self, terms):
        return lax.psum_scatter(terms, ("dp", "sp"), scatter_dimension=0)

    def gather_out(self, block):
        whole = lax.all_gather(block, ("dp", "sp"), axis=0, tiled=True)
        return lax.dynamic_slice_in_dim(whole, head_of(self.sp % HEADS) * HEAD, HEAD, 0)

    def reduce_out(self, terms):
        whole = jnp.zeros((HEADS * HEAD, terms.shape[1]), terms.dtype)
        whole = lax.dynamic_update_slice_in_dim(whole, terms, head_of(self.sp % HEADS) * HEAD, 0)
        return lax.psum_scatter(
            whole, ("dp", "sp"), scatter_dimension=0, tiled=True
        ).astype(F32)

    def whole_keys(self, block):
        return lax.all_gather(block, "sp", axis=0, tiled=True, axis_index_groups=self.peers)

    def reduce_keys(self, terms):
        return lax.psum_scatter(
            terms, "sp", scatter_dimension=0, tiled=True, axis_index_groups=self.peers
        )


def head_of(rank):
    return 2 * (rank % 4) + rank // 4


HEAD_ORDER = [2 * (rank % 4) + rank // 4 for rank in range(HEADS)]
RANK_ORDER = [HEAD_ORDER.index(head) for head in range(HEADS)]


def dot(left, right, contract):
    return lax.dot_general(
        left, right, (((contract[0],), (contract[1],)), ((), ())), preferred_element_type=F32
    )


def any_shards(
    block_input,
    segments,
    out_grad,
    ln1_gain,
    ln1_bias,
    w_qkv,
    b_qkv,
    w_attn_out,
    b_attn_out,
    ln2_gain,
    ln2_bias,
    w_up,
    b_up,
    w_down,
    b_down,
):
    dps, sps = lax.axis_size("dp"), lax.axis_size("sp")
    devices = dps * sps
    grid = AnyGrid()
    groups = devices // HEADS
    x_own = block_input[0]
    g_own = out_grad[0]
    tokens, width = x_own.shape
    rows = w_qkv.shape[0]
    cols_up = b_up.shape[0]
    cols_qkv = b_qkv.shape[0]
    length = tokens * HEADS
    scale = 1.0 / math.sqrt(HEAD)

    packed = jnp.concatenate(
        [
            ln1_gain,
            ln1_bias,
            ln2_gain,
            ln2_bias,
            b_attn_out,
            b_down,
            b_qkv,
            b_up,
            segments[0].astype(BF16),
        ]
    )
    small = grid.gather_small(packed)
    vectors = [
        small[:, k * rows : (k + 1) * rows].reshape(width).astype(F32) for k in range(6)
    ]
    gain_one, shift_one, gain_two, shift_two, bias_out, bias_down = vectors
    at = 6 * rows
    rank = grid.sp % HEADS
    bias_qkv = small[:, at : at + cols_qkv].reshape(3, HEADS, HEAD)
    bias_qkv = pick(bias_qkv, head_of(rank), 1).astype(F32).reshape(3 * HEAD)
    at += cols_qkv
    bias_up = small[:, at : at + cols_up].reshape(groups, HEADS, cols_up)
    bias_up = pick(bias_up, rank, 1).astype(F32).reshape(groups * cols_up)
    at += cols_up
    seg_all = pick(small[:, at:].reshape(dps, sps * tokens), grid.dp)
    seg_mine = lax.dynamic_slice_in_dim(seg_all, grid.part * length, length, 0)

    x_all = grid.gather_sp(x_own)
    up_blocks = w_up.reshape(rows, groups, HEADS, cols_up).transpose(2, 0, 1, 3)
    up_blocks = up_blocks.reshape(HEADS, rows, groups * cols_up)
    up_rows = grid.exchange_sp(up_blocks).reshape(HEADS * rows, groups * cols_up)
    weight_down = grid.gather_dp(w_down).reshape(groups * cols_up, width)
    weight_up = grid.gather_dp(up_rows).reshape(width, groups * cols_up)
    qkv_blocks = w_qkv.reshape(rows, 3, HEADS, HEAD)
    qkv_blocks = jnp.stack([qkv_blocks[:, :, head] for head in HEAD_ORDER])
    qkv_blocks = qkv_blocks.reshape(HEADS, rows, 3 * HEAD)
    qkv_rows = grid.exchange_sp(qkv_blocks).reshape(HEADS * rows, 3 * HEAD)
    weight_qkv = grid.gather_dp(qkv_rows).reshape(width, 3 * HEAD)
    weight_out = grid.gather_out(w_attn_out)
    g_all = grid.gather_sp(g_own)

    normed, _ = normalize(x_all.astype(F32))
    first_in = (normed * gain_one + shift_one).astype(BF16)
    second_in = (normed * gain_two + shift_two).astype(BF16)

    hidden = dot(second_in, weight_up, (1, 0)) + bias_up
    active_wide, gelu_pull = jax.vjp(lambda v: jax.nn.gelu(v, approximate=False), hidden)
    active = active_wide.astype(BF16)
    d_active = dot(g_all, weight_down, (1, 1))
    d_hidden = gelu_pull(d_active)[0].astype(BF16)
    term_down = dot(active, g_all, (0, 0)).astype(BF16)
    term_up = dot(second_in, d_hidden, (0, 0)).astype(BF16)

    joined = dot(first_in, weight_qkv, (1, 0)) + bias_qkv
    position = grid.part * length + jnp.arange(length, dtype=jnp.int32)
    cosine, sine = rotary_tables(position.astype(F32))
    queries = rotate(joined[:, :HEAD], cosine, sine).astype(BF16)
    key_rows = grid.whole_keys(rotate(joined[:, HEAD : 2 * HEAD], cosine, sine).astype(BF16))
    value_rows = grid.whole_keys(joined[:, 2 * HEAD :].astype(BF16))
    key_position = jnp.arange(key_rows.shape[0], dtype=jnp.int32)
    allowed = (seg_mine[:, None] == seg_all[None, :]) & (
        key_position[None, :] <= position[:, None]
    )
    scores = jnp.where(allowed, dot(queries, key_rows, (1, 1)) * scale, -1e30)
    top = jnp.max(scores, axis=-1, keepdims=True)
    weights = jnp.where(allowed, jnp.exp(scores - top), 0.0)
    weight_sum = jnp.sum(weights, axis=-1, keepdims=True)
    log_sum = top + jnp.log(weight_sum)
    context = dot(weights.astype(BF16), value_rows, (1, 0)) / weight_sum
    context_low = context.astype(BF16)

    out_terms = dot(context_low, weight_out, (1, 0)) + dot(active, weight_down, (1, 0))
    out_sum = grid.reduce_sp(out_terms.astype(BF16))
    block_output = (x_own.astype(F32) + out_sum + (bias_out + bias_down))[None]

    d_context = dot(g_all, weight_out, (1, 1)).astype(BF16)
    row_delta = jnp.sum(d_context.astype(F32) * context, axis=-1, keepdims=True)
    probs = jnp.where(allowed, jnp.exp(scores - log_sum), 0.0)
    d_probs = dot(d_context, value_rows, (1, 1))
    d_scores = (probs * (d_probs - row_delta)).astype(BF16)
    d_queries = dot(d_scores, key_rows, (1, 0)) * scale
    d_keys = grid.reduce_keys(dot(d_scores, queries, (0, 0)) * scale)
    d_values = grid.reduce_keys(dot(probs.astype(BF16), d_context, (0, 0)))
    d_joined = jnp.concatenate(
        [rotate(d_queries, cosine, -sine), rotate(d_keys, cosine, -sine), d_values], axis=1
    ).astype(BF16)

    d_first = dot(d_joined, weight_qkv, (1, 1))
    d_second = dot(d_hidden, weight_up, (1, 1))
    u_terms = d_first * gain_one + d_second * gain_two
    u_sum = grid.reduce_sp(u_terms.astype(BF16))
    normed_own, scale_own = normalize(x_own.astype(F32))
    u_mean = jnp.mean(u_sum, axis=-1, keepdims=True)
    u_along = jnp.mean(u_sum * normed_own, axis=-1, keepdims=True)
    input_grad = (g_own.astype(F32) + (u_sum - u_mean - normed_own * u_along) * scale_own)[None]

    term_qkv = dot(first_in, d_joined, (0, 0)).astype(BF16)
    term_out = dot(context_low, g_all, (0, 0)).astype(BF16)
    grad_down = grid.reduce_dp(term_down.reshape(groups, cols_up, width))
    up_sum = grid.reduce_dp(term_up.reshape(groups, HEADS * rows, groups * cols_up))
    up_back = grid.exchange_sp(up_sum.astype(BF16).reshape(HEADS, rows, groups * cols_up))
    grad_up = (
        up_back.astype(F32)
        .reshape(HEADS, rows, groups, cols_up)
        .transpose(1, 2, 0, 3)
        .reshape(rows, devices * cols_up)
    )
    grad_out = grid.reduce_out(term_out)
    qkv_sum = grid.reduce_dp(term_qkv.reshape(groups, HEADS * rows, 3 * HEAD))
    qkv_back = grid.exchange_sp(qkv_sum.astype(BF16).reshape(HEADS, rows, 3, HEAD)).astype(F32)
    grad_qkv = jnp.stack([qkv_back[place] for place in RANK_ORDER], axis=2)
    grad_qkv = grad_qkv.reshape(rows, 3 * HEADS * HEAD)

    sum_qkv = jnp.zeros((3, HEADS, HEAD), F32)
    sum_qkv = lax.dynamic_update_slice(
        sum_qkv,
        jnp.sum(d_joined.astype(F32), axis=0).reshape(3, 1, HEAD),
        (0, head_of(rank), 0),
    )
    sum_up = jnp.zeros((groups, HEADS, cols_up), F32)
    sum_up = lax.dynamic_update_slice(
        sum_up,
        jnp.sum(d_hidden.astype(F32), axis=0).reshape(groups, 1, cols_up),
        (0, rank, 0),
    )
    totals = [
        jnp.sum(d_first * normed, axis=0),
        jnp.sum(d_first, axis=0),
        jnp.sum(d_second * normed, axis=0),
        jnp.sum(d_second, axis=0),
        jnp.sum(g_own.astype(F32), axis=0),
        sum_qkv,
        sum_up,
    ]
    totals = jnp.concatenate([total.reshape(devices, -1) for total in totals], axis=1)
    owned = grid.reduce_small(totals)
    parts = [owned[k * rows : (k + 1) * rows] for k in range(5)]
    grad_g1, grad_s1, grad_g2, grad_s2, grad_bout = parts
    grad_bqkv = owned[5 * rows : 5 * rows + cols_qkv]
    grad_bup = owned[5 * rows + cols_qkv :]
    return (
        block_output,
        input_grad,
        grad_g1,
        grad_s1,
        grad_qkv,
        grad_bqkv,
        grad_out,
        grad_bout,
        grad_g2,
        grad_s2,
        grad_up,
        grad_bup,
        grad_down,
        grad_bout,
    )


def fill(dp, full, pieces):
    own, along_x, along_y, far_one, far_two = pieces
    take, cols = full.shape[0] // 4, full.shape[1]
    cut = far_one.shape[0]
    for mask, piece in enumerate((own, along_x, along_y)):
        full[pl.ds(pl.multiple_of((dp ^ mask) * take, 16), take), :] = piece[0:take, 0:cols]
    far = (dp ^ 3) * take
    full[pl.ds(pl.multiple_of(far, 16), cut), :] = far_one[:, 0:cols]
    full[pl.ds(pl.multiple_of(far + cut, 16), take - cut), :] = far_two[0 : take - cut, 0:cols]


def whole(shape):
    return pl.BlockSpec(shape, lambda *_: (0,) * len(shape), pipeline_mode=pl.Buffered(1))

def tile(cols):
    return pl.BlockSpec((TILE, cols), lambda i, *_: (i, 0))

def run(body, name, dp, inputs, specs, outs, out_specs, scratch, grid, flops=0, vmem=56):
    bytes_accessed = sum(math.prod(a.shape) * a.dtype.itemsize for a in [*inputs, *jax.tree.leaves(outs)])
    return pl.pallas_call(
        body, name=name,
        grid_spec=pltpu.PrefetchScalarGridSpec(num_scalar_prefetch=1, grid=grid, in_specs=specs, out_specs=out_specs, scratch_shapes=scratch),
        out_shape=outs,
        compiler_params=pltpu.CompilerParams(vmem_limit_bytes=vmem * 2**20, dimension_semantics=("arbitrary",) * len(grid)),
        cost_estimate=pl.CostEstimate(flops=flops, bytes_accessed=bytes_accessed, transcendentals=0),
    )(dp.reshape(1), *inputs)

def shape(dims, kind):
    return jax.ShapeDtypeStruct(dims, kind)

def norm_tile(x):
    v = x.astype(F32)
    center = v - jnp.mean(v, axis=-1, keepdims=True)
    scale = lax.rsqrt(jnp.mean(center * center, axis=-1, keepdims=True) + 1e-05)
    return center * scale, scale

def norms_body(dp, x, vec, first, second):
    normed, _ = norm_tile(x[...])
    first[...] = (normed * vec[0:1, :] + vec[1:2, :]).astype(BF16)
    second[...] = (normed * vec[2:3, :] + vec[3:4, :]).astype(BF16)

def norms(dp, x, vec):
    n, w = x.shape
    return run(norms_body, "norms", dp, [x, vec], [tile(w), whole(vec.shape)], [shape((n, w), BF16)] * 2, [tile(w)] * 2, [], (n // TILE,))

def turn(v, cos, s1, s2):
    left = v[:, :128]
    out = left * cos + pltpu.roll(left, 96, 1) * s1 + pltpu.roll(left, 32, 1) * s2
    return jnp.concatenate([out, v[:, 128:]], axis=1)

def qkv_body(dp, first, w0, wx, wy, w1, w2, bias, cos, s1, s2, q, k, v, full):
    @pl.when(pl.program_id(0) == 0)
    def _():
        fill(dp[0], full, (w0, wx, wy, w1, w2))
    joined = dot(first[...], full[...], (1, 0)) + bias[...]
    q[...] = turn(joined[:, :HEAD], cos[...], s1[...], s2[...]).astype(BF16)
    k[...] = turn(joined[:, HEAD:2 * HEAD], cos[...], s1[...], s2[...]).astype(BF16)
    v[...] = joined[:, 2 * HEAD:].astype(BF16)

def qkv(dp, first, pieces, bias, tables):
    n, w = first.shape
    return run(qkv_body, "qkv", dp, [first, *pieces, bias, *tables],
        [tile(w)] + [whole(p.shape) for p in pieces] + [whole(bias.shape)] + [tile(128)] * 3,
        [shape((n, HEAD), BF16)] * 3, [tile(HEAD)] * 3, [pltpu.VMEM((w, 3 * HEAD), BF16)], (n // TILE,), flops=2 * n * w * 3 * HEAD)

def mlp_forward_body(dp, second, u0, ux, uy, u1, u2, bias, active, slope, full):
    @pl.when(pl.program_id(0) == 0)
    def _():
        fill(dp[0], full, (u0, ux, uy, u1, u2))
    hidden = dot(second[...], full[...], (1, 0)) + bias[...]
    half_cdf = 0.5 + 0.5 * lax.erf(hidden * (1.0 / math.sqrt(2.0)))
    active[...] = (hidden * half_cdf).astype(BF16)
    slope[...] = half_cdf + hidden * (jnp.exp(-0.5 * hidden * hidden) * (1.0 / math.sqrt(2.0 * math.pi)))

def mlp_forward(dp, second, up, bias):
    n, w = second.shape
    h = up[0].shape[1]
    return run(mlp_forward_body, "mlp_forward", dp, [second, *up, bias],
        [tile(w)] + [whole(p.shape) for p in (*up, bias)],
        [shape((n, h), BF16), shape((n, h), F32)], [tile(h)] * 2,
        [pltpu.VMEM((w, h), BF16)], (n // TILE,), flops=2 * n * w * h)

def mlp_backward_body(dp, g, d0, dx, dy, d1, d2, slope, d_hidden, sums, full):
    @pl.when(pl.program_id(0) == 0)
    def _():
        fill(dp[0], full, (d0, dx, dy, d1, d2))
        sums[...] = jnp.zeros_like(sums)
    low = (slope[...] * dot(g[...], full[...], (1, 1))).astype(BF16)
    d_hidden[...] = low
    sums[...] += jnp.sum(low.astype(F32), axis=0, keepdims=True)

def mlp_backward(dp, g, down, slope):
    n, w = g.shape
    h = slope.shape[1]
    return run(mlp_backward_body, "mlp_backward", dp, [g, *down, slope],
        [tile(w)] + [whole(p.shape) for p in down] + [tile(h)],
        [shape((n, h), BF16), shape((1, h), F32)], [tile(h), whole((1, h))],
        [pltpu.VMEM((h, w), BF16)], (n // TILE,), flops=2 * n * w * h)

def masked_scores(index, q, keys, seg_q, seg_k):
    reach = keys.shape[0]
    scores = dot(q, keys, (1, 1)) * (1.0 / math.sqrt(HEAD))
    row = index * TILE + lax.broadcasted_iota(jnp.int32, (TILE, reach), 0)
    col = lax.broadcasted_iota(jnp.int32, (TILE, reach), 1)
    allowed = (seg_q[...] == seg_k[:, 0:reach]) & (col <= row)
    return jnp.where(allowed, scores, -1e30), allowed

def each_tile(count, block):
    for index in range(count):
        @pl.when(pl.program_id(0) == index)
        def _(index=index):
            block(index, (index + 1) * TILE)

def attend_forward_body(dp, q, k, v, seg_q, seg_k, context, low, log_sum):
    def block(index, reach):
        scores, allowed = masked_scores(index, q[...], k[0:reach, :], seg_q, seg_k)
        top = jnp.max(scores, axis=1, keepdims=True)
        weights = jnp.where(allowed, jnp.exp(scores - top), 0.0)
        weight_sum = jnp.sum(weights, axis=1, keepdims=True)
        mixed = dot(weights.astype(BF16), v[0:reach, :], (1, 0)) / weight_sum
        context[...] = mixed
        low[...] = mixed.astype(BF16)
        log_sum[...] = top + jnp.log(weight_sum)
    each_tile(k.shape[0] // TILE, block)

def attend_forward(dp, q, k, v, seg_col, seg_row):
    n = q.shape[0]
    return run(attend_forward_body, "attend_forward", dp, [q, k, v, seg_col, seg_row],
        [tile(HEAD), whole(k.shape), whole(v.shape), tile(1), whole(seg_row.shape)],
        [shape((n, HEAD), F32), shape((n, HEAD), BF16), shape((n, 1), F32)],
        [tile(HEAD)] * 2 + [tile(1)], [], (n // TILE,), flops=3 * n * n * HEAD)

def attend_backward_body(dp, q, k, v, g, w_out, context, log_sum, seg_q, seg_k, cos, s1, s2, kcos, ks1, ks2, dq, dk, dv, sums, dk_acc, dv_acc):
    step = pl.program_id(0)
    count = k.shape[0] // TILE
    scale = 1.0 / math.sqrt(HEAD)
    @pl.when(step == 0)
    def _():
        sums[...] = jnp.zeros_like(sums)
        dk_acc[...] = jnp.zeros_like(dk_acc)
        dv_acc[...] = jnp.zeros_like(dv_acc)
    d_ctx = dot(g[...], w_out[...], (1, 1)).astype(BF16)
    def block(index, reach):
        keys, values = k[0:reach, :], v[0:reach, :]
        scores, allowed = masked_scores(index, q[...], keys, seg_q, seg_k)
        probs = jnp.where(allowed, jnp.exp(scores - log_sum[...]), 0.0)
        delta = jnp.sum(d_ctx.astype(F32) * context[...], axis=1, keepdims=True)
        d_scores = (probs * (dot(d_ctx, values, (1, 1)) - delta)).astype(BF16)
        d_q = dot(d_scores, keys, (1, 0)) * scale
        low = turn(d_q, cos[...], -s1[...], -s2[...]).astype(BF16)
        dq[...] = low
        sums[:, 0:HEAD] += jnp.sum(low.astype(F32), axis=0, keepdims=True)
        dk_acc[0:reach, :] += dot(d_scores, q[...], (0, 0))
        dv_acc[0:reach, :] += dot(probs.astype(BF16), d_ctx, (0, 0))
    each_tile(count, block)
    @pl.when(step == count - 1)
    def _():
        low_k = turn(dk_acc[...] * scale, kcos[...], -ks1[...], -ks2[...]).astype(BF16)
        low_v = dv_acc[...].astype(BF16)
        dk[...] = low_k
        dv[...] = low_v
        sums[:, HEAD:2 * HEAD] = jnp.sum(low_k.astype(F32), axis=0, keepdims=True)
        sums[:, 2 * HEAD:] = jnp.sum(low_v.astype(F32), axis=0, keepdims=True)

def attend_backward(dp, q, k, v, g, w_out, context, log_sum, seg_col, seg_row, tables):
    n = q.shape[0]; w = g.shape[1]
    return run(attend_backward_body, "attend_backward", dp, [q, k, v, g, w_out, context, log_sum, seg_col, seg_row, *tables, *tables],
        [tile(HEAD), whole(k.shape), whole(v.shape), tile(w), whole(w_out.shape), tile(HEAD), tile(1), tile(1), whole(seg_row.shape)] + [tile(128)] * 3 + [whole((n, 128))] * 3,
        [shape((n, HEAD), BF16)] * 3 + [shape((1, 3 * HEAD), F32)],
        [tile(HEAD)] + [whole((n, HEAD))] * 2 + [whole((1, 3 * HEAD))],
        [pltpu.VMEM((n, HEAD), F32)] * 2, (n // TILE,), flops=2 * n * w * HEAD + 6 * n * n * HEAD)

def output_body(dp, ctx, active, w_out, d0, dx, dy, d1, d2, out, full):
    @pl.when(pl.program_id(0) == 0)
    def _():
        fill(dp[0], full, (d0, dx, dy, d1, d2))
    out[...] = (dot(ctx[...], w_out[...], (1, 0)) + dot(active[...], full[...], (1, 0))).astype(BF16)

def output(dp, ctx, active, w_out, down):
    n, h = active.shape; w = w_out.shape[1]
    return run(output_body, "output", dp, [ctx, active, w_out, *down],
        [tile(HEAD), tile(h), whole(w_out.shape)] + [whole(p.shape) for p in down],
        [shape((n, w), BF16)], [tile(w)], [pltpu.VMEM((h, w), BF16)], (n // TILE,), flops=2 * n * w * (h + HEAD))[0]

def inward_body(dp, x, dq, dk, dv, d_hidden, w0, wx, wy, w1, w2, u0, ux, uy, u1, u2, vec, u, sums, full_qkv, full_up):
    @pl.when(pl.program_id(0) == 0)
    def _():
        fill(dp[0], full_qkv, (w0, wx, wy, w1, w2))
        fill(dp[0], full_up, (u0, ux, uy, u1, u2))
        sums[...] = jnp.zeros_like(sums)
    normed, _ = norm_tile(x[...])
    d_joined = jnp.concatenate([dq[...], dk[...], dv[...]], axis=1)
    d_first = dot(d_joined, full_qkv[...], (1, 1))
    d_second = dot(d_hidden[...], full_up[...], (1, 1))
    u[...] = (d_first * vec[0:1, :] + d_second * vec[2:3, :]).astype(BF16)
    sums[0:1, :] += jnp.sum(d_first * normed, axis=0, keepdims=True)
    sums[1:2, :] += jnp.sum(d_first, axis=0, keepdims=True)
    sums[2:3, :] += jnp.sum(d_second * normed, axis=0, keepdims=True)
    sums[3:4, :] += jnp.sum(d_second, axis=0, keepdims=True)

def inward(dp, x, dq, dk, dv, d_hidden, wq, up, vec):
    n, w = x.shape; h = d_hidden.shape[1]
    return run(inward_body, "inward", dp, [x, dq, dk, dv, d_hidden, *wq, *up, vec],
        [tile(w)] + [tile(HEAD)] * 3 + [tile(h)] + [whole(p.shape) for p in (*wq, *up, vec)],
        [shape((n, w), BF16), shape((4, w), F32)], [tile(w), whole((4, w))],
        [pltpu.VMEM((w, 3 * HEAD), BF16), pltpu.VMEM((w, h), BF16)], (n // TILE,), flops=2 * n * w * (h + 3 * HEAD))

def terms_body(count, extra, dp, left, *refs):
    rights, outs = refs[:count], refs[count + extra :]
    right = rights[0][...] if count == 1 else jnp.concatenate([r[...] for r in rights], axis=1)
    cols = right.shape[1]
    for place in range(4):
        @pl.when(pl.program_id(0) == place)
        def _(place=place):
            term = dot(left[...], right, (0, 0)).astype(BF16)
            half = term.shape[0] // 2
            parts = [outs[6]] if place == 3 else [outs[2 * place], outs[2 * place + 1]]
            for part, out in enumerate(parts):
                rows = out.shape[0]
                out[:, 0:cols] = term[part * half : part * half + rows]
                if extra:
                    out[:, cols:] = refs[count][part * half : part * half + rows, :]

def order_mask(step):
    return jnp.where(step == 0, 3, jnp.where(step == 3, 0, step))

def terms(dp, left, rights, name, extra=()):
    n, w = left.shape; rows = w // 4; cols = sum(r.shape[1] for r in (*rights, *extra))
    outs = [shape((rows // 2, cols), BF16)] * 6 + [shape((rows, cols), BF16)]
    return run(functools.partial(terms_body, len(rights), len(extra)), name, dp, [left, *rights, *extra],
        [pl.BlockSpec((n, rows), lambda i, d: (0, d[0] ^ order_mask(i)))] + [whole(r.shape) for r in rights]
        + [pl.BlockSpec((rows, e.shape[1]), lambda i, d: (d[0] ^ order_mask(i), 0)) for e in extra],
        outs, [whole(o.shape) for o in outs], [], (4,), flops=2 * n * w * cols)


def up_blocks_body(source, out):
    for rank in range(HEADS):
        for group in range(4):
            at = (group * HEADS + rank) * 256
            out[rank, :, group * 256 : group * 256 + 256] = source[:, at : at + 256]


def qkv_blocks_body(source, packed, out):
    for rank in range(HEADS):
        for part in range(3):
            at = (part * HEADS + HEAD_ORDER[rank]) * HEAD
            out[rank, :, part * HEAD : part * HEAD + HEAD] = source[:, at : at + HEAD]
        out[rank, :, 3 * HEAD :] = packed[...]


def out_rows_body(dp, own, along_x, along_y, far, out):
    for mask, piece in enumerate((own, along_x, along_y)):
        out[dp[0] ^ mask] = piece[256:, :]
    out[dp[0] ^ 3] = far[128:, :]


def up_rows_body(source, out):
    for rank in range(HEADS):
        for group in range(4):
            at = (group * HEADS + rank) * 256
            out[:, at : at + 256] = source[rank, :, group * 256 : group * 256 + 256].astype(F32)


def qkv_rows_body(source, out):
    for rank in range(HEADS):
        for part in range(3):
            at = (part * HEADS + HEAD_ORDER[rank]) * HEAD
            out[:, at : at + HEAD] = source[rank, :, part * HEAD : part * HEAD + HEAD].astype(F32)


def repack(body, name, out, *sources):
    return pl.pallas_call(
        body,
        name=name,
        out_shape=out,
        compiler_params=pltpu.CompilerParams(vmem_limit_bytes=16 * 2**20),
        cost_estimate=pl.CostEstimate(
            flops=0,
            bytes_accessed=sources[0].size * 6,
            transcendentals=0,
        ),
    )(*sources)


def tie(value, *others):
    return lax.optimization_barrier((value, others))[0]


def stage(values, done):
    return lax.optimization_barrier((tuple(values), tuple(done)))[0]


def over_x(block):
    return lax.ppermute(block, "dp", swap(4, 1))


def over_y(block):
    return lax.ppermute(block, "dp", swap(4, 2))


def pass_on(near, far):
    _, x_low, y_top, _ = near
    far_x, far_y = far
    got_y_top = over_y((y_top.astype(F32) + far_x.astype(F32)).astype(BF16))
    got_x_low = over_x((x_low.astype(F32) + far_y.astype(F32)).astype(BF16))
    return got_y_top, got_x_low


def reduce_last(own, near, then, kind):
    half = own.shape[0] // 2
    got_x_top, got_y_low = near
    got_y_top, got_x_low = then
    top = own[:half].astype(F32) + got_x_top.astype(F32) + got_y_top.astype(F32)
    low = own[half:].astype(F32) + got_x_low.astype(F32) + got_y_low.astype(F32)
    return jnp.concatenate([top.astype(kind), low.astype(kind)], axis=0)


def rotary_lanes(length):
    position = jnp.arange(length, dtype=jnp.int32).astype(F32)
    cosine, sine = rotary_tables(position)
    blank = jnp.zeros((length, 32), F32)
    rest = jnp.zeros((length, 64), F32)
    cos = jnp.concatenate([cosine, jnp.ones((length, 64), F32)], axis=1)
    first = jnp.concatenate([-sine[:, :32], blank, rest], axis=1)
    second = jnp.concatenate([blank, sine[:, 32:], rest], axis=1)
    return cos, first, second


def line_shards(
    block_input,
    segments,
    out_grad,
    ln1_gain,
    ln1_bias,
    w_qkv,
    b_qkv,
    w_attn_out,
    b_attn_out,
    ln2_gain,
    ln2_bias,
    w_up,
    b_up,
    w_down,
    b_down,
):
    dp, sp = lax.axis_index("dp"), lax.axis_index("sp")
    dp = dp.astype(jnp.int32)
    x_own = block_input[0]
    g_own = out_grad[0]
    tokens, width = x_own.shape
    length = tokens * HEADS
    rows = w_qkv.shape[0]
    everywhere = ("dp", "sp")
    head = head_of(sp)

    fours = [[0, 1, 2, 3], [4, 5, 6, 7]]
    x_all = lax.all_gather(x_own, "sp", axis=0, tiled=True)
    down_own = jnp.concatenate([w_down, w_attn_out], axis=0)
    down_x, down_y = over_x(down_own), over_y(down_own)
    packed = jnp.concatenate(
        [
            jnp.stack([ln1_gain, ln1_bias, ln2_gain, ln2_bias, b_attn_out, b_down]),
            b_qkv.reshape(3, 64),
            b_up.reshape(4, 64),
            segments[0].astype(BF16).reshape(2, 64),
        ]
    )
    packed = jnp.pad(packed, ((0, rows - 15), (0, 64)))
    qkv_blocks = repack(
        qkv_blocks_body, "qkv_blocks", jax.ShapeDtypeStruct((HEADS, rows, 896), BF16), w_qkv, packed
    )
    up_blocks = repack(
        up_blocks_body, "up_blocks", jax.ShapeDtypeStruct((HEADS, rows, 1024), BF16), w_up
    )
    cos, sin_one, sin_two = rotary_lanes(length)
    qkv_rows = lax.all_to_all(qkv_blocks, "sp", 0, 0, tiled=True).reshape(HEADS * rows, 896)

    cut = w_down.shape[0] // 2
    half = HEADS * rows // 2
    down_far = over_x(down_y[:cut]), over_y(down_x[cut:])
    sum_out = jnp.sum(g_own.astype(F32), axis=0)
    up_blocks, qkv_rows, down_far, cos, sin_one, sin_two, sum_out = stage(
        (up_blocks, qkv_rows, down_far, cos, sin_one, sin_two, sum_out), ()
    )
    tables = (cos, sin_one, sin_two)
    down = (down_own, down_x, down_y, *down_far)
    up_rows = lax.all_to_all(up_blocks, "sp", 0, 0, tiled=True).reshape(HEADS * rows, 1024)
    qkv_x, qkv_y = over_x(qkv_rows), over_y(qkv_rows)
    out_rows = run(
        out_rows_body, "out_rows", dp, [*down[:3], down[4]], [whole(d.shape) for d in (*down[:3], down[4])],
        shape((4, rows, width), BF16), whole((4, rows, width)), [], (1,),
    )

    qkv_x, qkv_y, out_rows = stage((qkv_x, qkv_y, out_rows), ())
    qkv_far = over_x(qkv_y[:half]), over_y(qkv_x[half:])

    up_rows, qkv_far, g_late, out_rows = stage((up_rows, qkv_far, g_own, out_rows), ())
    w_in = (qkv_rows, qkv_x, qkv_y, *qkv_far)
    g_all = lax.all_gather(g_late, "sp", axis=0, tiled=True)
    up_x, up_y = over_x(up_rows), over_y(up_rows)
    w_out = lax.all_to_all(
        out_rows, "sp", 0, 0, tiled=True, axis_index_groups=fours
    ).reshape(HEAD, width)

    small = jnp.zeros((4, HEADS, 15, 64), BF16)
    far = jnp.concatenate([piece[:, 768:832] for piece in qkv_far], axis=0)
    for mask, piece in enumerate([piece[:, 768:832] for piece in w_in[:3]] + [far]):
        small = put(small, piece.reshape(HEADS, rows, 64)[:, :15], dp ^ mask)
    small = small.reshape(32, 15, 64)
    vectors = small[:, :6].transpose(1, 0, 2).reshape(6, width).astype(F32)
    norm_vec = vectors[:4]
    bias_qkv = pick(small[:, 6:9].reshape(3, HEADS, HEAD), head, 1).astype(F32).reshape(1, 768)
    bias_up = pick(small[:, 9:13].reshape(4, HEADS, 256), sp, 1).astype(F32).reshape(1, 1024)
    seg = pick(small[:, 13:].reshape(4, length), dp).astype(F32)
    seg_col, seg_row = seg.reshape(length, 1), seg.reshape(1, length)
    first_in, second_in = norms(dp, x_all, norm_vec)
    queries, key_rows, value_rows = qkv(dp, first_in, w_in, bias_qkv, tables)

    up_x, up_y, queries, w_out = stage((up_x, up_y, queries, w_out), (bias_up, seg_col, seg_row))
    up = (up_rows, up_x, up_y, over_x(up_y[:half]), over_y(up_x[half:]))

    wide_context, context, log_sum = attend_forward(
        dp, queries, key_rows, value_rows, seg_col, seg_row
    )
    up, context = stage((up, context), ())
    active, slope = mlp_forward(dp, second_in, up, bias_up)
    out_terms = output(dp, context, active, w_out, down)
    out_sum = lax.psum_scatter(out_terms, "sp", scatter_dimension=0, tiled=True)

    attn_terms = dot(tie(context, out_terms), g_all, (0, 0)).astype(BF16)
    attn_sent = lax.all_to_all(
        attn_terms.reshape(4, HEAD // 4, width), "sp", 0, 0, tiled=True, axis_index_groups=fours
    )
    d_hidden, up_sums = mlp_backward(dp, tie(g_all, attn_terms), down, slope)
    up_terms = terms(dp, second_in, [d_hidden], "up_terms")
    up_far = over_x(up_terms[0]), over_y(up_terms[1])
    d_q, d_k, d_v, qkv_sums = attend_backward(
        dp,
        tie(queries, up_terms),
        key_rows,
        value_rows,
        g_all,
        w_out,
        wide_context,
        log_sum,
        seg_col,
        seg_row,
        tables,
    )
    own, to_x, to_y, to_far = (pick(attn_sent, dp ^ mask) for mask in range(4))
    part = rows // 2
    attn_near = (to_x[:part], to_x[part:], to_y[:part], to_y[part:])
    up_near, to_far = stage((up_terms[2:6], to_far), (d_q,))
    up_near_got = over_x(up_near[0]), over_y(up_near[3])
    attn_far = over_x(to_far[:part]), over_y(to_far[part:])
    sum_qkv = lax.dynamic_update_slice(
        jnp.zeros((3, HEADS, HEAD), F32), qkv_sums.reshape(3, 1, HEAD), (0, head, 0)
    )
    sum_up = lax.dynamic_update_slice(
        jnp.zeros((4, HEADS, 256), F32), up_sums.reshape(4, 1, 256), (0, sp, 0)
    )
    early = jnp.concatenate(
        [sum_out.reshape(32, 64), sum_qkv.reshape(32, 192), sum_up.reshape(32, 256)], axis=1
    )
    u_terms, norm_sums = inward(
        dp, tie(x_all, up_far), d_q, d_k, d_v, d_hidden, w_in, up, norm_vec
    )
    up_near, attn_near = stage((up_near, attn_near), (up_near_got, attn_far))
    up_then = pass_on(up_near, up_far)
    attn_near_got = over_x(attn_near[0]), over_y(attn_near[3])
    u_terms, early, norm_sums = stage((u_terms, early, norm_sums), (out_sum, up_near_got))
    u_sum = lax.psum_scatter(u_terms, "sp", scatter_dimension=0, tiled=True)
    totals = jnp.concatenate(
        [norm_sums.reshape(4, 32, 64).transpose(1, 0, 2).reshape(32, 256), early], axis=1
    )
    totals = jnp.pad(totals.astype(BF16).reshape(32, 6, 128), ((0, 0), (0, rows - 6), (0, 0)))
    totals = totals.reshape(32 * rows, 128)
    qkv_terms = terms(dp, tie(first_in, u_terms), [d_q, d_k, d_v], "qkv_terms", (totals,))

    qkv_terms, up_then = stage((qkv_terms, up_then), (attn_near_got,))
    up_sum = reduce_last(up_terms[6], up_near_got, up_then, BF16)
    up_back = lax.all_to_all(up_sum.reshape(HEADS, rows, 1024), "sp", 0, 0, tiled=True)
    qkv_far = over_x(qkv_terms[0]), over_y(qkv_terms[1])
    qkv_near_got = over_x(qkv_terms[2]), over_y(qkv_terms[5])
    down_terms = terms(dp, tie(active, up_sum), [g_all], "down_terms")

    qkv_far, qkv_near_got, down_terms = stage((qkv_far, qkv_near_got, down_terms), ())
    qkv_then = pass_on(qkv_terms[2:6], qkv_far)
    attn_then = pass_on(attn_near, attn_far)

    qkv_then, down_terms = stage((qkv_then, down_terms), (attn_then, up_back))
    qkv_sum = reduce_last(qkv_terms[6], qkv_near_got, qkv_then, BF16)
    qkv_back = lax.all_to_all(qkv_sum.reshape(HEADS, rows, 896), "sp", 0, 0, tiled=True)
    down_far = over_x(down_terms[0]), over_y(down_terms[1])
    down_near_got = over_x(down_terms[2]), over_y(down_terms[5])

    down_far, down_terms = stage((down_far, down_terms), (down_near_got, qkv_sum))
    grad_out = reduce_last(own, attn_near_got, attn_then, F32)
    grad_up = repack(
        up_rows_body, "up_rows", jax.ShapeDtypeStruct((rows, HEADS * 1024), F32), up_back
    )
    down_then = pass_on(down_terms[2:6], down_far)
    down_then = stage(down_then, (qkv_back, grad_up, grad_out))
    grad_down = reduce_last(down_terms[6], down_near_got, down_then, F32)
    grad_qkv = repack(
        qkv_rows_body, "qkv_rows", jax.ShapeDtypeStruct((rows, HEADS * 768), F32), qkv_back
    )
    owned = jnp.sum(qkv_back[:, :6, 768:].astype(F32), axis=0).reshape(768)

    x_wide = x_own.astype(F32)
    block_output = (x_wide + out_sum.astype(F32) + (vectors[4] + vectors[5]))[None]
    u_wide = u_sum.astype(F32)
    normed, scale = normalize(x_wide)
    u_mean = jnp.mean(u_wide, axis=-1, keepdims=True)
    u_along = jnp.mean(u_wide * normed, axis=-1, keepdims=True)
    input_grad = (g_own.astype(F32) + (u_wide - u_mean - normed * u_along) * scale)[None]

    grad_g1, grad_s1, grad_g2, grad_s2, grad_bout = (
        owned[k * rows : (k + 1) * rows] for k in range(5)
    )
    return (
        block_output,
        input_grad,
        grad_g1,
        grad_s1,
        grad_qkv,
        owned[320:512],
        grad_out,
        grad_bout,
        grad_g2,
        grad_s2,
        grad_up,
        owned[512:],
        grad_down,
        grad_bout,
    )


def shards(*arrays):
    if (lax.axis_size("dp"), lax.axis_size("sp")) == (4, 8):
        return line_shards(*arrays)
    return any_shards(*arrays)


def solution(mesh):
    tokens = P("dp", "sp", None)
    split = P(("dp", "sp"))
    matrix = P(("dp", "sp"), None)
    return jax.shard_map(
        shards,
        mesh=mesh,
        in_specs=(
            tokens,
            P("dp", "sp"),
            tokens,
            split,
            split,
            matrix,
            split,
            matrix,
            split,
            split,
            split,
            matrix,
            split,
            matrix,
            split,
        ),
        out_specs=(
            tokens,
            tokens,
            split,
            split,
            matrix,
            split,
            matrix,
            split,
            split,
            split,
            matrix,
            split,
            matrix,
            split,
        ),
        check_vma=False,
    )
```

```python
import functools
import math

import jax
import jax.numpy as jnp
from jax import lax
from jax.experimental import pallas as pl
from jax.experimental.pallas import tpu as pltpu
from jax.sharding import PartitionSpec as P

HEADS = 8
HEAD = 256
ROT = 64
TILE = 256
BF16 = jnp.bfloat16
F32 = jnp.float32

def normalize(values):
    center = values - jnp.mean(values, axis=-1, keepdims=True)
    spread = jnp.mean(center * center, axis=-1, keepdims=True)
    scale = lax.rsqrt(spread + 1e-05)
    return center * scale, scale


def rotary_tables(positions):
    inverse_freq = 10000.0 ** (-jnp.arange(0, ROT, 2).astype(F32) / ROT)
    angles = positions[:, None] * inverse_freq[None, :]
    angles = jnp.concatenate([angles, angles], axis=1)
    return (jnp.cos(angles), jnp.sin(angles))


def rotate(values, cosine, sine):
    half_rot = ROT // 2
    rot_part = values[..., :ROT]
    turned = jnp.concatenate([-rot_part[..., half_rot:], rot_part[..., :half_rot]], axis=-1)
    rotated = rot_part * cosine + turned * sine
    return jnp.concatenate([rotated, values[..., ROT:]], axis=-1)


def pick(array, index, axis=0):
    return lax.dynamic_index_in_dim(array, index, axis, keepdims=False)


def put(array, piece, index):
    return lax.dynamic_update_slice_in_dim(array, piece[None], index, 0)


def swap(extent, mask):
    return [(i, i ^ mask) for i in range(extent)]


class AnyGrid:
    def __init__(self):
        self.dp = lax.axis_index("dp")
        self.sp = lax.axis_index("sp")
        self.dps = lax.axis_size("dp")
        self.sps = lax.axis_size("sp")
        self.parts = self.sps // HEADS
        self.part = self.sp // HEADS
        self.team = [
            [part * HEADS + rank for rank in range(HEADS)] for part in range(self.parts)
        ]
        self.peers = [
            [part * HEADS + rank for part in range(self.parts)] for rank in range(HEADS)
        ]

    def gather_dp(self, block):
        block = lax.all_gather(block, "sp", axis=0, axis_index_groups=self.peers)
        block = lax.all_gather(block, "dp", axis=0)
        return block.reshape((self.dps * self.parts,) + block.shape[2:])

    def reduce_dp(self, terms):
        block = terms.reshape((self.dps, self.parts) + terms.shape[1:])
        block = lax.psum_scatter(block, "dp", scatter_dimension=0)
        return lax.psum_scatter(
            block, "sp", scatter_dimension=0, axis_index_groups=self.peers
        ).astype(F32)

    def gather_sp(self, block):
        return lax.all_gather(block, "sp", axis=0, tiled=True, axis_index_groups=self.team)

    def reduce_sp(self, terms):
        return lax.psum_scatter(
            terms, "sp", scatter_dimension=0, tiled=True, axis_index_groups=self.team
        ).astype(F32)

    def exchange_sp(self, blocks):
        return lax.all_to_all(
            blocks, "sp", split_axis=0, concat_axis=0, tiled=True, axis_index_groups=self.team
        )

    def gather_small(self, vector):
        return lax.all_gather(vector, ("dp", "sp"), axis=0)

    def reduce_small(self, terms):
        return lax.psum_scatter(terms, ("dp", "sp"), scatter_dimension=0)

    def gather_out(self, block):
        whole = lax.all_gather(block, ("dp", "sp"), axis=0, tiled=True)
        return lax.dynamic_slice_in_dim(whole, head_of(self.sp % HEADS) * HEAD, HEAD, 0)

    def reduce_out(self, terms):
        whole = jnp.zeros((HEADS * HEAD, terms.shape[1]), terms.dtype)
        whole = lax.dynamic_update_slice_in_dim(whole, terms, head_of(self.sp % HEADS) * HEAD, 0)
        return lax.psum_scatter(
            whole, ("dp", "sp"), scatter_dimension=0, tiled=True
        ).astype(F32)

    def whole_keys(self, block):
        return lax.all_gather(block, "sp", axis=0, tiled=True, axis_index_groups=self.peers)

    def reduce_keys(self, terms):
        return lax.psum_scatter(
            terms, "sp", scatter_dimension=0, tiled=True, axis_index_groups=self.peers
        )


def head_of(rank):
    return 2 * (rank % 4) + rank // 4


HEAD_ORDER = [2 * (rank % 4) + rank // 4 for rank in range(HEADS)]
RANK_ORDER = [HEAD_ORDER.index(head) for head in range(HEADS)]


def dot(left, right, contract):
    return lax.dot_general(
        left, right, (((contract[0],), (contract[1],)), ((), ())), preferred_element_type=F32
    )


def any_shards(
    block_input,
    segments,
    out_grad,
    ln1_gain,
    ln1_bias,
    w_qkv,
    b_qkv,
    w_attn_out,
    b_attn_out,
    ln2_gain,
    ln2_bias,
    w_up,
    b_up,
    w_down,
    b_down,
):
    dps, sps = lax.axis_size("dp"), lax.axis_size("sp")
    devices = dps * sps
    grid = AnyGrid()
    groups = devices // HEADS
    x_own = block_input[0]
    g_own = out_grad[0]
    tokens, width = x_own.shape
    rows = w_qkv.shape[0]
    cols_up = b_up.shape[0]
    cols_qkv = b_qkv.shape[0]
    length = tokens * HEADS
    scale = 1.0 / math.sqrt(HEAD)

    packed = jnp.concatenate(
        [
            ln1_gain,
            ln1_bias,
            ln2_gain,
            ln2_bias,
            b_attn_out,
            b_down,
            b_qkv,
            b_up,
            segments[0].astype(BF16),
        ]
    )
    small = grid.gather_small(packed)
    vectors = [
        small[:, k * rows : (k + 1) * rows].reshape(width).astype(F32) for k in range(6)
    ]
    gain_one, shift_one, gain_two, shift_two, bias_out, bias_down = vectors
    at = 6 * rows
    rank = grid.sp % HEADS
    bias_qkv = small[:, at : at + cols_qkv].reshape(3, HEADS, HEAD)
    bias_qkv = pick(bias_qkv, head_of(rank), 1).astype(F32).reshape(3 * HEAD)
    at += cols_qkv
    bias_up = small[:, at : at + cols_up].reshape(groups, HEADS, cols_up)
    bias_up = pick(bias_up, rank, 1).astype(F32).reshape(groups * cols_up)
    at += cols_up
    seg_all = pick(small[:, at:].reshape(dps, sps * tokens), grid.dp)
    seg_mine = lax.dynamic_slice_in_dim(seg_all, grid.part * length, length, 0)

    x_all = grid.gather_sp(x_own)
    up_blocks = w_up.reshape(rows, groups, HEADS, cols_up).transpose(2, 0, 1, 3)
    up_blocks = up_blocks.reshape(HEADS, rows, groups * cols_up)
    up_rows = grid.exchange_sp(up_blocks).reshape(HEADS * rows, groups * cols_up)
    weight_down = grid.gather_dp(w_down).reshape(groups * cols_up, width)
    weight_up = grid.gather_dp(up_rows).reshape(width, groups * cols_up)
    qkv_blocks = w_qkv.reshape(rows, 3, HEADS, HEAD)
    qkv_blocks = jnp.stack([qkv_blocks[:, :, head] for head in HEAD_ORDER])
    qkv_blocks = qkv_blocks.reshape(HEADS, rows, 3 * HEAD)
    qkv_rows = grid.exchange_sp(qkv_blocks).reshape(HEADS * rows, 3 * HEAD)
    weight_qkv = grid.gather_dp(qkv_rows).reshape(width, 3 * HEAD)
    weight_out = grid.gather_out(w_attn_out)
    g_all = grid.gather_sp(g_own)

    normed, _ = normalize(x_all.astype(F32))
    first_in = (normed * gain_one + shift_one).astype(BF16)
    second_in = (normed * gain_two + shift_two).astype(BF16)

    hidden = dot(second_in, weight_up, (1, 0)) + bias_up
    active_wide, gelu_pull = jax.vjp(lambda v: jax.nn.gelu(v, approximate=False), hidden)
    active = active_wide.astype(BF16)
    d_active = dot(g_all, weight_down, (1, 1))
    d_hidden = gelu_pull(d_active)[0].astype(BF16)
    term_down = dot(active, g_all, (0, 0)).astype(BF16)
    term_up = dot(second_in, d_hidden, (0, 0)).astype(BF16)

    joined = dot(first_in, weight_qkv, (1, 0)) + bias_qkv
    position = grid.part * length + jnp.arange(length, dtype=jnp.int32)
    cosine, sine = rotary_tables(position.astype(F32))
    queries = rotate(joined[:, :HEAD], cosine, sine).astype(BF16)
    key_rows = grid.whole_keys(rotate(joined[:, HEAD : 2 * HEAD], cosine, sine).astype(BF16))
    value_rows = grid.whole_keys(joined[:, 2 * HEAD :].astype(BF16))
    key_position = jnp.arange(key_rows.shape[0], dtype=jnp.int32)
    allowed = (seg_mine[:, None] == seg_all[None, :]) & (
        key_position[None, :] <= position[:, None]
    )
    scores = jnp.where(allowed, dot(queries, key_rows, (1, 1)) * scale, -1e30)
    top = jnp.max(scores, axis=-1, keepdims=True)
    weights = jnp.where(allowed, jnp.exp(scores - top), 0.0)
    weight_sum = jnp.sum(weights, axis=-1, keepdims=True)
    log_sum = top + jnp.log(weight_sum)
    context = dot(weights.astype(BF16), value_rows, (1, 0)) / weight_sum
    context_low = context.astype(BF16)

    out_terms = dot(context_low, weight_out, (1, 0)) + dot(active, weight_down, (1, 0))
    out_sum = grid.reduce_sp(out_terms.astype(BF16))
    block_output = (x_own.astype(F32) + out_sum + (bias_out + bias_down))[None]

    d_context = dot(g_all, weight_out, (1, 1)).astype(BF16)
    row_delta = jnp.sum(d_context.astype(F32) * context, axis=-1, keepdims=True)
    probs = jnp.where(allowed, jnp.exp(scores - log_sum), 0.0)
    d_probs = dot(d_context, value_rows, (1, 1))
    d_scores = (probs * (d_probs - row_delta)).astype(BF16)
    d_queries = dot(d_scores, key_rows, (1, 0)) * scale
    d_keys = grid.reduce_keys(dot(d_scores, queries, (0, 0)) * scale)
    d_values = grid.reduce_keys(dot(probs.astype(BF16), d_context, (0, 0)))
    d_joined = jnp.concatenate(
        [rotate(d_queries, cosine, -sine), rotate(d_keys, cosine, -sine), d_values], axis=1
    ).astype(BF16)

    d_first = dot(d_joined, weight_qkv, (1, 1))
    d_second = dot(d_hidden, weight_up, (1, 1))
    u_terms = d_first * gain_one + d_second * gain_two
    u_sum = grid.reduce_sp(u_terms.astype(BF16))
    normed_own, scale_own = normalize(x_own.astype(F32))
    u_mean = jnp.mean(u_sum, axis=-1, keepdims=True)
    u_along = jnp.mean(u_sum * normed_own, axis=-1, keepdims=True)
    input_grad = (g_own.astype(F32) + (u_sum - u_mean - normed_own * u_along) * scale_own)[None]

    term_qkv = dot(first_in, d_joined, (0, 0)).astype(BF16)
    term_out = dot(context_low, g_all, (0, 0)).astype(BF16)
    grad_down = grid.reduce_dp(term_down.reshape(groups, cols_up, width))
    up_sum = grid.reduce_dp(term_up.reshape(groups, HEADS * rows, groups * cols_up))
    up_back = grid.exchange_sp(up_sum.astype(BF16).reshape(HEADS, rows, groups * cols_up))
    grad_up = (
        up_back.astype(F32)
        .reshape(HEADS, rows, groups, cols_up)
        .transpose(1, 2, 0, 3)
        .reshape(rows, devices * cols_up)
    )
    grad_out = grid.reduce_out(term_out)
    qkv_sum = grid.reduce_dp(term_qkv.reshape(groups, HEADS * rows, 3 * HEAD))
    qkv_back = grid.exchange_sp(qkv_sum.astype(BF16).reshape(HEADS, rows, 3, HEAD)).astype(F32)
    grad_qkv = jnp.stack([qkv_back[place] for place in RANK_ORDER], axis=2)
    grad_qkv = grad_qkv.reshape(rows, 3 * HEADS * HEAD)

    sum_qkv = jnp.zeros((3, HEADS, HEAD), F32)
    sum_qkv = lax.dynamic_update_slice(
        sum_qkv,
        jnp.sum(d_joined.astype(F32), axis=0).reshape(3, 1, HEAD),
        (0, head_of(rank), 0),
    )
    sum_up = jnp.zeros((groups, HEADS, cols_up), F32)
    sum_up = lax.dynamic_update_slice(
        sum_up,
        jnp.sum(d_hidden.astype(F32), axis=0).reshape(groups, 1, cols_up),
        (0, rank, 0),
    )
    totals = [
        jnp.sum(d_first * normed, axis=0),
        jnp.sum(d_first, axis=0),
        jnp.sum(d_second * normed, axis=0),
        jnp.sum(d_second, axis=0),
        jnp.sum(g_own.astype(F32), axis=0),
        sum_qkv,
        sum_up,
    ]
    totals = jnp.concatenate([total.reshape(devices, -1) for total in totals], axis=1)
    owned = grid.reduce_small(totals)
    parts = [owned[k * rows : (k + 1) * rows] for k in range(5)]
    grad_g1, grad_s1, grad_g2, grad_s2, grad_bout = parts
    grad_bqkv = owned[5 * rows : 5 * rows + cols_qkv]
    grad_bup = owned[5 * rows + cols_qkv :]
    return (
        block_output,
        input_grad,
        grad_g1,
        grad_s1,
        grad_qkv,
        grad_bqkv,
        grad_out,
        grad_bout,
        grad_g2,
        grad_s2,
        grad_up,
        grad_bup,
        grad_down,
        grad_bout,
    )


def fill(dp, full, pieces):
    own, along_x, along_y, far_one, far_two = pieces
    take, cols = full.shape[0] // 4, full.shape[1]
    cut = far_one.shape[0]
    for mask, piece in enumerate((own, along_x, along_y)):
        full[pl.ds(pl.multiple_of((dp ^ mask) * take, 16), take), :] = piece[0:take, 0:cols]
    far = (dp ^ 3) * take
    full[pl.ds(pl.multiple_of(far, 16), cut), :] = far_one[:, 0:cols]
    full[pl.ds(pl.multiple_of(far + cut, 16), take - cut), :] = far_two[0 : take - cut, 0:cols]


def whole(shape):
    return pl.BlockSpec(shape, lambda *_: (0,) * len(shape), pipeline_mode=pl.Buffered(1))

def tile(cols):
    return pl.BlockSpec((TILE, cols), lambda i, *_: (i, 0))

def run(body, name, dp, inputs, specs, outs, out_specs, scratch, grid, flops=0, vmem=56):
    bytes_accessed = sum(math.prod(a.shape) * a.dtype.itemsize for a in [*inputs, *jax.tree.leaves(outs)])
    return pl.pallas_call(
        body, name=name,
        grid_spec=pltpu.PrefetchScalarGridSpec(num_scalar_prefetch=1, grid=grid, in_specs=specs, out_specs=out_specs, scratch_shapes=scratch),
        out_shape=outs,
        compiler_params=pltpu.CompilerParams(vmem_limit_bytes=vmem * 2**20, dimension_semantics=("arbitrary",) * len(grid)),
        cost_estimate=pl.CostEstimate(flops=flops, bytes_accessed=bytes_accessed, transcendentals=0),
    )(dp.reshape(1), *inputs)

def shape(dims, kind):
    return jax.ShapeDtypeStruct(dims, kind)

def norm_tile(x):
    v = x.astype(F32)
    center = v - jnp.mean(v, axis=-1, keepdims=True)
    scale = lax.rsqrt(jnp.mean(center * center, axis=-1, keepdims=True) + 1e-05)
    return center * scale, scale

def norms_body(dp, x, vec, first, second):
    normed, _ = norm_tile(x[...])
    first[...] = (normed * vec[0:1, :] + vec[1:2, :]).astype(BF16)
    second[...] = (normed * vec[2:3, :] + vec[3:4, :]).astype(BF16)

def norms(dp, x, vec):
    n, w = x.shape
    return run(norms_body, "norms", dp, [x, vec], [tile(w), whole(vec.shape)], [shape((n, w), BF16)] * 2, [tile(w)] * 2, [], (n // TILE,))

def turn(v, cos, s1, s2):
    left = v[:, :128]
    out = left * cos + pltpu.roll(left, 96, 1) * s1 + pltpu.roll(left, 32, 1) * s2
    return jnp.concatenate([out, v[:, 128:]], axis=1)

def qkv_body(dp, first, w0, wx, wy, w1, w2, bias, cos, s1, s2, q, k, v, full):
    @pl.when(pl.program_id(0) == 0)
    def _():
        fill(dp[0], full, (w0, wx, wy, w1, w2))
    joined = dot(first[...], full[...], (1, 0)) + bias[...]
    q[...] = turn(joined[:, :HEAD], cos[...], s1[...], s2[...]).astype(BF16)
    k[...] = turn(joined[:, HEAD:2 * HEAD], cos[...], s1[...], s2[...]).astype(BF16)
    v[...] = joined[:, 2 * HEAD:].astype(BF16)

def qkv(dp, first, pieces, bias, tables):
    n, w = first.shape
    return run(qkv_body, "qkv", dp, [first, *pieces, bias, *tables],
        [tile(w)] + [whole(p.shape) for p in pieces] + [whole(bias.shape)] + [tile(128)] * 3,
        [shape((n, HEAD), BF16)] * 3, [tile(HEAD)] * 3, [pltpu.VMEM((w, 3 * HEAD), BF16)], (n // TILE,), flops=2 * n * w * 3 * HEAD)

def mlp_forward_body(dp, second, u0, ux, uy, u1, u2, bias, active, slope, full):
    @pl.when(pl.program_id(0) == 0)
    def _():
        fill(dp[0], full, (u0, ux, uy, u1, u2))
    hidden = dot(second[...], full[...], (1, 0)) + bias[...]
    half_cdf = 0.5 + 0.5 * lax.erf(hidden * (1.0 / math.sqrt(2.0)))
    active[...] = (hidden * half_cdf).astype(BF16)
    slope[...] = half_cdf + hidden * (jnp.exp(-0.5 * hidden * hidden) * (1.0 / math.sqrt(2.0 * math.pi)))

def mlp_forward(dp, second, up, bias):
    n, w = second.shape
    h = up[0].shape[1]
    return run(mlp_forward_body, "mlp_forward", dp, [second, *up, bias],
        [tile(w)] + [whole(p.shape) for p in (*up, bias)],
        [shape((n, h), BF16), shape((n, h), F32)], [tile(h)] * 2,
        [pltpu.VMEM((w, h), BF16)], (n // TILE,), flops=2 * n * w * h)

def masked_scores(index, q, keys, seg_q, seg_k):
    reach = keys.shape[0]
    scores = dot(q, keys, (1, 1)) * (1.0 / math.sqrt(HEAD))
    row = index * TILE + lax.broadcasted_iota(jnp.int32, (TILE, reach), 0)
    col = lax.broadcasted_iota(jnp.int32, (TILE, reach), 1)
    allowed = (seg_q[...] == seg_k[:, 0:reach]) & (col <= row)
    return jnp.where(allowed, scores, -1e30), allowed

def each_tile(count, block):
    for index in range(count):
        @pl.when(pl.program_id(0) == index)
        def _(index=index):
            block(index, (index + 1) * TILE)

def attend_forward_body(dp, q, k, v, seg_q, seg_k, context, low, log_sum):
    def block(index, reach):
        scores, allowed = masked_scores(index, q[...], k[0:reach, :], seg_q, seg_k)
        top = jnp.max(scores, axis=1, keepdims=True)
        weights = jnp.where(allowed, jnp.exp(scores - top), 0.0)
        weight_sum = jnp.sum(weights, axis=1, keepdims=True)
        mixed = dot(weights.astype(BF16), v[0:reach, :], (1, 0)) / weight_sum
        context[...] = mixed
        low[...] = mixed.astype(BF16)
        log_sum[...] = top + jnp.log(weight_sum)
    each_tile(k.shape[0] // TILE, block)

def attend_forward(dp, q, k, v, seg_col, seg_row):
    n = q.shape[0]
    return run(attend_forward_body, "attend_forward", dp, [q, k, v, seg_col, seg_row],
        [tile(HEAD), whole(k.shape), whole(v.shape), tile(1), whole(seg_row.shape)],
        [shape((n, HEAD), F32), shape((n, HEAD), BF16), shape((n, 1), F32)],
        [tile(HEAD)] * 2 + [tile(1)], [], (n // TILE,), flops=3 * n * n * HEAD)

def output_body(dp, ctx, active, w_out, d0, dx, dy, d1, d2, out, full):
    @pl.when(pl.program_id(0) == 0)
    def _():
        fill(dp[0], full, (d0, dx, dy, d1, d2))
    out[...] = (dot(ctx[...], w_out[...], (1, 0)) + dot(active[...], full[...], (1, 0))).astype(BF16)

def output(dp, ctx, active, w_out, down):
    n, h = active.shape; w = w_out.shape[1]
    return run(output_body, "output", dp, [ctx, active, w_out, *down],
        [tile(HEAD), tile(h), whole(w_out.shape)] + [whole(p.shape) for p in down],
        [shape((n, w), BF16)], [tile(w)], [pltpu.VMEM((h, w), BF16)], (n // TILE,), flops=2 * n * w * (h + HEAD))[0]

SLAB = 512

def sections(half):
    return (
        (0, 0, 3, 0, half),
        (1, half, 3, half, half),
        (0, half, 1, 0, half),
        (1, 0, 2, half, half),
        (2, 0, 1, half, half),
        (3, 0, 2, 0, half),
        (4, 0, 0, 0, half),
        (4, half, 0, half, half),
    )

def term_shapes(rows, cols):
    counts = (rows, rows, rows // 2, rows // 2, rows)
    return [shape((count, cols), BF16) for count in counts]

class Copies:
    def __init__(self, sems):
        self.sems, self.count = sems, 0

    def start(self, source, target):
        copy = pltpu.make_async_copy(source, target, self.sems.at[self.count])
        self.count += 1
        copy.start()
        return copy

    def lay(self, dp, full, pieces):
        take, cols = full.shape[0] // 4, full.shape[1]
        cut = pieces[3].shape[0]
        copies = []
        for mask in range(3):
            at = pl.multiple_of((dp ^ mask) * take, 16)
            copies.append(
                self.start(pieces[mask].at[pl.ds(0, take), pl.ds(0, cols)], full.at[pl.ds(at, take), :])
            )
        far = (dp ^ 3) * take
        copies.append(
            self.start(pieces[3].at[:, pl.ds(0, cols)], full.at[pl.ds(pl.multiple_of(far, 16), cut), :])
        )
        copies.append(
            self.start(
                pieces[4].at[pl.ds(0, take - cut), pl.ds(0, cols)],
                full.at[pl.ds(pl.multiple_of(far + cut, 16), take - cut), :],
            )
        )
        return copies

    def slabs(self, source, target):
        return [
            self.start(source.at[pl.ds(at, SLAB), :], target.at[pl.ds(at, SLAB), :])
            for at in range(0, source.shape[0], SLAB)
        ]

    def send_terms(self, dp, staged, outs):
        rows = staged.shape[0] // 4
        sent = []
        for out, at, mask, low, count in sections(rows // 2):
            source = pl.multiple_of((dp ^ mask) * rows + low, rows // 2)
            sent.append(self.start(staged.at[pl.ds(source, count), :], outs[out].at[pl.ds(at, count), :]))
        return sent

def wait_all(copies):
    for copy in copies:
        copy.wait()

def anywhere(count):
    return [pl.BlockSpec(memory_space=pl.ANY)] * count

def middle_body(dp, *refs):
    slope, g, d0, dx, dy, d1, d2, second, context = refs[:9]
    d_hidden, sums, attn_terms = refs[9:12]
    up_outs = refs[12:17]
    s_slope, s_g, full, s_second, s_context, s_hidden, staged, s_attn, sems = refs[17:]
    me = dp[0]
    copies = Copies(sems)
    got_full = copies.lay(me, full, (d0, dx, dy, d1, d2))
    got_g, got_slope = [], []
    n = g.shape[0]
    spans = [pl.ds(at, SLAB) for at in range(0, n, SLAB)]
    for span in spans:
        got_g.append(copies.start(g.at[span, :], s_g.at[span, :]))
        got_slope.append(copies.start(slope.at[span, :], s_slope.at[span, :]))
    got_second = copies.slabs(second, s_second)
    got_context = copies.start(context, s_context)
    wait_all(got_full)
    sent = []
    total = jnp.zeros(sums.shape, F32)
    for index, span in enumerate(spans):
        got_g[index].wait()
        got_slope[index].wait()
        low = (s_slope[span, :] * dot(s_g[span, :], full[...], (1, 1))).astype(BF16)
        s_hidden[span, :] = low
        total += jnp.sum(low.astype(F32), axis=0, keepdims=True)
        sent.append(copies.start(s_hidden.at[span, :], d_hidden.at[span, :]))
    sums[...] = total
    wait_all(got_second)
    for at in range(0, staged.shape[0], 1024):
        staged[at : at + 1024, :] = dot(s_second[:, at : at + 1024], s_hidden[...], (0, 0)).astype(BF16)
    sent += copies.send_terms(me, staged, up_outs)
    got_context.wait()
    s_attn[...] = dot(s_context[...], s_g[...], (0, 0)).astype(BF16)
    sent.append(copies.start(s_attn, attn_terms))
    wait_all(sent)

def middle(dp, slope, g, down, second, context):
    n, w = second.shape
    h = slope.shape[1]
    rows = w // 4
    outs = [shape((n, h), BF16), shape((1, h), F32), shape((HEAD, w), BF16)]
    outs += term_shapes(rows, h)
    result = run(middle_body, "middle", dp, [slope, g, *down, second, context],
        anywhere(9), outs, anywhere(1) + [whole((1, h))] + anywhere(6),
        [pltpu.VMEM((n, h), F32), pltpu.VMEM((n, w), BF16), pltpu.VMEM((h, w), BF16), pltpu.VMEM((n, w), BF16),
         pltpu.VMEM((n, HEAD), BF16), pltpu.VMEM((n, h), BF16),
         pltpu.VMEM((w, h), BF16), pltpu.VMEM((HEAD, w), BF16), pltpu.SemaphoreType.DMA((40,))],
        (1,), flops=4 * n * w * h)
    return result[0], result[1], result[2], result[3:]

def last_body(dp, *refs):
    q, k, v, wide, log_sum, seg_q, seg_k, cos, s1, s2, vec = refs[:11]
    g, w_out, first, x, hidden = refs[11:16]
    w_pieces, u_pieces = refs[16:21], refs[21:26]
    sums_joined, sums_norm, u_terms = refs[26:29]
    qkv_outs = refs[29:34]
    (s_g, s_w_out, s_first, s_x, s_hidden, full_qkv, full_up,
     s_dj, dk_acc, dv_acc, staged, s_u, sems) = refs[34:]
    me = dp[0]
    copies = Copies(sems)
    got_w_out = copies.start(w_out, s_w_out)
    n = q.shape[0]
    got_g = copies.slabs(g, s_g)
    got_first = copies.slabs(first, s_first)
    got_full = copies.lay(me, full_qkv, w_pieces) + copies.lay(me, full_up, u_pieces)
    got_x = copies.slabs(x, s_x)
    got_hidden = copies.slabs(hidden, s_hidden)
    scale = 1.0 / math.sqrt(HEAD)
    dk_acc[...] = jnp.zeros_like(dk_acc)
    dv_acc[...] = jnp.zeros_like(dv_acc)
    got_w_out.wait()
    total_q = jnp.zeros((1, HEAD), F32)
    for index in range(n // TILE):
        span = pl.ds(index * TILE, TILE)
        reach = (index + 1) * TILE
        if index * TILE % SLAB == 0:
            got_g[index * TILE // SLAB].wait()
        d_ctx = dot(s_g[span, :], s_w_out[...], (1, 1)).astype(BF16)
        keys, values, queries = k[0:reach, :], v[0:reach, :], q[span, :]
        scores, allowed = masked_scores(index, queries, keys, seg_q.at[span, :], seg_k)
        probs = jnp.where(allowed, jnp.exp(scores - log_sum[span, :]), 0.0)
        delta = jnp.sum(d_ctx.astype(F32) * wide[span, :], axis=1, keepdims=True)
        d_scores = (probs * (dot(d_ctx, values, (1, 1)) - delta)).astype(BF16)
        d_q = dot(d_scores, keys, (1, 0)) * scale
        low_q = turn(d_q, cos[span, :], -s1[span, :], -s2[span, :]).astype(BF16)
        s_dj[span, 0:HEAD] = low_q
        total_q += jnp.sum(low_q.astype(F32), axis=0, keepdims=True)
        dk_acc[0:reach, :] += dot(d_scores, queries, (0, 0))
        dv_acc[0:reach, :] += dot(probs.astype(BF16), d_ctx, (0, 0))
    low_k = turn(dk_acc[...] * scale, cos[...], -s1[...], -s2[...]).astype(BF16)
    low_v = dv_acc[...].astype(BF16)
    s_dj[:, HEAD : 2 * HEAD] = low_k
    s_dj[:, 2 * HEAD :] = low_v
    sums_joined[:, 0:HEAD] = total_q
    sums_joined[:, HEAD : 2 * HEAD] = jnp.sum(low_k.astype(F32), axis=0, keepdims=True)
    sums_joined[:, 2 * HEAD :] = jnp.sum(low_v.astype(F32), axis=0, keepdims=True)
    wait_all(got_first)
    for at in range(0, staged.shape[0], 1024):
        staged[at : at + 1024, :] = dot(s_first[:, at : at + 1024], s_dj[...], (0, 0)).astype(BF16)
    sent = copies.send_terms(me, staged, qkv_outs)
    wait_all(got_full)
    sums_norm[...] = jnp.zeros_like(sums_norm)
    for index in range(n // TILE):
        span = pl.ds(index * TILE, TILE)
        if index * TILE % SLAB == 0:
            got_x[index * TILE // SLAB].wait()
            got_hidden[index * TILE // SLAB].wait()
        d_first = dot(s_dj[span, :], full_qkv[...], (1, 1))
        d_second = dot(s_hidden[span, :], full_up[...], (1, 1))
        s_u[span, :] = (d_first * vec[0:1, :] + d_second * vec[2:3, :]).astype(BF16)
        sent.append(copies.start(s_u.at[span, :], u_terms.at[span, :]))
        normed, _ = norm_tile(s_x[span, :])
        sums_norm[0:1, :] += jnp.sum(d_first * normed, axis=0, keepdims=True)
        sums_norm[1:2, :] += jnp.sum(d_first, axis=0, keepdims=True)
        sums_norm[2:3, :] += jnp.sum(d_second * normed, axis=0, keepdims=True)
        sums_norm[3:4, :] += jnp.sum(d_second, axis=0, keepdims=True)
    wait_all(sent)

def last(dp, q, k, v, wide, log_sum, seg_col, seg_row, tables, vec, g, w_out, first, x, hidden, w_in, up):
    n, w = x.shape
    h = hidden.shape[1]
    rows = w // 4
    near = [q, k, v, wide, log_sum, seg_col, seg_row, *tables, vec]
    outs = [shape((1, 3 * HEAD), F32), shape((4, w), F32), shape((n, w), BF16)]
    outs += term_shapes(rows, 3 * HEAD)
    result = run(last_body, "last", dp, [*near, g, w_out, first, x, hidden, *w_in, *up],
        [whole(a.shape) for a in near] + anywhere(15), outs,
        [whole((1, 3 * HEAD)), whole((4, w))] + anywhere(6),
        [pltpu.VMEM((n, w), BF16), pltpu.VMEM((HEAD, w), BF16), pltpu.VMEM((n, w), BF16),
         pltpu.VMEM((n, w), BF16), pltpu.VMEM((n, h), BF16), pltpu.VMEM((w, 3 * HEAD), BF16), pltpu.VMEM((w, h), BF16),
         pltpu.VMEM((n, 3 * HEAD), BF16), pltpu.VMEM((n, HEAD), F32), pltpu.VMEM((n, HEAD), F32),
         pltpu.VMEM((w, 3 * HEAD), BF16), pltpu.VMEM((n, w), BF16),
         pltpu.SemaphoreType.DMA((48,))],
        (1,), flops=2 * n * w * (4 * HEAD + 3 * HEAD + h) + 6 * n * n * HEAD)
    return result[0], result[1], result[2], result[3:]

def outward_body(dp, *refs):
    left, right, attn = refs[:3]
    outs = refs[3:8]
    s_left, s_right, s_attn, staged, sems = refs[8:]
    me = dp[0]
    copies = Copies(sems)
    got_right = copies.slabs(right, s_right)
    got_left = copies.start(left, s_left)
    got_attn = copies.start(attn, s_attn)
    rows, extra = staged.shape[0] // 4, attn.shape[1]
    half, part = rows // 2, extra // 2
    one = half + part
    wait_all(got_right)
    got_left.wait()
    staged[...] = dot(s_left[...], s_right[...], (0, 0)).astype(BF16)
    got_attn.wait()
    sent = []
    for out, at, mask, low, _ in sections(half):
        source = pl.multiple_of((me ^ mask) * rows + low, half)
        at = one if at else 0
        target = outs[out]
        sent.append(copies.start(staged.at[pl.ds(source, half), :], target.at[pl.ds(at, half), :]))
        source = part if low else 0
        sent.append(
            copies.start(
                s_attn.at[me ^ mask, pl.ds(source, part), :], target.at[pl.ds(at + half, part), :]
            )
        )
    wait_all(sent)

def outward(dp, left, right, attn):
    n, h = left.shape; w = right.shape[1]
    outs = term_shapes(h // 4 + attn.shape[1], w)
    return run(outward_body, "outward", dp, [left, right, attn], anywhere(3), outs, anywhere(5),
        [pltpu.VMEM((n, h), BF16), pltpu.VMEM((n, w), BF16), pltpu.VMEM(attn.shape, BF16),
         pltpu.VMEM((h, w), BF16), pltpu.SemaphoreType.DMA((24,))],
        (1,), flops=2 * n * h * w)


def up_blocks_body(source, out):
    for rank in range(HEADS):
        for group in range(4):
            at = (group * HEADS + rank) * 256
            out[rank, :, group * 256 : group * 256 + 256] = source[:, at : at + 256]


def qkv_blocks_body(source, packed, out):
    for rank in range(HEADS):
        for part in range(3):
            at = (part * HEADS + HEAD_ORDER[rank]) * HEAD
            out[rank, :, part * HEAD : part * HEAD + HEAD] = source[:, at : at + HEAD]
        out[rank, :, 3 * HEAD :] = packed[...]


def out_rows_body(dp, own, along_x, along_y, far, out):
    for mask, piece in enumerate((own, along_x, along_y)):
        out[dp[0] ^ mask] = piece[256:, :]
    out[dp[0] ^ 3] = far[128:, :]


def up_rows_body(source, out):
    for rank in range(HEADS):
        for group in range(4):
            at = (group * HEADS + rank) * 256
            out[:, at : at + 256] = source[rank, :, group * 256 : group * 256 + 256].astype(F32)


def qkv_rows_body(source, out):
    for rank in range(HEADS):
        for part in range(3):
            at = (part * HEADS + HEAD_ORDER[rank]) * HEAD
            out[:, at : at + HEAD] = source[rank, :, part * HEAD : part * HEAD + HEAD].astype(F32)


def repack(body, name, out, *sources):
    return pl.pallas_call(
        body,
        name=name,
        out_shape=out,
        compiler_params=pltpu.CompilerParams(vmem_limit_bytes=16 * 2**20),
        cost_estimate=pl.CostEstimate(
            flops=0,
            bytes_accessed=sources[0].size * 6,
            transcendentals=0,
        ),
    )(*sources)


def tie(value, *others):
    return lax.optimization_barrier((value, others))[0]


def stage(values, done):
    return lax.optimization_barrier((tuple(values), tuple(done)))[0]


def over_x(block):
    return lax.ppermute(block, "dp", swap(4, 1))


def over_y(block):
    return lax.ppermute(block, "dp", swap(4, 2))


def small_call(body, name, outs, *sources):
    return pl.pallas_call(
        body,
        name=name,
        out_shape=outs,
        compiler_params=pltpu.CompilerParams(vmem_limit_bytes=56 * 2**20),
        cost_estimate=pl.CostEstimate(flops=0, bytes_accessed=sources[0].size * 8, transcendentals=0),
    )(*sources)


def send_both(terms):
    return over_x(terms[0]), over_y(terms[1])


def pass_on_body(x_low, y_top, got_x, got_y, to_x, to_y):
    half = x_low.shape[0]
    to_y[...] = (y_top[...].astype(F32) + got_x[:half].astype(F32)).astype(BF16)
    to_x[...] = (x_low[...].astype(F32) + got_y[half:].astype(F32)).astype(BF16)


def pass_on(terms, got):
    out = jax.ShapeDtypeStruct(terms[2].shape, BF16)
    to_x, to_y = small_call(pass_on_body, "pass_on", (out, out), terms[2], terms[3], *got)
    return over_x(to_x), over_y(to_y)


def reduce_last_body(own, got_x, got_y, x_low, y_top, out):
    half = x_low.shape[0]
    top = got_x[half:].astype(F32) + y_top[...].astype(F32)
    low = got_y[:half].astype(F32) + x_low[...].astype(F32)
    out[:half] = (own[:half].astype(F32) + top).astype(out.dtype)
    out[half:] = (own[half:].astype(F32) + low).astype(out.dtype)


def reduce_last(terms, got, then):
    out = jax.ShapeDtypeStruct(terms[4].shape, BF16)
    return small_call(reduce_last_body, "reduce_last", out, terms[4], *got, *then)


def reduce_both_body(own, got_x, got_y, x_low, y_top, first, second):
    one = x_low.shape[0]
    half, part = first.shape[0] // 2, second.shape[0] // 2
    top = got_x[one:].astype(F32) + y_top[...].astype(F32)
    low = got_y[:one].astype(F32) + x_low[...].astype(F32)
    for index, others in enumerate((top, low)):
        total = own[index * one : (index + 1) * one].astype(F32) + others
        first[index * half : (index + 1) * half] = total[:half]
        second[index * part : (index + 1) * part] = total[half:]


def reduce_both(terms, got, then, rows, part):
    outs = [jax.ShapeDtypeStruct((count, terms[4].shape[1]), F32) for count in (rows, part)]
    return small_call(reduce_both_body, "reduce_both", outs, terms[4], *got, *then)


def rotary_lanes(length):
    position = jnp.arange(length, dtype=jnp.int32).astype(F32)
    cosine, sine = rotary_tables(position)
    blank = jnp.zeros((length, 32), F32)
    rest = jnp.zeros((length, 64), F32)
    cos = jnp.concatenate([cosine, jnp.ones((length, 64), F32)], axis=1)
    first = jnp.concatenate([-sine[:, :32], blank, rest], axis=1)
    second = jnp.concatenate([blank, sine[:, 32:], rest], axis=1)
    return cos, first, second


def line_shards(
    block_input,
    segments,
    out_grad,
    ln1_gain,
    ln1_bias,
    w_qkv,
    b_qkv,
    w_attn_out,
    b_attn_out,
    ln2_gain,
    ln2_bias,
    w_up,
    b_up,
    w_down,
    b_down,
):
    dp, sp = lax.axis_index("dp"), lax.axis_index("sp")
    dp = dp.astype(jnp.int32)
    x_own = block_input[0]
    g_own = out_grad[0]
    tokens, width = x_own.shape
    length = tokens * HEADS
    rows = w_qkv.shape[0]
    everywhere = ("dp", "sp")
    head = head_of(sp)

    fours = [[0, 1, 2, 3], [4, 5, 6, 7]]
    x_all = lax.all_gather(x_own, "sp", axis=0, tiled=True)
    down_own = jnp.concatenate([w_down, w_attn_out], axis=0)
    down_x, down_y = over_x(down_own), over_y(down_own)
    packed = jnp.concatenate(
        [
            jnp.stack([ln1_gain, ln1_bias, ln2_gain, ln2_bias, b_attn_out, b_down]),
            b_qkv.reshape(3, 64),
            b_up.reshape(4, 64),
            segments[0].astype(BF16).reshape(2, 64),
        ]
    )
    packed = jnp.pad(packed, ((0, rows - 15), (0, 64)))
    qkv_blocks = repack(
        qkv_blocks_body, "qkv_blocks", jax.ShapeDtypeStruct((HEADS, rows, 896), BF16), w_qkv, packed
    )
    up_blocks = repack(
        up_blocks_body, "up_blocks", jax.ShapeDtypeStruct((HEADS, rows, 1024), BF16), w_up
    )
    cos, sin_one, sin_two = rotary_lanes(length)
    qkv_rows = lax.all_to_all(qkv_blocks, "sp", 0, 0, tiled=True).reshape(HEADS * rows, 896)

    cut = w_down.shape[0] // 2
    half = HEADS * rows // 2
    down_far = over_x(down_y[:cut]), over_y(down_x[cut:])
    sum_out = jnp.sum(g_own.astype(F32), axis=0)
    up_blocks, qkv_rows, down_far, cos, sin_one, sin_two, sum_out = stage(
        (up_blocks, qkv_rows, down_far, cos, sin_one, sin_two, sum_out), ()
    )
    tables = (cos, sin_one, sin_two)
    down = (down_own, down_x, down_y, *down_far)
    up_rows = lax.all_to_all(up_blocks, "sp", 0, 0, tiled=True).reshape(HEADS * rows, 1024)
    qkv_x, qkv_y = over_x(qkv_rows), over_y(qkv_rows)
    out_rows = run(
        out_rows_body, "out_rows", dp, [*down[:3], down[4]], [whole(d.shape) for d in (*down[:3], down[4])],
        shape((4, rows, width), BF16), whole((4, rows, width)), [], (1,),
    )

    qkv_x, qkv_y, out_rows = stage((qkv_x, qkv_y, out_rows), ())
    qkv_far = over_x(qkv_y[:half]), over_y(qkv_x[half:])

    up_rows, qkv_far, g_late, out_rows = stage((up_rows, qkv_far, g_own, out_rows), ())
    w_in = (qkv_rows, qkv_x, qkv_y, *qkv_far)
    g_all = lax.all_gather(g_late, "sp", axis=0, tiled=True)
    up_x, up_y = over_x(up_rows), over_y(up_rows)
    w_out = lax.all_to_all(
        out_rows, "sp", 0, 0, tiled=True, axis_index_groups=fours
    ).reshape(HEAD, width)

    small = jnp.zeros((4, HEADS, 15, 64), BF16)
    far = jnp.concatenate([piece[:, 768:832] for piece in qkv_far], axis=0)
    for mask, piece in enumerate([piece[:, 768:832] for piece in w_in[:3]] + [far]):
        small = put(small, piece.reshape(HEADS, rows, 64)[:, :15], dp ^ mask)
    small = small.reshape(32, 15, 64)
    vectors = small[:, :6].transpose(1, 0, 2).reshape(6, width).astype(F32)
    norm_vec = vectors[:4]
    bias_qkv = pick(small[:, 6:9].reshape(3, HEADS, HEAD), head, 1).astype(F32).reshape(1, 768)
    bias_up = pick(small[:, 9:13].reshape(4, HEADS, 256), sp, 1).astype(F32).reshape(1, 1024)
    seg = pick(small[:, 13:].reshape(4, length), dp).astype(F32)
    seg_col, seg_row = seg.reshape(length, 1), seg.reshape(1, length)
    first_in, second_in = norms(dp, x_all, norm_vec)
    queries, key_rows, value_rows = qkv(dp, first_in, w_in, bias_qkv, tables)

    up_x, up_y, queries = stage((up_x, up_y, queries), (bias_up, seg_col, seg_row))
    up = (up_rows, up_x, up_y, over_x(up_y[:half]), over_y(up_x[half:]))

    wide_context, context, log_sum = attend_forward(
        dp, queries, key_rows, value_rows, seg_col, seg_row
    )
    up, context = stage((up, context), ())
    active, slope = mlp_forward(dp, second_in, up, bias_up)

    out_terms = output(dp, context, active, w_out, down)
    out_sum = lax.psum_scatter(out_terms, "sp", scatter_dimension=0, tiled=True)
    d_hidden, up_sums, attn_terms, up_terms = middle(
        dp, slope, tie(g_all, out_terms), down, second_in, context
    )
    attn_sent = lax.all_to_all(
        attn_terms.reshape(4, HEAD // 4, width), "sp", 0, 0, tiled=True, axis_index_groups=fours
    )
    up_got = send_both(up_terms)
    sum_up = lax.dynamic_update_slice(
        jnp.zeros((4, HEADS, 256), F32), up_sums.reshape(4, 1, 256), (0, sp, 0)
    )
    qkv_sums, norm_sums, u_terms, qkv_terms = last(
        dp,
        tie(queries, attn_terms),
        key_rows,
        value_rows,
        wide_context,
        log_sum,
        seg_col,
        seg_row,
        tables,
        norm_vec,
        g_all,
        w_out,
        first_in,
        x_all,
        d_hidden,
        w_in,
        up,
    )
    u_terms, up_got, qkv_terms, down_left, norm_sums, attn_sent = stage(
        (u_terms, up_got, qkv_terms, active, norm_sums, attn_sent), ()
    )
    up_then = pass_on(up_terms, up_got)
    qkv_got = send_both(qkv_terms)
    u_sum = lax.psum_scatter(u_terms, "sp", scatter_dimension=0, tiled=True)
    sum_qkv = lax.dynamic_update_slice(
        jnp.zeros((3, HEADS, HEAD), F32), qkv_sums.reshape(3, 1, HEAD), (0, head, 0)
    )
    totals = jnp.concatenate(
        [
            norm_sums.reshape(4, 32, 64).transpose(1, 0, 2).reshape(32, 256),
            sum_out.reshape(32, 64),
            sum_qkv.reshape(32, 192),
            sum_up.reshape(32, 256),
        ],
        axis=1,
    )
    down_terms = outward(dp, down_left, g_all, attn_sent)

    up_then, qkv_got, down_terms, totals = stage((up_then, qkv_got, down_terms, totals), ())
    qkv_then = pass_on(qkv_terms, qkv_got)
    down_got = send_both(down_terms)
    up_sum = reduce_last(up_terms, up_got, up_then)
    up_back = lax.all_to_all(up_sum.reshape(HEADS, rows, 1024), "sp", 0, 0, tiled=True)
    qkv_sum = reduce_last(qkv_terms, qkv_got, qkv_then)
    qkv_sum, out_sum = stage((qkv_sum, out_sum), (up_back,))
    qkv_back = lax.all_to_all(qkv_sum.reshape(HEADS, rows, 768), "sp", 0, 0, tiled=True)

    down_got = stage(down_got, (qkv_sum,))
    down_then = pass_on(down_terms, down_got)
    grad_up = repack(
        up_rows_body, "up_rows", jax.ShapeDtypeStruct((rows, HEADS * 1024), F32), up_back
    )
    owned = lax.all_to_all(tie(totals, qkv_back), everywhere, 0, 0, tiled=True)
    down_then = stage(down_then, (owned, grad_up))
    grad_down, grad_out = reduce_both(
        down_terms, down_got, down_then, w_down.shape[0], w_attn_out.shape[0]
    )
    grad_qkv = repack(
        qkv_rows_body, "qkv_rows", jax.ShapeDtypeStruct((rows, HEADS * 768), F32), qkv_back
    )
    owned = jnp.sum(owned, axis=0)

    x_wide = x_own.astype(F32)
    block_output = (x_wide + out_sum.astype(F32) + (vectors[4] + vectors[5]))[None]
    u_wide = u_sum.astype(F32)
    normed, scale = normalize(x_wide)
    u_mean = jnp.mean(u_wide, axis=-1, keepdims=True)
    u_along = jnp.mean(u_wide * normed, axis=-1, keepdims=True)
    input_grad = (g_own.astype(F32) + (u_wide - u_mean - normed * u_along) * scale)[None]

    grad_g1, grad_s1, grad_g2, grad_s2, grad_bout = (
        owned[k * rows : (k + 1) * rows] for k in range(5)
    )
    return (
        block_output,
        input_grad,
        grad_g1,
        grad_s1,
        grad_qkv,
        owned[320:512],
        grad_out,
        grad_bout,
        grad_g2,
        grad_s2,
        grad_up,
        owned[512:],
        grad_down,
        grad_bout,
    )


def shards(*arrays):
    if (lax.axis_size("dp"), lax.axis_size("sp")) == (4, 8):
        return line_shards(*arrays)
    return any_shards(*arrays)


def solution(mesh):
    tokens = P("dp", "sp", None)
    split = P(("dp", "sp"))
    matrix = P(("dp", "sp"), None)
    return jax.shard_map(
        shards,
        mesh=mesh,
        in_specs=(
            tokens,
            P("dp", "sp"),
            tokens,
            split,
            split,
            matrix,
            split,
            matrix,
            split,
            split,
            split,
            matrix,
            split,
            matrix,
            split,
        ),
        out_specs=(
            tokens,
            tokens,
            split,
            split,
            matrix,
            split,
            matrix,
            split,
            split,
            split,
            matrix,
            split,
            matrix,
            split,
        ),
        check_vma=False,
    )
```

```python
import functools
import math

import jax
import jax.numpy as jnp
from jax import lax
from jax.experimental import pallas as pl
from jax.experimental.pallas import tpu as pltpu
from jax.sharding import PartitionSpec as P

HEADS = 8
HEAD = 256
ROT = 64
TILE = 256
BF16 = jnp.bfloat16
F32 = jnp.float32

def normalize(values):
    center = values - jnp.mean(values, axis=-1, keepdims=True)
    spread = jnp.mean(center * center, axis=-1, keepdims=True)
    scale = lax.rsqrt(spread + 1e-05)
    return center * scale, scale


def rotary_tables(positions):
    inverse_freq = 10000.0 ** (-jnp.arange(0, ROT, 2).astype(F32) / ROT)
    angles = positions[:, None] * inverse_freq[None, :]
    angles = jnp.concatenate([angles, angles], axis=1)
    return (jnp.cos(angles), jnp.sin(angles))


def rotate(values, cosine, sine):
    half_rot = ROT // 2
    rot_part = values[..., :ROT]
    turned = jnp.concatenate([-rot_part[..., half_rot:], rot_part[..., :half_rot]], axis=-1)
    rotated = rot_part * cosine + turned * sine
    return jnp.concatenate([rotated, values[..., ROT:]], axis=-1)


def pick(array, index, axis=0):
    return lax.dynamic_index_in_dim(array, index, axis, keepdims=False)


def put(array, piece, index):
    return lax.dynamic_update_slice_in_dim(array, piece[None], index, 0)


def swap(extent, mask):
    return [(i, i ^ mask) for i in range(extent)]


class AnyGrid:
    def __init__(self):
        self.dp = lax.axis_index("dp")
        self.sp = lax.axis_index("sp")
        self.dps = lax.axis_size("dp")
        self.sps = lax.axis_size("sp")
        self.parts = self.sps // HEADS
        self.part = self.sp // HEADS
        self.team = [
            [part * HEADS + rank for rank in range(HEADS)] for part in range(self.parts)
        ]
        self.peers = [
            [part * HEADS + rank for part in range(self.parts)] for rank in range(HEADS)
        ]

    def gather_dp(self, block):
        block = lax.all_gather(block, "sp", axis=0, axis_index_groups=self.peers)
        block = lax.all_gather(block, "dp", axis=0)
        return block.reshape((self.dps * self.parts,) + block.shape[2:])

    def reduce_dp(self, terms):
        block = terms.reshape((self.dps, self.parts) + terms.shape[1:])
        block = lax.psum_scatter(block, "dp", scatter_dimension=0)
        return lax.psum_scatter(
            block, "sp", scatter_dimension=0, axis_index_groups=self.peers
        ).astype(F32)

    def gather_sp(self, block):
        return lax.all_gather(block, "sp", axis=0, tiled=True, axis_index_groups=self.team)

    def reduce_sp(self, terms):
        return lax.psum_scatter(
            terms, "sp", scatter_dimension=0, tiled=True, axis_index_groups=self.team
        ).astype(F32)

    def exchange_sp(self, blocks):
        return lax.all_to_all(
            blocks, "sp", split_axis=0, concat_axis=0, tiled=True, axis_index_groups=self.team
        )

    def gather_small(self, vector):
        return lax.all_gather(vector, ("dp", "sp"), axis=0)

    def reduce_small(self, terms):
        return lax.psum_scatter(terms, ("dp", "sp"), scatter_dimension=0)

    def gather_out(self, block):
        whole = lax.all_gather(block, ("dp", "sp"), axis=0, tiled=True)
        return lax.dynamic_slice_in_dim(whole, head_of(self.sp % HEADS) * HEAD, HEAD, 0)

    def reduce_out(self, terms):
        whole = jnp.zeros((HEADS * HEAD, terms.shape[1]), terms.dtype)
        whole = lax.dynamic_update_slice_in_dim(whole, terms, head_of(self.sp % HEADS) * HEAD, 0)
        return lax.psum_scatter(
            whole, ("dp", "sp"), scatter_dimension=0, tiled=True
        ).astype(F32)

    def whole_keys(self, block):
        return lax.all_gather(block, "sp", axis=0, tiled=True, axis_index_groups=self.peers)

    def reduce_keys(self, terms):
        return lax.psum_scatter(
            terms, "sp", scatter_dimension=0, tiled=True, axis_index_groups=self.peers
        )


def head_of(rank):
    return 2 * (rank % 4) + rank // 4


HEAD_ORDER = [2 * (rank % 4) + rank // 4 for rank in range(HEADS)]
RANK_ORDER = [HEAD_ORDER.index(head) for head in range(HEADS)]


def dot(left, right, contract):
    return lax.dot_general(
        left, right, (((contract[0],), (contract[1],)), ((), ())), preferred_element_type=F32
    )


def any_shards(
    block_input,
    segments,
    out_grad,
    ln1_gain,
    ln1_bias,
    w_qkv,
    b_qkv,
    w_attn_out,
    b_attn_out,
    ln2_gain,
    ln2_bias,
    w_up,
    b_up,
    w_down,
    b_down,
):
    dps, sps = lax.axis_size("dp"), lax.axis_size("sp")
    devices = dps * sps
    grid = AnyGrid()
    groups = devices // HEADS
    x_own = block_input[0]
    g_own = out_grad[0]
    tokens, width = x_own.shape
    rows = w_qkv.shape[0]
    cols_up = b_up.shape[0]
    cols_qkv = b_qkv.shape[0]
    length = tokens * HEADS
    scale = 1.0 / math.sqrt(HEAD)

    packed = jnp.concatenate(
        [
            ln1_gain,
            ln1_bias,
            ln2_gain,
            ln2_bias,
            b_attn_out,
            b_down,
            b_qkv,
            b_up,
            segments[0].astype(BF16),
        ]
    )
    small = grid.gather_small(packed)
    vectors = [
        small[:, k * rows : (k + 1) * rows].reshape(width).astype(F32) for k in range(6)
    ]
    gain_one, shift_one, gain_two, shift_two, bias_out, bias_down = vectors
    at = 6 * rows
    rank = grid.sp % HEADS
    bias_qkv = small[:, at : at + cols_qkv].reshape(3, HEADS, HEAD)
    bias_qkv = pick(bias_qkv, head_of(rank), 1).astype(F32).reshape(3 * HEAD)
    at += cols_qkv
    bias_up = small[:, at : at + cols_up].reshape(groups, HEADS, cols_up)
    bias_up = pick(bias_up, rank, 1).astype(F32).reshape(groups * cols_up)
    at += cols_up
    seg_all = pick(small[:, at:].reshape(dps, sps * tokens), grid.dp)
    seg_mine = lax.dynamic_slice_in_dim(seg_all, grid.part * length, length, 0)

    x_all = grid.gather_sp(x_own)
    up_blocks = w_up.reshape(rows, groups, HEADS, cols_up).transpose(2, 0, 1, 3)
    up_blocks = up_blocks.reshape(HEADS, rows, groups * cols_up)
    up_rows = grid.exchange_sp(up_blocks).reshape(HEADS * rows, groups * cols_up)
    weight_down = grid.gather_dp(w_down).reshape(groups * cols_up, width)
    weight_up = grid.gather_dp(up_rows).reshape(width, groups * cols_up)
    qkv_blocks = w_qkv.reshape(rows, 3, HEADS, HEAD)
    qkv_blocks = jnp.stack([qkv_blocks[:, :, head] for head in HEAD_ORDER])
    qkv_blocks = qkv_blocks.reshape(HEADS, rows, 3 * HEAD)
    qkv_rows = grid.exchange_sp(qkv_blocks).reshape(HEADS * rows, 3 * HEAD)
    weight_qkv = grid.gather_dp(qkv_rows).reshape(width, 3 * HEAD)
    weight_out = grid.gather_out(w_attn_out)
    g_all = grid.gather_sp(g_own)

    normed, _ = normalize(x_all.astype(F32))
    first_in = (normed * gain_one + shift_one).astype(BF16)
    second_in = (normed * gain_two + shift_two).astype(BF16)

    hidden = dot(second_in, weight_up, (1, 0)) + bias_up
    active_wide, gelu_pull = jax.vjp(lambda v: jax.nn.gelu(v, approximate=False), hidden)
    active = active_wide.astype(BF16)
    d_active = dot(g_all, weight_down, (1, 1))
    d_hidden = gelu_pull(d_active)[0].astype(BF16)
    term_down = dot(active, g_all, (0, 0)).astype(BF16)
    term_up = dot(second_in, d_hidden, (0, 0)).astype(BF16)

    joined = dot(first_in, weight_qkv, (1, 0)) + bias_qkv
    position = grid.part * length + jnp.arange(length, dtype=jnp.int32)
    cosine, sine = rotary_tables(position.astype(F32))
    queries = rotate(joined[:, :HEAD], cosine, sine).astype(BF16)
    key_rows = grid.whole_keys(rotate(joined[:, HEAD : 2 * HEAD], cosine, sine).astype(BF16))
    value_rows = grid.whole_keys(joined[:, 2 * HEAD :].astype(BF16))
    key_position = jnp.arange(key_rows.shape[0], dtype=jnp.int32)
    allowed = (seg_mine[:, None] == seg_all[None, :]) & (
        key_position[None, :] <= position[:, None]
    )
    scores = jnp.where(allowed, dot(queries, key_rows, (1, 1)) * scale, -1e30)
    top = jnp.max(scores, axis=-1, keepdims=True)
    weights = jnp.where(allowed, jnp.exp(scores - top), 0.0)
    weight_sum = jnp.sum(weights, axis=-1, keepdims=True)
    log_sum = top + jnp.log(weight_sum)
    context = dot(weights.astype(BF16), value_rows, (1, 0)) / weight_sum
    context_low = context.astype(BF16)

    out_terms = dot(context_low, weight_out, (1, 0)) + dot(active, weight_down, (1, 0))
    out_sum = grid.reduce_sp(out_terms.astype(BF16))
    block_output = (x_own.astype(F32) + out_sum + (bias_out + bias_down))[None]

    d_context = dot(g_all, weight_out, (1, 1)).astype(BF16)
    row_delta = jnp.sum(d_context.astype(F32) * context, axis=-1, keepdims=True)
    probs = jnp.where(allowed, jnp.exp(scores - log_sum), 0.0)
    d_probs = dot(d_context, value_rows, (1, 1))
    d_scores = (probs * (d_probs - row_delta)).astype(BF16)
    d_queries = dot(d_scores, key_rows, (1, 0)) * scale
    d_keys = grid.reduce_keys(dot(d_scores, queries, (0, 0)) * scale)
    d_values = grid.reduce_keys(dot(probs.astype(BF16), d_context, (0, 0)))
    d_joined = jnp.concatenate(
        [rotate(d_queries, cosine, -sine), rotate(d_keys, cosine, -sine), d_values], axis=1
    ).astype(BF16)

    d_first = dot(d_joined, weight_qkv, (1, 1))
    d_second = dot(d_hidden, weight_up, (1, 1))
    u_terms = d_first * gain_one + d_second * gain_two
    u_sum = grid.reduce_sp(u_terms.astype(BF16))
    normed_own, scale_own = normalize(x_own.astype(F32))
    u_mean = jnp.mean(u_sum, axis=-1, keepdims=True)
    u_along = jnp.mean(u_sum * normed_own, axis=-1, keepdims=True)
    input_grad = (g_own.astype(F32) + (u_sum - u_mean - normed_own * u_along) * scale_own)[None]

    term_qkv = dot(first_in, d_joined, (0, 0)).astype(BF16)
    term_out = dot(context_low, g_all, (0, 0)).astype(BF16)
    grad_down = grid.reduce_dp(term_down.reshape(groups, cols_up, width))
    up_sum = grid.reduce_dp(term_up.reshape(groups, HEADS * rows, groups * cols_up))
    up_back = grid.exchange_sp(up_sum.astype(BF16).reshape(HEADS, rows, groups * cols_up))
    grad_up = (
        up_back.astype(F32)
        .reshape(HEADS, rows, groups, cols_up)
        .transpose(1, 2, 0, 3)
        .reshape(rows, devices * cols_up)
    )
    grad_out = grid.reduce_out(term_out)
    qkv_sum = grid.reduce_dp(term_qkv.reshape(groups, HEADS * rows, 3 * HEAD))
    qkv_back = grid.exchange_sp(qkv_sum.astype(BF16).reshape(HEADS, rows, 3, HEAD)).astype(F32)
    grad_qkv = jnp.stack([qkv_back[place] for place in RANK_ORDER], axis=2)
    grad_qkv = grad_qkv.reshape(rows, 3 * HEADS * HEAD)

    sum_qkv = jnp.zeros((3, HEADS, HEAD), F32)
    sum_qkv = lax.dynamic_update_slice(
        sum_qkv,
        jnp.sum(d_joined.astype(F32), axis=0).reshape(3, 1, HEAD),
        (0, head_of(rank), 0),
    )
    sum_up = jnp.zeros((groups, HEADS, cols_up), F32)
    sum_up = lax.dynamic_update_slice(
        sum_up,
        jnp.sum(d_hidden.astype(F32), axis=0).reshape(groups, 1, cols_up),
        (0, rank, 0),
    )
    totals = [
        jnp.sum(d_first * normed, axis=0),
        jnp.sum(d_first, axis=0),
        jnp.sum(d_second * normed, axis=0),
        jnp.sum(d_second, axis=0),
        jnp.sum(g_own.astype(F32), axis=0),
        sum_qkv,
        sum_up,
    ]
    totals = jnp.concatenate([total.reshape(devices, -1) for total in totals], axis=1)
    owned = grid.reduce_small(totals)
    parts = [owned[k * rows : (k + 1) * rows] for k in range(5)]
    grad_g1, grad_s1, grad_g2, grad_s2, grad_bout = parts
    grad_bqkv = owned[5 * rows : 5 * rows + cols_qkv]
    grad_bup = owned[5 * rows + cols_qkv :]
    return (
        block_output,
        input_grad,
        grad_g1,
        grad_s1,
        grad_qkv,
        grad_bqkv,
        grad_out,
        grad_bout,
        grad_g2,
        grad_s2,
        grad_up,
        grad_bup,
        grad_down,
        grad_bout,
    )


def fill(dp, full, pieces):
    own, along_x, along_y, far_one, far_two = pieces
    take, cols = full.shape[0] // 4, full.shape[1]
    cut = far_one.shape[0]
    for mask, piece in enumerate((own, along_x, along_y)):
        full[pl.ds(pl.multiple_of((dp ^ mask) * take, 16), take), :] = piece[0:take, 0:cols]
    far = (dp ^ 3) * take
    full[pl.ds(pl.multiple_of(far, 16), cut), :] = far_one[:, 0:cols]
    full[pl.ds(pl.multiple_of(far + cut, 16), take - cut), :] = far_two[0 : take - cut, 0:cols]


def whole(shape):
    return pl.BlockSpec(shape, lambda *_: (0,) * len(shape), pipeline_mode=pl.Buffered(1))

def tile(cols):
    return pl.BlockSpec((TILE, cols), lambda i, *_: (i, 0))

def run(body, name, dp, inputs, specs, outs, out_specs, scratch, grid, flops=0, vmem=56):
    bytes_accessed = sum(math.prod(a.shape) * a.dtype.itemsize for a in [*inputs, *jax.tree.leaves(outs)])
    return pl.pallas_call(
        body, name=name,
        grid_spec=pltpu.PrefetchScalarGridSpec(num_scalar_prefetch=1, grid=grid, in_specs=specs, out_specs=out_specs, scratch_shapes=scratch),
        out_shape=outs,
        compiler_params=pltpu.CompilerParams(vmem_limit_bytes=vmem * 2**20, dimension_semantics=("arbitrary",) * len(grid)),
        cost_estimate=pl.CostEstimate(flops=flops, bytes_accessed=bytes_accessed, transcendentals=0),
    )(dp.reshape(1), *inputs)

def shape(dims, kind):
    return jax.ShapeDtypeStruct(dims, kind)

def norm_tile(x):
    v = x.astype(F32)
    center = v - jnp.mean(v, axis=-1, keepdims=True)
    scale = lax.rsqrt(jnp.mean(center * center, axis=-1, keepdims=True) + 1e-05)
    return center * scale, scale

def norms_body(dp, x, vec, first, second):
    normed, _ = norm_tile(x[...])
    first[...] = (normed * vec[0:1, :] + vec[1:2, :]).astype(BF16)
    second[...] = (normed * vec[2:3, :] + vec[3:4, :]).astype(BF16)

def norms(dp, x, vec):
    n, w = x.shape
    return run(norms_body, "norms", dp, [x, vec], [tile(w), whole(vec.shape)], [shape((n, w), BF16)] * 2, [tile(w)] * 2, [], (n // TILE,))

def turn(v, cos, s1, s2):
    left = v[:, :128]
    out = left * cos + pltpu.roll(left, 96, 1) * s1 + pltpu.roll(left, 32, 1) * s2
    return jnp.concatenate([out, v[:, 128:]], axis=1)

def qkv_body(dp, first, w0, wx, wy, w1, w2, bias, cos, s1, s2, q, k, v, full):
    @pl.when(pl.program_id(0) == 0)
    def _():
        fill(dp[0], full, (w0, wx, wy, w1, w2))
    joined = dot(first[...], full[...], (1, 0)) + bias[...]
    q[...] = turn(joined[:, :HEAD], cos[...], s1[...], s2[...]).astype(BF16)
    k[...] = turn(joined[:, HEAD:2 * HEAD], cos[...], s1[...], s2[...]).astype(BF16)
    v[...] = joined[:, 2 * HEAD:].astype(BF16)

def qkv(dp, first, pieces, bias, tables):
    n, w = first.shape
    return run(qkv_body, "qkv", dp, [first, *pieces, bias, *tables],
        [tile(w)] + [whole(p.shape) for p in pieces] + [whole(bias.shape)] + [tile(128)] * 3,
        [shape((n, HEAD), BF16)] * 3, [tile(HEAD)] * 3, [pltpu.VMEM((w, 3 * HEAD), BF16)], (n // TILE,), flops=2 * n * w * 3 * HEAD)

def mlp_forward_body(dp, second, u0, ux, uy, u1, u2, bias, active, slope, full):
    @pl.when(pl.program_id(0) == 0)
    def _():
        fill(dp[0], full, (u0, ux, uy, u1, u2))
    hidden = dot(second[...], full[...], (1, 0)) + bias[...]
    half_cdf = 0.5 + 0.5 * lax.erf(hidden * (1.0 / math.sqrt(2.0)))
    active[...] = (hidden * half_cdf).astype(BF16)
    slope[...] = half_cdf + hidden * (jnp.exp(-0.5 * hidden * hidden) * (1.0 / math.sqrt(2.0 * math.pi)))

def mlp_forward(dp, second, up, bias):
    n, w = second.shape
    h = up[0].shape[1]
    return run(mlp_forward_body, "mlp_forward", dp, [second, *up, bias],
        [tile(w)] + [whole(p.shape) for p in (*up, bias)],
        [shape((n, h), BF16), shape((n, h), F32)], [tile(h)] * 2,
        [pltpu.VMEM((w, h), BF16)], (n // TILE,), flops=2 * n * w * h)

def masked_scores(index, q, keys, seg_q, seg_k):
    reach = keys.shape[0]
    scores = dot(q, keys, (1, 1)) * (1.0 / math.sqrt(HEAD))
    row = index * TILE + lax.broadcasted_iota(jnp.int32, (TILE, reach), 0)
    col = lax.broadcasted_iota(jnp.int32, (TILE, reach), 1)
    allowed = (seg_q[...] == seg_k[:, 0:reach]) & (col <= row)
    return jnp.where(allowed, scores, -1e30), allowed

def each_tile(count, block):
    for index in range(count):
        @pl.when(pl.program_id(0) == index)
        def _(index=index):
            block(index, (index + 1) * TILE)

def attend_forward_body(dp, q, k, v, seg_q, seg_k, context, low, log_sum):
    def block(index, reach):
        scores, allowed = masked_scores(index, q[...], k[0:reach, :], seg_q, seg_k)
        top = jnp.max(scores, axis=1, keepdims=True)
        weights = jnp.where(allowed, jnp.exp(scores - top), 0.0)
        weight_sum = jnp.sum(weights, axis=1, keepdims=True)
        mixed = dot(weights.astype(BF16), v[0:reach, :], (1, 0)) / weight_sum
        context[...] = mixed
        low[...] = mixed.astype(BF16)
        log_sum[...] = top + jnp.log(weight_sum)
    each_tile(k.shape[0] // TILE, block)

def attend_forward(dp, q, k, v, seg_col, seg_row):
    n = q.shape[0]
    return run(attend_forward_body, "attend_forward", dp, [q, k, v, seg_col, seg_row],
        [tile(HEAD), whole(k.shape), whole(v.shape), tile(1), whole(seg_row.shape)],
        [shape((n, HEAD), F32), shape((n, HEAD), BF16), shape((n, 1), F32)],
        [tile(HEAD)] * 2 + [tile(1)], [], (n // TILE,), flops=3 * n * n * HEAD)

def output_body(dp, ctx, active, w_out, d0, dx, dy, d1, d2, out, full):
    @pl.when(pl.program_id(0) == 0)
    def _():
        fill(dp[0], full, (d0, dx, dy, d1, d2))
    out[...] = (dot(ctx[...], w_out[...], (1, 0)) + dot(active[...], full[...], (1, 0))).astype(BF16)

def output(dp, ctx, active, w_out, down):
    n, h = active.shape; w = w_out.shape[1]
    return run(output_body, "output", dp, [ctx, active, w_out, *down],
        [tile(HEAD), tile(h), whole(w_out.shape)] + [whole(p.shape) for p in down],
        [shape((n, w), BF16)], [tile(w)], [pltpu.VMEM((h, w), BF16)], (n // TILE,), flops=2 * n * w * (h + HEAD))[0]

SLAB = 512

def sections(half):
    return (
        (0, 0, 3, 0, half),
        (1, half, 3, half, half),
        (0, half, 1, 0, half),
        (1, 0, 2, half, half),
        (2, 0, 1, half, half),
        (3, 0, 2, 0, half),
        (4, 0, 0, 0, half),
        (4, half, 0, half, half),
    )

def term_shapes(rows, cols):
    counts = (rows, rows, rows // 2, rows // 2, rows)
    return [shape((count, cols), BF16) for count in counts]

class Copies:
    def __init__(self, sems):
        self.sems, self.count = sems, 0

    def start(self, source, target):
        copy = pltpu.make_async_copy(source, target, self.sems.at[self.count])
        self.count += 1
        copy.start()
        return copy

    def lay(self, dp, full, pieces):
        take, cols = full.shape[0] // 4, full.shape[1]
        cut = pieces[3].shape[0]
        copies = []
        for mask in range(3):
            at = pl.multiple_of((dp ^ mask) * take, 16)
            copies.append(
                self.start(pieces[mask].at[pl.ds(0, take), pl.ds(0, cols)], full.at[pl.ds(at, take), :])
            )
        far = (dp ^ 3) * take
        copies.append(
            self.start(pieces[3].at[:, pl.ds(0, cols)], full.at[pl.ds(pl.multiple_of(far, 16), cut), :])
        )
        copies.append(
            self.start(
                pieces[4].at[pl.ds(0, take - cut), pl.ds(0, cols)],
                full.at[pl.ds(pl.multiple_of(far + cut, 16), take - cut), :],
            )
        )
        return copies

    def slabs(self, source, target):
        return [
            self.start(source.at[pl.ds(at, SLAB), :], target.at[pl.ds(at, SLAB), :])
            for at in range(0, source.shape[0], SLAB)
        ]

    def send_terms(self, dp, staged, outs):
        rows = staged.shape[0] // 4
        sent = []
        for out, at, mask, low, count in sections(rows // 2):
            source = pl.multiple_of((dp ^ mask) * rows + low, rows // 2)
            sent.append(self.start(staged.at[pl.ds(source, count), :], outs[out].at[pl.ds(at, count), :]))
        return sent

def wait_all(copies):
    for copy in copies:
        copy.wait()

def anywhere(count):
    return [pl.BlockSpec(memory_space=pl.ANY)] * count

def middle_body(dp, *refs):
    slope, g, d0, dx, dy, d1, d2, second, context = refs[:9]
    d_hidden, sums, attn_terms = refs[9:12]
    up_outs = refs[12:17]
    s_slope, s_g, full, s_second, s_context, s_hidden, staged, s_attn, sems = refs[17:]
    me = dp[0]
    copies = Copies(sems)
    got_full = copies.lay(me, full, (d0, dx, dy, d1, d2))
    got_g, got_slope = [], []
    n = g.shape[0]
    spans = [pl.ds(at, SLAB) for at in range(0, n, SLAB)]
    for span in spans:
        got_g.append(copies.start(g.at[span, :], s_g.at[span, :]))
        got_slope.append(copies.start(slope.at[span, :], s_slope.at[span, :]))
    got_second = copies.slabs(second, s_second)
    got_context = copies.start(context, s_context)
    wait_all(got_full)
    sent = []
    total = jnp.zeros(sums.shape, F32)
    for index, span in enumerate(spans):
        got_g[index].wait()
        got_slope[index].wait()
        low = (s_slope[span, :] * dot(s_g[span, :], full[...], (1, 1))).astype(BF16)
        s_hidden[span, :] = low
        total += jnp.sum(low.astype(F32), axis=0, keepdims=True)
        sent.append(copies.start(s_hidden.at[span, :], d_hidden.at[span, :]))
    sums[...] = total
    wait_all(got_second)
    for at in range(0, staged.shape[0], 1024):
        staged[at : at + 1024, :] = dot(s_second[:, at : at + 1024], s_hidden[...], (0, 0)).astype(BF16)
    sent += copies.send_terms(me, staged, up_outs)
    got_context.wait()
    s_attn[...] = dot(s_context[...], s_g[...], (0, 0)).astype(BF16)
    sent.append(copies.start(s_attn, attn_terms))
    wait_all(sent)

def middle(dp, slope, g, down, second, context):
    n, w = second.shape
    h = slope.shape[1]
    rows = w // 4
    outs = [shape((n, h), BF16), shape((1, h), F32), shape((HEAD, w), BF16)]
    outs += term_shapes(rows, h)
    result = run(middle_body, "middle", dp, [slope, g, *down, second, context],
        anywhere(9), outs, anywhere(1) + [whole((1, h))] + anywhere(6),
        [pltpu.VMEM((n, h), F32), pltpu.VMEM((n, w), BF16), pltpu.VMEM((h, w), BF16), pltpu.VMEM((n, w), BF16),
         pltpu.VMEM((n, HEAD), BF16), pltpu.VMEM((n, h), BF16),
         pltpu.VMEM((w, h), BF16), pltpu.VMEM((HEAD, w), BF16), pltpu.SemaphoreType.DMA((40,))],
        (1,), flops=4 * n * w * h)
    return result[0], result[1], result[2], result[3:]

def last_body(dp, *refs):
    q, k, v, wide, log_sum, seg_q, seg_k, cos, s1, s2, vec = refs[:11]
    g, w_out, first, x, hidden = refs[11:16]
    w_pieces, u_pieces = refs[16:21], refs[21:26]
    sums_joined, sums_norm, u_terms = refs[26:29]
    qkv_outs = refs[29:34]
    (s_g, s_w_out, s_first, s_x, s_hidden, full_qkv, full_up,
     s_dj, dk_acc, dv_acc, staged, s_u, sems) = refs[34:]
    me = dp[0]
    copies = Copies(sems)
    got_w_out = copies.start(w_out, s_w_out)
    n = q.shape[0]
    got_g = copies.slabs(g, s_g)
    got_first = copies.slabs(first, s_first)
    got_full = copies.lay(me, full_qkv, w_pieces) + copies.lay(me, full_up, u_pieces)
    got_x = copies.slabs(x, s_x)
    got_hidden = copies.slabs(hidden, s_hidden)
    scale = 1.0 / math.sqrt(HEAD)
    dk_acc[...] = jnp.zeros_like(dk_acc)
    dv_acc[...] = jnp.zeros_like(dv_acc)
    got_w_out.wait()
    total_q = jnp.zeros((1, HEAD), F32)
    for index in range(n // TILE):
        span = pl.ds(index * TILE, TILE)
        reach = (index + 1) * TILE
        if index * TILE % SLAB == 0:
            got_g[index * TILE // SLAB].wait()
        d_ctx = dot(s_g[span, :], s_w_out[...], (1, 1)).astype(BF16)
        keys, values, queries = k[0:reach, :], v[0:reach, :], q[span, :]
        scores, allowed = masked_scores(index, queries, keys, seg_q.at[span, :], seg_k)
        probs = jnp.where(allowed, jnp.exp(scores - log_sum[span, :]), 0.0)
        delta = jnp.sum(d_ctx.astype(F32) * wide[span, :], axis=1, keepdims=True)
        d_scores = (probs * (dot(d_ctx, values, (1, 1)) - delta)).astype(BF16)
        d_q = dot(d_scores, keys, (1, 0)) * scale
        low_q = turn(d_q, cos[span, :], -s1[span, :], -s2[span, :]).astype(BF16)
        s_dj[span, 0:HEAD] = low_q
        total_q += jnp.sum(low_q.astype(F32), axis=0, keepdims=True)
        dk_acc[0:reach, :] += dot(d_scores, queries, (0, 0))
        dv_acc[0:reach, :] += dot(probs.astype(BF16), d_ctx, (0, 0))
    low_k = turn(dk_acc[...] * scale, cos[...], -s1[...], -s2[...]).astype(BF16)
    low_v = dv_acc[...].astype(BF16)
    s_dj[:, HEAD : 2 * HEAD] = low_k
    s_dj[:, 2 * HEAD :] = low_v
    sums_joined[:, 0:HEAD] = total_q
    sums_joined[:, HEAD : 2 * HEAD] = jnp.sum(low_k.astype(F32), axis=0, keepdims=True)
    sums_joined[:, 2 * HEAD :] = jnp.sum(low_v.astype(F32), axis=0, keepdims=True)
    wait_all(got_first)
    for at in range(0, staged.shape[0], 1024):
        staged[at : at + 1024, :] = dot(s_first[:, at : at + 1024], s_dj[...], (0, 0)).astype(BF16)
    sent = copies.send_terms(me, staged, qkv_outs)
    wait_all(got_full)
    sums_norm[...] = jnp.zeros_like(sums_norm)
    for index in range(n // TILE):
        span = pl.ds(index * TILE, TILE)
        if index * TILE % SLAB == 0:
            got_x[index * TILE // SLAB].wait()
            got_hidden[index * TILE // SLAB].wait()
        d_first = dot(s_dj[span, :], full_qkv[...], (1, 1))
        d_second = dot(s_hidden[span, :], full_up[...], (1, 1))
        s_u[span, :] = (d_first * vec[0:1, :] + d_second * vec[2:3, :]).astype(BF16)
        sent.append(copies.start(s_u.at[span, :], u_terms.at[span, :]))
        normed, _ = norm_tile(s_x[span, :])
        sums_norm[0:1, :] += jnp.sum(d_first * normed, axis=0, keepdims=True)
        sums_norm[1:2, :] += jnp.sum(d_first, axis=0, keepdims=True)
        sums_norm[2:3, :] += jnp.sum(d_second * normed, axis=0, keepdims=True)
        sums_norm[3:4, :] += jnp.sum(d_second, axis=0, keepdims=True)
    wait_all(sent)

def last(dp, q, k, v, wide, log_sum, seg_col, seg_row, tables, vec, g, w_out, first, x, hidden, w_in, up):
    n, w = x.shape
    h = hidden.shape[1]
    rows = w // 4
    near = [q, k, v, wide, log_sum, seg_col, seg_row, *tables, vec]
    outs = [shape((1, 3 * HEAD), F32), shape((4, w), F32), shape((n, w), BF16)]
    outs += term_shapes(rows, 3 * HEAD)
    result = run(last_body, "last", dp, [*near, g, w_out, first, x, hidden, *w_in, *up],
        [whole(a.shape) for a in near] + anywhere(15), outs,
        [whole((1, 3 * HEAD)), whole((4, w))] + anywhere(6),
        [pltpu.VMEM((n, w), BF16), pltpu.VMEM((HEAD, w), BF16), pltpu.VMEM((n, w), BF16),
         pltpu.VMEM((n, w), BF16), pltpu.VMEM((n, h), BF16), pltpu.VMEM((w, 3 * HEAD), BF16), pltpu.VMEM((w, h), BF16),
         pltpu.VMEM((n, 3 * HEAD), BF16), pltpu.VMEM((n, HEAD), F32), pltpu.VMEM((n, HEAD), F32),
         pltpu.VMEM((w, 3 * HEAD), BF16), pltpu.VMEM((n, w), BF16),
         pltpu.SemaphoreType.DMA((48,))],
        (1,), flops=2 * n * w * (4 * HEAD + 3 * HEAD + h) + 6 * n * n * HEAD)
    return result[0], result[1], result[2], result[3:]

def outward_body(dp, *refs):
    left, right, attn = refs[:3]
    outs = refs[3:8]
    s_left, s_right, s_attn, staged, sems = refs[8:]
    me = dp[0]
    copies = Copies(sems)
    got_right = copies.slabs(right, s_right)
    got_left = copies.start(left, s_left)
    got_attn = copies.start(attn, s_attn)
    rows, extra = staged.shape[0] // 4, attn.shape[1]
    half, part = rows // 2, extra // 2
    one = half + part
    wait_all(got_right)
    got_left.wait()
    staged[...] = dot(s_left[...], s_right[...], (0, 0)).astype(BF16)
    got_attn.wait()
    sent = []
    for out, at, mask, low, _ in sections(half):
        source = pl.multiple_of((me ^ mask) * rows + low, half)
        at = one if at else 0
        target = outs[out]
        sent.append(copies.start(staged.at[pl.ds(source, half), :], target.at[pl.ds(at, half), :]))
        source = part if low else 0
        sent.append(
            copies.start(
                s_attn.at[me ^ mask, pl.ds(source, part), :], target.at[pl.ds(at + half, part), :]
            )
        )
    wait_all(sent)

def outward(dp, left, right, attn):
    n, h = left.shape; w = right.shape[1]
    outs = term_shapes(h // 4 + attn.shape[1], w)
    return run(outward_body, "outward", dp, [left, right, attn], anywhere(3), outs, anywhere(5),
        [pltpu.VMEM((n, h), BF16), pltpu.VMEM((n, w), BF16), pltpu.VMEM(attn.shape, BF16),
         pltpu.VMEM((h, w), BF16), pltpu.SemaphoreType.DMA((24,))],
        (1,), flops=2 * n * h * w)


def up_blocks_body(source, out):
    for rank in range(HEADS):
        for group in range(4):
            at = (group * HEADS + rank) * 256
            out[rank, :, group * 256 : group * 256 + 256] = source[:, at : at + 256]


def qkv_blocks_body(source, packed, out):
    for rank in range(HEADS):
        for part in range(3):
            at = (part * HEADS + HEAD_ORDER[rank]) * HEAD
            out[rank, :, part * HEAD : part * HEAD + HEAD] = source[:, at : at + HEAD]
        out[rank, :, 3 * HEAD :] = packed[...]


def out_rows_body(dp, own, along_x, along_y, far, out):
    for mask, piece in enumerate((own, along_x, along_y)):
        out[dp[0] ^ mask] = piece[256:, :]
    out[dp[0] ^ 3] = far[128:, :]


def up_rows_body(source, out):
    for rank in range(HEADS):
        for group in range(4):
            at = (group * HEADS + rank) * 256
            out[:, at : at + 256] = source[rank, :, group * 256 : group * 256 + 256].astype(F32)


def qkv_rows_body(source, out):
    for rank in range(HEADS):
        for part in range(3):
            at = (part * HEADS + HEAD_ORDER[rank]) * HEAD
            out[:, at : at + HEAD] = source[rank, :, part * HEAD : part * HEAD + HEAD].astype(F32)


def repack(body, name, out, *sources):
    return pl.pallas_call(
        body,
        name=name,
        out_shape=out,
        compiler_params=pltpu.CompilerParams(vmem_limit_bytes=16 * 2**20),
        cost_estimate=pl.CostEstimate(
            flops=0,
            bytes_accessed=sources[0].size * 6,
            transcendentals=0,
        ),
    )(*sources)


def tie(value, *others):
    return lax.optimization_barrier((value, others))[0]


def stage(values, done):
    return lax.optimization_barrier((tuple(values), tuple(done)))[0]


def over_x(block):
    return lax.ppermute(block, "dp", swap(4, 1))


def over_y(block):
    return lax.ppermute(block, "dp", swap(4, 2))


def small_call(body, name, outs, *sources):
    return pl.pallas_call(
        body,
        name=name,
        out_shape=outs,
        compiler_params=pltpu.CompilerParams(vmem_limit_bytes=24 * 2**20),
        cost_estimate=pl.CostEstimate(flops=0, bytes_accessed=sources[0].size * 8, transcendentals=0),
    )(*sources)


def send_both(terms):
    return over_x(terms[0]), over_y(terms[1])


def pass_on_body(x_low, y_top, got_x, got_y, to_x, to_y):
    half = x_low.shape[0]
    to_y[...] = (y_top[...].astype(F32) + got_x[:half].astype(F32)).astype(BF16)
    to_x[...] = (x_low[...].astype(F32) + got_y[half:].astype(F32)).astype(BF16)


def pass_on(terms, got):
    out = jax.ShapeDtypeStruct(terms[2].shape, BF16)
    to_x, to_y = small_call(pass_on_body, "pass_on", (out, out), terms[2], terms[3], *got)
    return (over_x(to_x), over_y(to_y)), to_x


def reduce_last_body(own, got_x, got_y, x_low, y_top, out):
    half = x_low.shape[0]
    top = got_x[half:].astype(F32) + y_top[...].astype(F32)
    low = got_y[:half].astype(F32) + x_low[...].astype(F32)
    out[:half] = (own[:half].astype(F32) + top).astype(out.dtype)
    out[half:] = (own[half:].astype(F32) + low).astype(out.dtype)


def reduce_last(terms, got, then):
    out = jax.ShapeDtypeStruct(terms[4].shape, BF16)
    return small_call(reduce_last_body, "reduce_last", out, terms[4], *got, *then)


def reduce_both_body(own, got_x, got_y, x_low, y_top, first, second):
    one = x_low.shape[0]
    half, part = first.shape[0] // 2, second.shape[0] // 2
    top = got_x[one:].astype(F32) + y_top[...].astype(F32)
    low = got_y[:one].astype(F32) + x_low[...].astype(F32)
    for index, others in enumerate((top, low)):
        total = own[index * one : (index + 1) * one].astype(F32) + others
        first[index * half : (index + 1) * half] = total[:half]
        second[index * part : (index + 1) * part] = total[half:]


def reduce_both(terms, got, then, rows, part):
    outs = [jax.ShapeDtypeStruct((count, terms[4].shape[1]), F32) for count in (rows, part)]
    return small_call(reduce_both_body, "reduce_both", outs, terms[4], *got, *then)


def rotary_lanes(length):
    position = jnp.arange(length, dtype=jnp.int32).astype(F32)
    cosine, sine = rotary_tables(position)
    blank = jnp.zeros((length, 32), F32)
    rest = jnp.zeros((length, 64), F32)
    cos = jnp.concatenate([cosine, jnp.ones((length, 64), F32)], axis=1)
    first = jnp.concatenate([-sine[:, :32], blank, rest], axis=1)
    second = jnp.concatenate([blank, sine[:, 32:], rest], axis=1)
    return cos, first, second


def line_shards(
    block_input,
    segments,
    out_grad,
    ln1_gain,
    ln1_bias,
    w_qkv,
    b_qkv,
    w_attn_out,
    b_attn_out,
    ln2_gain,
    ln2_bias,
    w_up,
    b_up,
    w_down,
    b_down,
):
    dp, sp = lax.axis_index("dp"), lax.axis_index("sp")
    dp = dp.astype(jnp.int32)
    x_own = block_input[0]
    g_own = out_grad[0]
    tokens, width = x_own.shape
    length = tokens * HEADS
    rows = w_qkv.shape[0]
    everywhere = ("dp", "sp")
    head = head_of(sp)

    fours = [[0, 1, 2, 3], [4, 5, 6, 7]]
    x_all = lax.all_gather(x_own, "sp", axis=0, tiled=True)
    down_own = jnp.concatenate([w_down, w_attn_out], axis=0)
    down_x, down_y = over_x(down_own), over_y(down_own)
    packed = jnp.concatenate(
        [
            jnp.stack([ln1_gain, ln1_bias, ln2_gain, ln2_bias, b_attn_out, b_down]),
            b_qkv.reshape(3, 64),
            b_up.reshape(4, 64),
            segments[0].astype(BF16).reshape(2, 64),
        ]
    )
    packed = jnp.pad(packed, ((0, rows - 15), (0, 64)))
    qkv_blocks = repack(
        qkv_blocks_body, "qkv_blocks", jax.ShapeDtypeStruct((HEADS, rows, 896), BF16), w_qkv, packed
    )
    up_blocks = repack(
        up_blocks_body, "up_blocks", jax.ShapeDtypeStruct((HEADS, rows, 1024), BF16), w_up
    )
    cos, sin_one, sin_two = rotary_lanes(length)
    qkv_rows = lax.all_to_all(qkv_blocks, "sp", 0, 0, tiled=True).reshape(HEADS * rows, 896)

    cut = w_down.shape[0] // 2
    half = HEADS * rows // 2
    down_far = over_x(down_y[:cut]), over_y(down_x[cut:])
    sum_out = jnp.sum(g_own.astype(F32), axis=0)
    up_blocks, qkv_rows, down_far, cos, sin_one, sin_two, sum_out = stage(
        (up_blocks, qkv_rows, down_far, cos, sin_one, sin_two, sum_out), ()
    )
    tables = (cos, sin_one, sin_two)
    down = (down_own, down_x, down_y, *down_far)
    up_rows = lax.all_to_all(up_blocks, "sp", 0, 0, tiled=True).reshape(HEADS * rows, 1024)
    qkv_x, qkv_y = over_x(qkv_rows), over_y(qkv_rows)
    out_rows = run(
        out_rows_body, "out_rows", dp, [*down[:3], down[4]], [whole(d.shape) for d in (*down[:3], down[4])],
        shape((4, rows, width), BF16), whole((4, rows, width)), [], (1,),
    )

    qkv_x, qkv_y, out_rows = stage((qkv_x, qkv_y, out_rows), ())
    qkv_far = over_x(qkv_y[:half]), over_y(qkv_x[half:])

    up_rows, qkv_far, g_late, out_rows = stage((up_rows, qkv_far, g_own, out_rows), ())
    w_in = (qkv_rows, qkv_x, qkv_y, *qkv_far)
    g_all = lax.all_gather(g_late, "sp", axis=0, tiled=True)
    up_x, up_y = over_x(up_rows), over_y(up_rows)
    w_out = lax.all_to_all(
        out_rows, "sp", 0, 0, tiled=True, axis_index_groups=fours
    ).reshape(HEAD, width)

    small = jnp.zeros((4, HEADS, 15, 64), BF16)
    far = jnp.concatenate([piece[:, 768:832] for piece in qkv_far], axis=0)
    for mask, piece in enumerate([piece[:, 768:832] for piece in w_in[:3]] + [far]):
        small = put(small, piece.reshape(HEADS, rows, 64)[:, :15], dp ^ mask)
    small = small.reshape(32, 15, 64)
    vectors = small[:, :6].transpose(1, 0, 2).reshape(6, width).astype(F32)
    norm_vec = vectors[:4]
    bias_qkv = pick(small[:, 6:9].reshape(3, HEADS, HEAD), head, 1).astype(F32).reshape(1, 768)
    bias_up = pick(small[:, 9:13].reshape(4, HEADS, 256), sp, 1).astype(F32).reshape(1, 1024)
    seg = pick(small[:, 13:].reshape(4, length), dp).astype(F32)
    seg_col, seg_row = seg.reshape(length, 1), seg.reshape(1, length)
    first_in, second_in = norms(dp, x_all, norm_vec)
    queries, key_rows, value_rows = qkv(dp, first_in, w_in, bias_qkv, tables)

    up_x, up_y, queries = stage((up_x, up_y, queries), (bias_up, seg_col, seg_row))
    up = (up_rows, up_x, up_y, over_x(up_y[:half]), over_y(up_x[half:]))

    wide_context, context, log_sum = attend_forward(
        dp, queries, key_rows, value_rows, seg_col, seg_row
    )
    up, context = stage((up, context), ())
    active, slope = mlp_forward(dp, second_in, up, bias_up)

    out_terms = output(dp, context, active, w_out, down)
    out_sum = lax.psum_scatter(out_terms, "sp", scatter_dimension=0, tiled=True)
    d_hidden, up_sums, attn_terms, up_terms = middle(
        dp, slope, tie(g_all, out_terms), down, second_in, context
    )
    attn_sent = lax.all_to_all(
        attn_terms.reshape(4, HEAD // 4, width), "sp", 0, 0, tiled=True, axis_index_groups=fours
    )
    up_got = send_both(up_terms)
    sum_up = lax.dynamic_update_slice(
        jnp.zeros((4, HEADS, 256), F32), up_sums.reshape(4, 1, 256), (0, sp, 0)
    )
    qkv_sums, norm_sums, u_terms, qkv_terms = last(
        dp,
        tie(queries, attn_terms),
        key_rows,
        value_rows,
        wide_context,
        log_sum,
        seg_col,
        seg_row,
        tables,
        norm_vec,
        g_all,
        w_out,
        first_in,
        x_all,
        d_hidden,
        w_in,
        up,
    )
    u_terms, up_got, qkv_terms, down_left, norm_sums, attn_sent = stage(
        (u_terms, up_got, qkv_terms, active, norm_sums, attn_sent), ()
    )
    up_then, passed = pass_on(up_terms, up_got)
    qkv_terms = stage(qkv_terms, (passed,))
    qkv_got = send_both(qkv_terms)
    u_sum = lax.psum_scatter(u_terms, "sp", scatter_dimension=0, tiled=True)
    sum_qkv = lax.dynamic_update_slice(
        jnp.zeros((3, HEADS, HEAD), F32), qkv_sums.reshape(3, 1, HEAD), (0, head, 0)
    )
    totals = jnp.concatenate(
        [
            norm_sums.reshape(4, 32, 64).transpose(1, 0, 2).reshape(32, 256),
            sum_out.reshape(32, 64),
            sum_qkv.reshape(32, 192),
            sum_up.reshape(32, 256),
        ],
        axis=1,
    )
    up_sum = reduce_last(up_terms, up_got, up_then)
    down_terms = outward(dp, tie(down_left, up_sum), g_all, attn_sent)

    qkv_got, down_terms, totals = stage((qkv_got, down_terms, totals), (up_sum,))
    qkv_then, _ = pass_on(qkv_terms, qkv_got)
    down_got = send_both(down_terms)
    up_back = lax.all_to_all(up_sum.reshape(HEADS, rows, 1024), "sp", 0, 0, tiled=True)
    qkv_sum = reduce_last(qkv_terms, qkv_got, qkv_then)
    qkv_sum, out_sum = stage((qkv_sum, out_sum), (up_back,))
    qkv_back = lax.all_to_all(qkv_sum.reshape(HEADS, rows, 768), "sp", 0, 0, tiled=True)

    down_got = stage(down_got, (qkv_sum,))
    down_then, _ = pass_on(down_terms, down_got)
    grad_up = repack(
        up_rows_body, "up_rows", jax.ShapeDtypeStruct((rows, HEADS * 1024), F32), up_back
    )
    owned = lax.all_to_all(tie(totals, qkv_back), everywhere, 0, 0, tiled=True)
    down_then = stage(down_then, (owned, grad_up))
    grad_down, grad_out = reduce_both(
        down_terms, down_got, down_then, w_down.shape[0], w_attn_out.shape[0]
    )
    grad_qkv = repack(
        qkv_rows_body, "qkv_rows", jax.ShapeDtypeStruct((rows, HEADS * 768), F32), qkv_back
    )
    owned = jnp.sum(owned, axis=0)

    x_wide = x_own.astype(F32)
    block_output = (x_wide + out_sum.astype(F32) + (vectors[4] + vectors[5]))[None]
    u_wide = u_sum.astype(F32)
    normed, scale = normalize(x_wide)
    u_mean = jnp.mean(u_wide, axis=-1, keepdims=True)
    u_along = jnp.mean(u_wide * normed, axis=-1, keepdims=True)
    input_grad = (g_own.astype(F32) + (u_wide - u_mean - normed * u_along) * scale)[None]

    grad_g1, grad_s1, grad_g2, grad_s2, grad_bout = (
        owned[k * rows : (k + 1) * rows] for k in range(5)
    )
    return (
        block_output,
        input_grad,
        grad_g1,
        grad_s1,
        grad_qkv,
        owned[320:512],
        grad_out,
        grad_bout,
        grad_g2,
        grad_s2,
        grad_up,
        owned[512:],
        grad_down,
        grad_bout,
    )


def shards(*arrays):
    if (lax.axis_size("dp"), lax.axis_size("sp")) == (4, 8):
        return line_shards(*arrays)
    return any_shards(*arrays)


def solution(mesh):
    tokens = P("dp", "sp", None)
    split = P(("dp", "sp"))
    matrix = P(("dp", "sp"), None)
    return jax.shard_map(
        shards,
        mesh=mesh,
        in_specs=(
            tokens,
            P("dp", "sp"),
            tokens,
            split,
            split,
            matrix,
            split,
            matrix,
            split,
            split,
            split,
            matrix,
            split,
            matrix,
            split,
        ),
        out_specs=(
            tokens,
            tokens,
            split,
            split,
            matrix,
            split,
            matrix,
            split,
            split,
            split,
            matrix,
            split,
            matrix,
            split,
        ),
        check_vma=False,
    )
```

```python
import functools
import math

import jax
import jax.numpy as jnp
from jax import lax
from jax.experimental import pallas as pl
from jax.experimental.pallas import tpu as pltpu
from jax.sharding import PartitionSpec as P

HEADS = 8
HEAD = 256
ROT = 64
TILE = 256
BF16 = jnp.bfloat16
F32 = jnp.float32

def normalize(values):
    center = values - jnp.mean(values, axis=-1, keepdims=True)
    spread = jnp.mean(center * center, axis=-1, keepdims=True)
    scale = lax.rsqrt(spread + 1e-05)
    return center * scale, scale


def rotary_tables(positions):
    inverse_freq = 10000.0 ** (-jnp.arange(0, ROT, 2).astype(F32) / ROT)
    angles = positions[:, None] * inverse_freq[None, :]
    angles = jnp.concatenate([angles, angles], axis=1)
    return (jnp.cos(angles), jnp.sin(angles))


def rotate(values, cosine, sine):
    half_rot = ROT // 2
    rot_part = values[..., :ROT]
    turned = jnp.concatenate([-rot_part[..., half_rot:], rot_part[..., :half_rot]], axis=-1)
    rotated = rot_part * cosine + turned * sine
    return jnp.concatenate([rotated, values[..., ROT:]], axis=-1)


def pick(array, index, axis=0):
    return lax.dynamic_index_in_dim(array, index, axis, keepdims=False)


def put(array, piece, index):
    return lax.dynamic_update_slice_in_dim(array, piece[None], index, 0)


def swap(extent, mask):
    return [(i, i ^ mask) for i in range(extent)]


class AnyGrid:
    def __init__(self):
        self.dp = lax.axis_index("dp")
        self.sp = lax.axis_index("sp")
        self.dps = lax.axis_size("dp")
        self.sps = lax.axis_size("sp")
        self.parts = self.sps // HEADS
        self.part = self.sp // HEADS
        self.team = [
            [part * HEADS + rank for rank in range(HEADS)] for part in range(self.parts)
        ]
        self.peers = [
            [part * HEADS + rank for part in range(self.parts)] for rank in range(HEADS)
        ]

    def gather_dp(self, block):
        block = lax.all_gather(block, "sp", axis=0, axis_index_groups=self.peers)
        block = lax.all_gather(block, "dp", axis=0)
        return block.reshape((self.dps * self.parts,) + block.shape[2:])

    def reduce_dp(self, terms):
        block = terms.reshape((self.dps, self.parts) + terms.shape[1:])
        block = lax.psum_scatter(block, "dp", scatter_dimension=0)
        return lax.psum_scatter(
            block, "sp", scatter_dimension=0, axis_index_groups=self.peers
        ).astype(F32)

    def gather_sp(self, block):
        return lax.all_gather(block, "sp", axis=0, tiled=True, axis_index_groups=self.team)

    def reduce_sp(self, terms):
        return lax.psum_scatter(
            terms, "sp", scatter_dimension=0, tiled=True, axis_index_groups=self.team
        ).astype(F32)

    def exchange_sp(self, blocks):
        return lax.all_to_all(
            blocks, "sp", split_axis=0, concat_axis=0, tiled=True, axis_index_groups=self.team
        )

    def gather_small(self, vector):
        return lax.all_gather(vector, ("dp", "sp"), axis=0)

    def reduce_small(self, terms):
        return lax.psum_scatter(terms, ("dp", "sp"), scatter_dimension=0)

    def gather_out(self, block):
        whole = lax.all_gather(block, ("dp", "sp"), axis=0, tiled=True)
        return lax.dynamic_slice_in_dim(whole, head_of(self.sp % HEADS) * HEAD, HEAD, 0)

    def reduce_out(self, terms):
        whole = jnp.zeros((HEADS * HEAD, terms.shape[1]), terms.dtype)
        whole = lax.dynamic_update_slice_in_dim(whole, terms, head_of(self.sp % HEADS) * HEAD, 0)
        return lax.psum_scatter(
            whole, ("dp", "sp"), scatter_dimension=0, tiled=True
        ).astype(F32)

    def whole_keys(self, block):
        return lax.all_gather(block, "sp", axis=0, tiled=True, axis_index_groups=self.peers)

    def reduce_keys(self, terms):
        return lax.psum_scatter(
            terms, "sp", scatter_dimension=0, tiled=True, axis_index_groups=self.peers
        )


def head_of(rank):
    return 2 * (rank % 4) + rank // 4


HEAD_ORDER = [2 * (rank % 4) + rank // 4 for rank in range(HEADS)]
RANK_ORDER = [HEAD_ORDER.index(head) for head in range(HEADS)]


def dot(left, right, contract):
    return lax.dot_general(
        left, right, (((contract[0],), (contract[1],)), ((), ())), preferred_element_type=F32
    )


def any_shards(
    block_input,
    segments,
    out_grad,
    ln1_gain,
    ln1_bias,
    w_qkv,
    b_qkv,
    w_attn_out,
    b_attn_out,
    ln2_gain,
    ln2_bias,
    w_up,
    b_up,
    w_down,
    b_down,
):
    dps, sps = lax.axis_size("dp"), lax.axis_size("sp")
    devices = dps * sps
    grid = AnyGrid()
    groups = devices // HEADS
    x_own = block_input[0]
    g_own = out_grad[0]
    tokens, width = x_own.shape
    rows = w_qkv.shape[0]
    cols_up = b_up.shape[0]
    cols_qkv = b_qkv.shape[0]
    length = tokens * HEADS
    scale = 1.0 / math.sqrt(HEAD)

    packed = jnp.concatenate(
        [
            ln1_gain,
            ln1_bias,
            ln2_gain,
            ln2_bias,
            b_attn_out,
            b_down,
            b_qkv,
            b_up,
            segments[0].astype(BF16),
        ]
    )
    small = grid.gather_small(packed)
    vectors = [
        small[:, k * rows : (k + 1) * rows].reshape(width).astype(F32) for k in range(6)
    ]
    gain_one, shift_one, gain_two, shift_two, bias_out, bias_down = vectors
    at = 6 * rows
    rank = grid.sp % HEADS
    bias_qkv = small[:, at : at + cols_qkv].reshape(3, HEADS, HEAD)
    bias_qkv = pick(bias_qkv, head_of(rank), 1).astype(F32).reshape(3 * HEAD)
    at += cols_qkv
    bias_up = small[:, at : at + cols_up].reshape(groups, HEADS, cols_up)
    bias_up = pick(bias_up, rank, 1).astype(F32).reshape(groups * cols_up)
    at += cols_up
    seg_all = pick(small[:, at:].reshape(dps, sps * tokens), grid.dp)
    seg_mine = lax.dynamic_slice_in_dim(seg_all, grid.part * length, length, 0)

    x_all = grid.gather_sp(x_own)
    up_blocks = w_up.reshape(rows, groups, HEADS, cols_up).transpose(2, 0, 1, 3)
    up_blocks = up_blocks.reshape(HEADS, rows, groups * cols_up)
    up_rows = grid.exchange_sp(up_blocks).reshape(HEADS * rows, groups * cols_up)
    weight_down = grid.gather_dp(w_down).reshape(groups * cols_up, width)
    weight_up = grid.gather_dp(up_rows).reshape(width, groups * cols_up)
    qkv_blocks = w_qkv.reshape(rows, 3, HEADS, HEAD)
    qkv_blocks = jnp.stack([qkv_blocks[:, :, head] for head in HEAD_ORDER])
    qkv_blocks = qkv_blocks.reshape(HEADS, rows, 3 * HEAD)
    qkv_rows = grid.exchange_sp(qkv_blocks).reshape(HEADS * rows, 3 * HEAD)
    weight_qkv = grid.gather_dp(qkv_rows).reshape(width, 3 * HEAD)
    weight_out = grid.gather_out(w_attn_out)
    g_all = grid.gather_sp(g_own)

    normed, _ = normalize(x_all.astype(F32))
    first_in = (normed * gain_one + shift_one).astype(BF16)
    second_in = (normed * gain_two + shift_two).astype(BF16)

    hidden = dot(second_in, weight_up, (1, 0)) + bias_up
    active_wide, gelu_pull = jax.vjp(lambda v: jax.nn.gelu(v, approximate=False), hidden)
    active = active_wide.astype(BF16)
    d_active = dot(g_all, weight_down, (1, 1))
    d_hidden = gelu_pull(d_active)[0].astype(BF16)
    term_down = dot(active, g_all, (0, 0)).astype(BF16)
    term_up = dot(second_in, d_hidden, (0, 0)).astype(BF16)

    joined = dot(first_in, weight_qkv, (1, 0)) + bias_qkv
    position = grid.part * length + jnp.arange(length, dtype=jnp.int32)
    cosine, sine = rotary_tables(position.astype(F32))
    queries = rotate(joined[:, :HEAD], cosine, sine).astype(BF16)
    key_rows = grid.whole_keys(rotate(joined[:, HEAD : 2 * HEAD], cosine, sine).astype(BF16))
    value_rows = grid.whole_keys(joined[:, 2 * HEAD :].astype(BF16))
    key_position = jnp.arange(key_rows.shape[0], dtype=jnp.int32)
    allowed = (seg_mine[:, None] == seg_all[None, :]) & (
        key_position[None, :] <= position[:, None]
    )
    scores = jnp.where(allowed, dot(queries, key_rows, (1, 1)) * scale, -1e30)
    top = jnp.max(scores, axis=-1, keepdims=True)
    weights = jnp.where(allowed, jnp.exp(scores - top), 0.0)
    weight_sum = jnp.sum(weights, axis=-1, keepdims=True)
    log_sum = top + jnp.log(weight_sum)
    context = dot(weights.astype(BF16), value_rows, (1, 0)) / weight_sum
    context_low = context.astype(BF16)

    out_terms = dot(context_low, weight_out, (1, 0)) + dot(active, weight_down, (1, 0))
    out_sum = grid.reduce_sp(out_terms.astype(BF16))
    block_output = (x_own.astype(F32) + out_sum + (bias_out + bias_down))[None]

    d_context = dot(g_all, weight_out, (1, 1)).astype(BF16)
    row_delta = jnp.sum(d_context.astype(F32) * context, axis=-1, keepdims=True)
    probs = jnp.where(allowed, jnp.exp(scores - log_sum), 0.0)
    d_probs = dot(d_context, value_rows, (1, 1))
    d_scores = (probs * (d_probs - row_delta)).astype(BF16)
    d_queries = dot(d_scores, key_rows, (1, 0)) * scale
    d_keys = grid.reduce_keys(dot(d_scores, queries, (0, 0)) * scale)
    d_values = grid.reduce_keys(dot(probs.astype(BF16), d_context, (0, 0)))
    d_joined = jnp.concatenate(
        [rotate(d_queries, cosine, -sine), rotate(d_keys, cosine, -sine), d_values], axis=1
    ).astype(BF16)

    d_first = dot(d_joined, weight_qkv, (1, 1))
    d_second = dot(d_hidden, weight_up, (1, 1))
    u_terms = d_first * gain_one + d_second * gain_two
    u_sum = grid.reduce_sp(u_terms.astype(BF16))
    normed_own, scale_own = normalize(x_own.astype(F32))
    u_mean = jnp.mean(u_sum, axis=-1, keepdims=True)
    u_along = jnp.mean(u_sum * normed_own, axis=-1, keepdims=True)
    input_grad = (g_own.astype(F32) + (u_sum - u_mean - normed_own * u_along) * scale_own)[None]

    term_qkv = dot(first_in, d_joined, (0, 0)).astype(BF16)
    term_out = dot(context_low, g_all, (0, 0)).astype(BF16)
    grad_down = grid.reduce_dp(term_down.reshape(groups, cols_up, width))
    up_sum = grid.reduce_dp(term_up.reshape(groups, HEADS * rows, groups * cols_up))
    up_back = grid.exchange_sp(up_sum.astype(BF16).reshape(HEADS, rows, groups * cols_up))
    grad_up = (
        up_back.astype(F32)
        .reshape(HEADS, rows, groups, cols_up)
        .transpose(1, 2, 0, 3)
        .reshape(rows, devices * cols_up)
    )
    grad_out = grid.reduce_out(term_out)
    qkv_sum = grid.reduce_dp(term_qkv.reshape(groups, HEADS * rows, 3 * HEAD))
    qkv_back = grid.exchange_sp(qkv_sum.astype(BF16).reshape(HEADS, rows, 3, HEAD)).astype(F32)
    grad_qkv = jnp.stack([qkv_back[place] for place in RANK_ORDER], axis=2)
    grad_qkv = grad_qkv.reshape(rows, 3 * HEADS * HEAD)

    sum_qkv = jnp.zeros((3, HEADS, HEAD), F32)
    sum_qkv = lax.dynamic_update_slice(
        sum_qkv,
        jnp.sum(d_joined.astype(F32), axis=0).reshape(3, 1, HEAD),
        (0, head_of(rank), 0),
    )
    sum_up = jnp.zeros((groups, HEADS, cols_up), F32)
    sum_up = lax.dynamic_update_slice(
        sum_up,
        jnp.sum(d_hidden.astype(F32), axis=0).reshape(groups, 1, cols_up),
        (0, rank, 0),
    )
    totals = [
        jnp.sum(d_first * normed, axis=0),
        jnp.sum(d_first, axis=0),
        jnp.sum(d_second * normed, axis=0),
        jnp.sum(d_second, axis=0),
        jnp.sum(g_own.astype(F32), axis=0),
        sum_qkv,
        sum_up,
    ]
    totals = jnp.concatenate([total.reshape(devices, -1) for total in totals], axis=1)
    owned = grid.reduce_small(totals)
    parts = [owned[k * rows : (k + 1) * rows] for k in range(5)]
    grad_g1, grad_s1, grad_g2, grad_s2, grad_bout = parts
    grad_bqkv = owned[5 * rows : 5 * rows + cols_qkv]
    grad_bup = owned[5 * rows + cols_qkv :]
    return (
        block_output,
        input_grad,
        grad_g1,
        grad_s1,
        grad_qkv,
        grad_bqkv,
        grad_out,
        grad_bout,
        grad_g2,
        grad_s2,
        grad_up,
        grad_bup,
        grad_down,
        grad_bout,
    )


def fill(dp, full, pieces):
    own, along_x, along_y, far_one, far_two = pieces
    take, cols = full.shape[0] // 4, full.shape[1]
    cut = far_one.shape[0]
    for mask, piece in enumerate((own, along_x, along_y)):
        full[pl.ds(pl.multiple_of((dp ^ mask) * take, 16), take), :] = piece[0:take, 0:cols]
    far = (dp ^ 3) * take
    full[pl.ds(pl.multiple_of(far, 16), cut), :] = far_one[:, 0:cols]
    full[pl.ds(pl.multiple_of(far + cut, 16), take - cut), :] = far_two[0 : take - cut, 0:cols]


def whole(shape):
    return pl.BlockSpec(shape, lambda *_: (0,) * len(shape), pipeline_mode=pl.Buffered(1))

def tile(cols):
    return pl.BlockSpec((TILE, cols), lambda i, *_: (i, 0))

def run(body, name, dp, inputs, specs, outs, out_specs, scratch, grid, flops=0, vmem=56):
    bytes_accessed = sum(math.prod(a.shape) * a.dtype.itemsize for a in [*inputs, *jax.tree.leaves(outs)])
    return pl.pallas_call(
        body, name=name,
        grid_spec=pltpu.PrefetchScalarGridSpec(num_scalar_prefetch=1, grid=grid, in_specs=specs, out_specs=out_specs, scratch_shapes=scratch),
        out_shape=outs,
        compiler_params=pltpu.CompilerParams(vmem_limit_bytes=vmem * 2**20, dimension_semantics=("arbitrary",) * len(grid)),
        cost_estimate=pl.CostEstimate(flops=flops, bytes_accessed=bytes_accessed, transcendentals=0),
    )(dp.reshape(1), *inputs)

def shape(dims, kind):
    return jax.ShapeDtypeStruct(dims, kind)

def norm_tile(x):
    v = x.astype(F32)
    center = v - jnp.mean(v, axis=-1, keepdims=True)
    scale = lax.rsqrt(jnp.mean(center * center, axis=-1, keepdims=True) + 1e-05)
    return center * scale, scale

def norms_body(dp, x, vec, first, second):
    normed, _ = norm_tile(x[...])
    first[...] = (normed * vec[0:1, :] + vec[1:2, :]).astype(BF16)
    second[...] = (normed * vec[2:3, :] + vec[3:4, :]).astype(BF16)

def norms(dp, x, vec):
    n, w = x.shape
    return run(norms_body, "norms", dp, [x, vec], [tile(w), whole(vec.shape)], [shape((n, w), BF16)] * 2, [tile(w)] * 2, [], (n // TILE,))

def turn(v, cos, s1, s2):
    left = v[:, :128]
    out = left * cos + pltpu.roll(left, 96, 1) * s1 + pltpu.roll(left, 32, 1) * s2
    return jnp.concatenate([out, v[:, 128:]], axis=1)

def qkv_body(dp, first, w0, wx, wy, w1, w2, bias, cos, s1, s2, q, k, v, full):
    @pl.when(pl.program_id(0) == 0)
    def _():
        fill(dp[0], full, (w0, wx, wy, w1, w2))
    joined = dot(first[...], full[...], (1, 0)) + bias[...]
    q[...] = turn(joined[:, :HEAD], cos[...], s1[...], s2[...]).astype(BF16)
    k[...] = turn(joined[:, HEAD:2 * HEAD], cos[...], s1[...], s2[...]).astype(BF16)
    v[...] = joined[:, 2 * HEAD:].astype(BF16)

def qkv(dp, first, pieces, bias, tables):
    n, w = first.shape
    return run(qkv_body, "qkv", dp, [first, *pieces, bias, *tables],
        [tile(w)] + [whole(p.shape) for p in pieces] + [whole(bias.shape)] + [tile(128)] * 3,
        [shape((n, HEAD), BF16)] * 3, [tile(HEAD)] * 3, [pltpu.VMEM((w, 3 * HEAD), BF16)], (n // TILE,), flops=2 * n * w * 3 * HEAD)

def mlp_forward_body(dp, second, u0, ux, uy, u1, u2, bias, active, slope, full):
    @pl.when(pl.program_id(0) == 0)
    def _():
        fill(dp[0], full, (u0, ux, uy, u1, u2))
    hidden = dot(second[...], full[...], (1, 0)) + bias[...]
    half_cdf = 0.5 + 0.5 * lax.erf(hidden * (1.0 / math.sqrt(2.0)))
    active[...] = (hidden * half_cdf).astype(BF16)
    slope[...] = half_cdf + hidden * (jnp.exp(-0.5 * hidden * hidden) * (1.0 / math.sqrt(2.0 * math.pi)))

def mlp_forward(dp, second, up, bias):
    n, w = second.shape
    h = up[0].shape[1]
    return run(mlp_forward_body, "mlp_forward", dp, [second, *up, bias],
        [tile(w)] + [whole(p.shape) for p in (*up, bias)],
        [shape((n, h), BF16), shape((n, h), F32)], [tile(h)] * 2,
        [pltpu.VMEM((w, h), BF16)], (n // TILE,), flops=2 * n * w * h)

def masked_scores(index, q, keys, seg_q, seg_k):
    reach = keys.shape[0]
    scores = dot(q, keys, (1, 1)) * (1.0 / math.sqrt(HEAD))
    row = index * TILE + lax.broadcasted_iota(jnp.int32, (TILE, reach), 0)
    col = lax.broadcasted_iota(jnp.int32, (TILE, reach), 1)
    allowed = (seg_q[...] == seg_k[:, 0:reach]) & (col <= row)
    return jnp.where(allowed, scores, -1e30), allowed

def each_tile(count, block):
    for index in range(count):
        @pl.when(pl.program_id(0) == index)
        def _(index=index):
            block(index, (index + 1) * TILE)

def attend_forward_body(dp, q, k, v, seg_q, seg_k, context, low, log_sum):
    def block(index, reach):
        scores, allowed = masked_scores(index, q[...], k[0:reach, :], seg_q, seg_k)
        top = jnp.max(scores, axis=1, keepdims=True)
        weights = jnp.where(allowed, jnp.exp(scores - top), 0.0)
        weight_sum = jnp.sum(weights, axis=1, keepdims=True)
        mixed = dot(weights.astype(BF16), v[0:reach, :], (1, 0)) / weight_sum
        context[...] = mixed
        low[...] = mixed.astype(BF16)
        log_sum[...] = top + jnp.log(weight_sum)
    each_tile(k.shape[0] // TILE, block)

def attend_forward(dp, q, k, v, seg_col, seg_row):
    n = q.shape[0]
    return run(attend_forward_body, "attend_forward", dp, [q, k, v, seg_col, seg_row],
        [tile(HEAD), whole(k.shape), whole(v.shape), tile(1), whole(seg_row.shape)],
        [shape((n, HEAD), F32), shape((n, HEAD), BF16), shape((n, 1), F32)],
        [tile(HEAD)] * 2 + [tile(1)], [], (n // TILE,), flops=3 * n * n * HEAD)

def output_body(dp, ctx, active, w_out, d0, dx, dy, d1, d2, out, full):
    @pl.when(pl.program_id(0) == 0)
    def _():
        fill(dp[0], full, (d0, dx, dy, d1, d2))
    out[...] = (dot(ctx[...], w_out[...], (1, 0)) + dot(active[...], full[...], (1, 0))).astype(BF16)

def output(dp, ctx, active, w_out, down):
    n, h = active.shape; w = w_out.shape[1]
    return run(output_body, "output", dp, [ctx, active, w_out, *down],
        [tile(HEAD), tile(h), whole(w_out.shape)] + [whole(p.shape) for p in down],
        [shape((n, w), BF16)], [tile(w)], [pltpu.VMEM((h, w), BF16)], (n // TILE,), flops=2 * n * w * (h + HEAD))[0]

SLAB = 512

def sections(half):
    return (
        (0, 0, 3, 0, half),
        (1, half, 3, half, half),
        (0, half, 1, 0, half),
        (1, 0, 2, half, half),
        (2, 0, 1, half, half),
        (3, 0, 2, 0, half),
        (4, 0, 0, 0, half),
        (4, half, 0, half, half),
    )

def term_shapes(rows, cols):
    counts = (rows, rows, rows // 2, rows // 2, rows)
    return [shape((count, cols), BF16) for count in counts]

class Copies:
    def __init__(self, sems):
        self.sems, self.count = sems, 0

    def start(self, source, target):
        copy = pltpu.make_async_copy(source, target, self.sems.at[self.count])
        self.count += 1
        copy.start()
        return copy

    def lay(self, dp, full, pieces):
        take, cols = full.shape[0] // 4, full.shape[1]
        cut = pieces[3].shape[0]
        copies = []
        for mask in range(3):
            at = pl.multiple_of((dp ^ mask) * take, 16)
            copies.append(
                self.start(pieces[mask].at[pl.ds(0, take), pl.ds(0, cols)], full.at[pl.ds(at, take), :])
            )
        far = (dp ^ 3) * take
        copies.append(
            self.start(pieces[3].at[:, pl.ds(0, cols)], full.at[pl.ds(pl.multiple_of(far, 16), cut), :])
        )
        copies.append(
            self.start(
                pieces[4].at[pl.ds(0, take - cut), pl.ds(0, cols)],
                full.at[pl.ds(pl.multiple_of(far + cut, 16), take - cut), :],
            )
        )
        return copies

    def slabs(self, source, target):
        return [
            self.start(source.at[pl.ds(at, SLAB), :], target.at[pl.ds(at, SLAB), :])
            for at in range(0, source.shape[0], SLAB)
        ]

    def send_terms(self, dp, staged, outs):
        rows = staged.shape[0] // 4
        sent = []
        for out, at, mask, low, count in sections(rows // 2):
            source = pl.multiple_of((dp ^ mask) * rows + low, rows // 2)
            sent.append(self.start(staged.at[pl.ds(source, count), :], outs[out].at[pl.ds(at, count), :]))
        return sent

def wait_all(copies):
    for copy in copies:
        copy.wait()

def anywhere(count):
    return [pl.BlockSpec(memory_space=pl.ANY)] * count

def middle_body(dp, *refs):
    slope, g, d0, dx, dy, d1, d2, second, context = refs[:9]
    d_hidden, sums, attn_terms = refs[9:12]
    up_outs = refs[12:17]
    s_slope, s_g, full, s_second, s_context, s_hidden, staged, s_attn, sems = refs[17:]
    me = dp[0]
    copies = Copies(sems)
    got_full = copies.lay(me, full, (d0, dx, dy, d1, d2))
    got_g, got_slope = [], []
    n = g.shape[0]
    spans = [pl.ds(at, SLAB) for at in range(0, n, SLAB)]
    for span in spans:
        got_g.append(copies.start(g.at[span, :], s_g.at[span, :]))
        got_slope.append(copies.start(slope.at[span, :], s_slope.at[span, :]))
    got_second = copies.slabs(second, s_second)
    got_context = copies.start(context, s_context)
    wait_all(got_full)
    sent = []
    total = jnp.zeros(sums.shape, F32)
    for index, span in enumerate(spans):
        got_g[index].wait()
        got_slope[index].wait()
        low = (s_slope[span, :] * dot(s_g[span, :], full[...], (1, 1))).astype(BF16)
        s_hidden[span, :] = low
        total += jnp.sum(low.astype(F32), axis=0, keepdims=True)
        sent.append(copies.start(s_hidden.at[span, :], d_hidden.at[span, :]))
    sums[...] = total
    wait_all(got_second)
    for at in range(0, staged.shape[0], 1024):
        staged[at : at + 1024, :] = dot(s_second[:, at : at + 1024], s_hidden[...], (0, 0)).astype(BF16)
    sent += copies.send_terms(me, staged, up_outs)
    got_context.wait()
    s_attn[...] = dot(s_context[...], s_g[...], (0, 0)).astype(BF16)
    sent.append(copies.start(s_attn, attn_terms))
    wait_all(sent)

def middle(dp, slope, g, down, second, context):
    n, w = second.shape
    h = slope.shape[1]
    rows = w // 4
    outs = [shape((n, h), BF16), shape((1, h), F32), shape((HEAD, w), BF16)]
    outs += term_shapes(rows, h)
    result = run(middle_body, "middle", dp, [slope, g, *down, second, context],
        anywhere(9), outs, anywhere(1) + [whole((1, h))] + anywhere(6),
        [pltpu.VMEM((n, h), F32), pltpu.VMEM((n, w), BF16), pltpu.VMEM((h, w), BF16), pltpu.VMEM((n, w), BF16),
         pltpu.VMEM((n, HEAD), BF16), pltpu.VMEM((n, h), BF16),
         pltpu.VMEM((w, h), BF16), pltpu.VMEM((HEAD, w), BF16), pltpu.SemaphoreType.DMA((40,))],
        (1,), flops=4 * n * w * h)
    return result[0], result[1], result[2], result[3:]

def last_body(dp, *refs):
    q, k, v, wide, log_sum, seg_q, seg_k, cos, s1, s2, vec = refs[:11]
    g, w_out, first, x, hidden = refs[11:16]
    w_pieces, u_pieces = refs[16:21], refs[21:26]
    sums_joined, sums_norm, u_terms = refs[26:29]
    qkv_outs = refs[29:34]
    (s_g, s_w_out, s_first, s_x, s_hidden, full_qkv, full_up,
     s_dj, dk_acc, dv_acc, staged, s_u, sems) = refs[34:]
    me = dp[0]
    copies = Copies(sems)
    got_w_out = copies.start(w_out, s_w_out)
    n = q.shape[0]
    got_g = copies.slabs(g, s_g)
    got_first = copies.slabs(first, s_first)
    got_full = copies.lay(me, full_qkv, w_pieces) + copies.lay(me, full_up, u_pieces)
    got_x = copies.slabs(x, s_x)
    got_hidden = copies.slabs(hidden, s_hidden)
    scale = 1.0 / math.sqrt(HEAD)
    dk_acc[...] = jnp.zeros_like(dk_acc)
    dv_acc[...] = jnp.zeros_like(dv_acc)
    got_w_out.wait()
    total_q = jnp.zeros((1, HEAD), F32)
    for index in range(n // TILE):
        span = pl.ds(index * TILE, TILE)
        reach = (index + 1) * TILE
        if index * TILE % SLAB == 0:
            got_g[index * TILE // SLAB].wait()
        d_ctx = dot(s_g[span, :], s_w_out[...], (1, 1)).astype(BF16)
        keys, values, queries = k[0:reach, :], v[0:reach, :], q[span, :]
        scores, allowed = masked_scores(index, queries, keys, seg_q.at[span, :], seg_k)
        probs = jnp.where(allowed, jnp.exp(scores - log_sum[span, :]), 0.0)
        delta = jnp.sum(d_ctx.astype(F32) * wide[span, :], axis=1, keepdims=True)
        d_scores = (probs * (dot(d_ctx, values, (1, 1)) - delta)).astype(BF16)
        d_q = dot(d_scores, keys, (1, 0)) * scale
        low_q = turn(d_q, cos[span, :], -s1[span, :], -s2[span, :]).astype(BF16)
        s_dj[span, 0:HEAD] = low_q
        total_q += jnp.sum(low_q.astype(F32), axis=0, keepdims=True)
        dk_acc[0:reach, :] += dot(d_scores, queries, (0, 0))
        dv_acc[0:reach, :] += dot(probs.astype(BF16), d_ctx, (0, 0))
    low_k = turn(dk_acc[...] * scale, cos[...], -s1[...], -s2[...]).astype(BF16)
    low_v = dv_acc[...].astype(BF16)
    s_dj[:, HEAD : 2 * HEAD] = low_k
    s_dj[:, 2 * HEAD :] = low_v
    sums_joined[:, 0:HEAD] = total_q
    sums_joined[:, HEAD : 2 * HEAD] = jnp.sum(low_k.astype(F32), axis=0, keepdims=True)
    sums_joined[:, 2 * HEAD :] = jnp.sum(low_v.astype(F32), axis=0, keepdims=True)
    wait_all(got_first)
    for at in range(0, staged.shape[0], 1024):
        staged[at : at + 1024, :] = dot(s_first[:, at : at + 1024], s_dj[...], (0, 0)).astype(BF16)
    sent = copies.send_terms(me, staged, qkv_outs)
    wait_all(got_full)
    sums_norm[...] = jnp.zeros_like(sums_norm)
    for index in range(n // TILE):
        span = pl.ds(index * TILE, TILE)
        if index * TILE % SLAB == 0:
            got_x[index * TILE // SLAB].wait()
            got_hidden[index * TILE // SLAB].wait()
        d_first = dot(s_dj[span, :], full_qkv[...], (1, 1))
        d_second = dot(s_hidden[span, :], full_up[...], (1, 1))
        s_u[span, :] = (d_first * vec[0:1, :] + d_second * vec[2:3, :]).astype(BF16)
        sent.append(copies.start(s_u.at[span, :], u_terms.at[span, :]))
        normed, _ = norm_tile(s_x[span, :])
        sums_norm[0:1, :] += jnp.sum(d_first * normed, axis=0, keepdims=True)
        sums_norm[1:2, :] += jnp.sum(d_first, axis=0, keepdims=True)
        sums_norm[2:3, :] += jnp.sum(d_second * normed, axis=0, keepdims=True)
        sums_norm[3:4, :] += jnp.sum(d_second, axis=0, keepdims=True)
    wait_all(sent)

def last(dp, q, k, v, wide, log_sum, seg_col, seg_row, tables, vec, g, w_out, first, x, hidden, w_in, up):
    n, w = x.shape
    h = hidden.shape[1]
    rows = w // 4
    near = [q, k, v, wide, log_sum, seg_col, seg_row, *tables, vec]
    outs = [shape((1, 3 * HEAD), F32), shape((4, w), F32), shape((n, w), BF16)]
    outs += term_shapes(rows, 3 * HEAD)
    result = run(last_body, "last", dp, [*near, g, w_out, first, x, hidden, *w_in, *up],
        [whole(a.shape) for a in near] + anywhere(15), outs,
        [whole((1, 3 * HEAD)), whole((4, w))] + anywhere(6),
        [pltpu.VMEM((n, w), BF16), pltpu.VMEM((HEAD, w), BF16), pltpu.VMEM((n, w), BF16),
         pltpu.VMEM((n, w), BF16), pltpu.VMEM((n, h), BF16), pltpu.VMEM((w, 3 * HEAD), BF16), pltpu.VMEM((w, h), BF16),
         pltpu.VMEM((n, 3 * HEAD), BF16), pltpu.VMEM((n, HEAD), F32), pltpu.VMEM((n, HEAD), F32),
         pltpu.VMEM((w, 3 * HEAD), BF16), pltpu.VMEM((n, w), BF16),
         pltpu.SemaphoreType.DMA((48,))],
        (1,), flops=2 * n * w * (4 * HEAD + 3 * HEAD + h) + 6 * n * n * HEAD)
    return result[0], result[1], result[2], result[3:]

def outward_body(dp, *refs):
    left, right, attn = refs[:3]
    outs = refs[3:8]
    s_left, s_right, s_attn, staged, sems = refs[8:]
    me = dp[0]
    copies = Copies(sems)
    got_right = copies.slabs(right, s_right)
    got_left = copies.start(left, s_left)
    got_attn = copies.start(attn, s_attn)
    rows, extra = staged.shape[0] // 4, attn.shape[1]
    half, part = rows // 2, extra // 2
    one = half + part
    wait_all(got_right)
    got_left.wait()
    staged[...] = dot(s_left[...], s_right[...], (0, 0)).astype(BF16)
    got_attn.wait()
    sent = []
    for out, at, mask, low, _ in sections(half):
        source = pl.multiple_of((me ^ mask) * rows + low, half)
        at = one if at else 0
        target = outs[out]
        sent.append(copies.start(staged.at[pl.ds(source, half), :], target.at[pl.ds(at, half), :]))
        source = part if low else 0
        sent.append(
            copies.start(
                s_attn.at[me ^ mask, pl.ds(source, part), :], target.at[pl.ds(at + half, part), :]
            )
        )
    wait_all(sent)

def outward(dp, left, right, attn):
    n, h = left.shape; w = right.shape[1]
    outs = term_shapes(h // 4 + attn.shape[1], w)
    return run(outward_body, "outward", dp, [left, right, attn], anywhere(3), outs, anywhere(5),
        [pltpu.VMEM((n, h), BF16), pltpu.VMEM((n, w), BF16), pltpu.VMEM(attn.shape, BF16),
         pltpu.VMEM((h, w), BF16), pltpu.SemaphoreType.DMA((24,))],
        (1,), flops=2 * n * h * w)


def up_blocks_body(source, out):
    for rank in range(HEADS):
        for group in range(4):
            at = (group * HEADS + rank) * 256
            out[rank, :, group * 256 : group * 256 + 256] = source[:, at : at + 256]


def qkv_blocks_body(source, packed, out):
    for rank in range(HEADS):
        for part in range(3):
            at = (part * HEADS + HEAD_ORDER[rank]) * HEAD
            out[rank, :, part * HEAD : part * HEAD + HEAD] = source[:, at : at + HEAD]
        out[rank, :, 3 * HEAD :] = packed[...]


def out_rows_body(dp, own, along_x, along_y, far, out):
    for mask, piece in enumerate((own, along_x, along_y)):
        out[dp[0] ^ mask] = piece[256:, :]
    out[dp[0] ^ 3] = far[128:, :]


def up_rows_body(source, out):
    for rank in range(HEADS):
        for group in range(4):
            at = (group * HEADS + rank) * 256
            out[:, at : at + 256] = source[rank, :, group * 256 : group * 256 + 256].astype(F32)


def qkv_rows_body(source, out):
    for rank in range(HEADS):
        for part in range(3):
            at = (part * HEADS + HEAD_ORDER[rank]) * HEAD
            out[:, at : at + HEAD] = source[rank, :, part * HEAD : part * HEAD + HEAD].astype(F32)


def repack(body, name, out, *sources):
    return pl.pallas_call(
        body,
        name=name,
        out_shape=out,
        compiler_params=pltpu.CompilerParams(vmem_limit_bytes=16 * 2**20),
        cost_estimate=pl.CostEstimate(
            flops=0,
            bytes_accessed=sources[0].size * 6,
            transcendentals=0,
        ),
    )(*sources)


def tie(value, *others):
    return lax.optimization_barrier((value, others))[0]


def stage(values, done):
    return lax.optimization_barrier((tuple(values), tuple(done)))[0]


def over_x(block):
    return lax.ppermute(block, "dp", swap(4, 1))


def over_y(block):
    return lax.ppermute(block, "dp", swap(4, 2))


def small_call(body, name, outs, *sources):
    return pl.pallas_call(
        body,
        name=name,
        out_shape=outs,
        compiler_params=pltpu.CompilerParams(vmem_limit_bytes=24 * 2**20),
        cost_estimate=pl.CostEstimate(flops=0, bytes_accessed=sources[0].size * 8, transcendentals=0),
    )(*sources)


def send_both(terms):
    return over_x(terms[0]), over_y(terms[1])


def pass_on_body(x_low, y_top, got_x, got_y, to_x, to_y):
    half = x_low.shape[0]
    to_y[...] = (y_top[...].astype(F32) + got_x[:half].astype(F32)).astype(BF16)
    to_x[...] = (x_low[...].astype(F32) + got_y[half:].astype(F32)).astype(BF16)


def pass_on(terms, got):
    out = jax.ShapeDtypeStruct(terms[2].shape, BF16)
    to_x, to_y = small_call(pass_on_body, "pass_on", (out, out), terms[2], terms[3], *got)
    return (over_x(to_x), over_y(to_y)), to_x


def reduce_last_body(own, got_x, got_y, x_low, y_top, out):
    half = x_low.shape[0]
    top = got_x[half:].astype(F32) + y_top[...].astype(F32)
    low = got_y[:half].astype(F32) + x_low[...].astype(F32)
    out[:half] = (own[:half].astype(F32) + top).astype(out.dtype)
    out[half:] = (own[half:].astype(F32) + low).astype(out.dtype)


def reduce_last(terms, got, then):
    out = jax.ShapeDtypeStruct(terms[4].shape, BF16)
    return small_call(reduce_last_body, "reduce_last", out, terms[4], *got, *then)


def reduce_both_body(own, got_x, got_y, x_low, y_top, first, second):
    one = x_low.shape[0]
    half, part = first.shape[0] // 2, second.shape[0] // 2
    top = got_x[one:].astype(F32) + y_top[...].astype(F32)
    low = got_y[:one].astype(F32) + x_low[...].astype(F32)
    for index, others in enumerate((top, low)):
        total = own[index * one : (index + 1) * one].astype(F32) + others
        first[index * half : (index + 1) * half] = total[:half]
        second[index * part : (index + 1) * part] = total[half:]


def reduce_both(terms, got, then, rows, part):
    outs = [jax.ShapeDtypeStruct((count, terms[4].shape[1]), F32) for count in (rows, part)]
    return small_call(reduce_both_body, "reduce_both", outs, terms[4], *got, *then)


def rotary_lanes(length):
    position = jnp.arange(length, dtype=jnp.int32).astype(F32)
    cosine, sine = rotary_tables(position)
    blank = jnp.zeros((length, 32), F32)
    rest = jnp.zeros((length, 64), F32)
    cos = jnp.concatenate([cosine, jnp.ones((length, 64), F32)], axis=1)
    first = jnp.concatenate([-sine[:, :32], blank, rest], axis=1)
    second = jnp.concatenate([blank, sine[:, 32:], rest], axis=1)
    return cos, first, second


def line_shards(
    block_input,
    segments,
    out_grad,
    ln1_gain,
    ln1_bias,
    w_qkv,
    b_qkv,
    w_attn_out,
    b_attn_out,
    ln2_gain,
    ln2_bias,
    w_up,
    b_up,
    w_down,
    b_down,
):
    dp, sp = lax.axis_index("dp"), lax.axis_index("sp")
    dp = dp.astype(jnp.int32)
    x_own = block_input[0]
    g_own = out_grad[0]
    tokens, width = x_own.shape
    length = tokens * HEADS
    rows = w_qkv.shape[0]
    everywhere = ("dp", "sp")
    head = head_of(sp)

    fours = [[0, 1, 2, 3], [4, 5, 6, 7]]
    x_all = lax.all_gather(x_own, "sp", axis=0, tiled=True)
    down_own = jnp.concatenate([w_down, w_attn_out], axis=0)
    down_x, down_y = over_x(down_own), over_y(down_own)
    packed = jnp.concatenate(
        [
            jnp.stack([ln1_gain, ln1_bias, ln2_gain, ln2_bias, b_attn_out, b_down]),
            b_qkv.reshape(3, 64),
            b_up.reshape(4, 64),
            segments[0].astype(BF16).reshape(2, 64),
        ]
    )
    packed = jnp.pad(packed, ((0, rows - 15), (0, 64)))
    qkv_blocks = repack(
        qkv_blocks_body, "qkv_blocks", jax.ShapeDtypeStruct((HEADS, rows, 896), BF16), w_qkv, packed
    )
    up_blocks = repack(
        up_blocks_body, "up_blocks", jax.ShapeDtypeStruct((HEADS, rows, 1024), BF16), w_up
    )
    cos, sin_one, sin_two = rotary_lanes(length)
    qkv_rows = lax.all_to_all(qkv_blocks, "sp", 0, 0, tiled=True).reshape(HEADS * rows, 896)

    cut = w_down.shape[0] // 2
    half = HEADS * rows // 2
    down_far = over_x(down_y[:cut]), over_y(down_x[cut:])
    sum_out = jnp.sum(g_own.astype(F32), axis=0)
    up_blocks, qkv_rows, down_far, cos, sin_one, sin_two, sum_out = stage(
        (up_blocks, qkv_rows, down_far, cos, sin_one, sin_two, sum_out), ()
    )
    tables = (cos, sin_one, sin_two)
    down = (down_own, down_x, down_y, *down_far)
    up_rows = lax.all_to_all(up_blocks, "sp", 0, 0, tiled=True).reshape(HEADS * rows, 1024)
    qkv_x, qkv_y = over_x(qkv_rows), over_y(qkv_rows)
    out_rows = run(
        out_rows_body, "out_rows", dp, [*down[:3], down[4]], [whole(d.shape) for d in (*down[:3], down[4])],
        shape((4, rows, width), BF16), whole((4, rows, width)), [], (1,),
    )

    qkv_x, qkv_y, out_rows = stage((qkv_x, qkv_y, out_rows), ())
    qkv_far = over_x(qkv_y[:half]), over_y(qkv_x[half:])

    up_rows, qkv_far, g_late, out_rows = stage((up_rows, qkv_far, g_own, out_rows), ())
    w_in = (qkv_rows, qkv_x, qkv_y, *qkv_far)
    g_all = lax.all_gather(g_late, "sp", axis=0, tiled=True)
    up_x, up_y = over_x(up_rows), over_y(up_rows)
    w_out = lax.all_to_all(
        out_rows, "sp", 0, 0, tiled=True, axis_index_groups=fours
    ).reshape(HEAD, width)

    small = jnp.zeros((4, HEADS, 15, 64), BF16)
    far = jnp.concatenate([piece[:, 768:832] for piece in qkv_far], axis=0)
    for mask, piece in enumerate([piece[:, 768:832] for piece in w_in[:3]] + [far]):
        small = put(small, piece.reshape(HEADS, rows, 64)[:, :15], dp ^ mask)
    small = small.reshape(32, 15, 64)
    vectors = small[:, :6].transpose(1, 0, 2).reshape(6, width).astype(F32)
    norm_vec = vectors[:4]
    bias_qkv = pick(small[:, 6:9].reshape(3, HEADS, HEAD), head, 1).astype(F32).reshape(1, 768)
    bias_up = pick(small[:, 9:13].reshape(4, HEADS, 256), sp, 1).astype(F32).reshape(1, 1024)
    seg = pick(small[:, 13:].reshape(4, length), dp).astype(F32)
    seg_col, seg_row = seg.reshape(length, 1), seg.reshape(1, length)
    first_in, second_in = norms(dp, x_all, norm_vec)
    queries, key_rows, value_rows = qkv(dp, first_in, w_in, bias_qkv, tables)

    up_x, up_y, queries = stage((up_x, up_y, queries), (bias_up, seg_col, seg_row))
    up = (up_rows, up_x, up_y, over_x(up_y[:half]), over_y(up_x[half:]))

    wide_context, context, log_sum = attend_forward(
        dp, queries, key_rows, value_rows, seg_col, seg_row
    )
    up, context = stage((up, context), ())
    active, slope = mlp_forward(dp, second_in, up, bias_up)

    out_terms = output(dp, context, active, w_out, down)
    out_sum = lax.psum_scatter(out_terms, "sp", scatter_dimension=0, tiled=True)
    d_hidden, up_sums, attn_terms, up_terms = middle(
        dp, slope, tie(g_all, out_terms), down, second_in, context
    )
    attn_sent = lax.all_to_all(
        attn_terms.reshape(4, HEAD // 4, width), "sp", 0, 0, tiled=True, axis_index_groups=fours
    )
    up_got = send_both(up_terms)
    sum_up = lax.dynamic_update_slice(
        jnp.zeros((4, HEADS, 256), F32), up_sums.reshape(4, 1, 256), (0, sp, 0)
    )
    qkv_sums, norm_sums, u_terms, qkv_terms = last(
        dp,
        tie(queries, attn_terms),
        key_rows,
        value_rows,
        wide_context,
        log_sum,
        seg_col,
        seg_row,
        tables,
        norm_vec,
        g_all,
        w_out,
        first_in,
        x_all,
        d_hidden,
        w_in,
        up,
    )
    u_terms, up_got, qkv_terms, down_left, norm_sums, attn_sent = stage(
        (u_terms, up_got, qkv_terms, active, norm_sums, attn_sent), ()
    )
    up_then, passed = pass_on(up_terms, up_got)
    qkv_terms = stage(qkv_terms, (passed,))
    qkv_got = send_both(qkv_terms)
    u_sum = lax.psum_scatter(u_terms, "sp", scatter_dimension=0, tiled=True)
    sum_qkv = lax.dynamic_update_slice(
        jnp.zeros((3, HEADS, HEAD), F32), qkv_sums.reshape(3, 1, HEAD), (0, head, 0)
    )
    totals = jnp.concatenate(
        [
            norm_sums.reshape(4, 32, 64).transpose(1, 0, 2).reshape(32, 256),
            sum_out.reshape(32, 64),
            sum_qkv.reshape(32, 192),
            sum_up.reshape(32, 256),
        ],
        axis=1,
    )
    up_sum = reduce_last(up_terms, up_got, up_then)
    down_terms = outward(dp, tie(down_left, up_sum), g_all, attn_sent)

    qkv_got, down_terms, totals = stage((qkv_got, down_terms, totals), (up_sum,))
    qkv_then, _ = pass_on(qkv_terms, qkv_got)
    down_got = send_both(down_terms)
    up_back = lax.all_to_all(up_sum.reshape(HEADS, rows, 1024), "sp", 0, 0, tiled=True)
    qkv_sum = reduce_last(qkv_terms, qkv_got, qkv_then)
    qkv_sum, out_sum = stage((qkv_sum, out_sum), (up_back,))
    qkv_back = lax.all_to_all(qkv_sum.reshape(HEADS, rows, 768), "sp", 0, 0, tiled=True)

    down_got = stage(down_got, (qkv_sum,))
    down_then, _ = pass_on(down_terms, down_got)
    grad_up = repack(
        up_rows_body, "up_rows", jax.ShapeDtypeStruct((rows, HEADS * 1024), F32), up_back
    )
    owned = lax.all_to_all(tie(totals, qkv_back, grad_up), everywhere, 0, 0, tiled=True)
    down_then = stage(down_then, (owned, grad_up))
    grad_down, grad_out = reduce_both(
        down_terms, down_got, down_then, w_down.shape[0], w_attn_out.shape[0]
    )
    grad_qkv = repack(
        qkv_rows_body, "qkv_rows", jax.ShapeDtypeStruct((rows, HEADS * 768), F32), qkv_back
    )
    owned = jnp.sum(owned, axis=0)

    x_wide = x_own.astype(F32)
    block_output = (x_wide + out_sum.astype(F32) + (vectors[4] + vectors[5]))[None]
    u_wide = u_sum.astype(F32)
    normed, scale = normalize(x_wide)
    u_mean = jnp.mean(u_wide, axis=-1, keepdims=True)
    u_along = jnp.mean(u_wide * normed, axis=-1, keepdims=True)
    input_grad = (g_own.astype(F32) + (u_wide - u_mean - normed * u_along) * scale)[None]

    grad_g1, grad_s1, grad_g2, grad_s2, grad_bout = (
        owned[k * rows : (k + 1) * rows] for k in range(5)
    )
    return (
        block_output,
        input_grad,
        grad_g1,
        grad_s1,
        grad_qkv,
        owned[320:512],
        grad_out,
        grad_bout,
        grad_g2,
        grad_s2,
        grad_up,
        owned[512:],
        grad_down,
        grad_bout,
    )


def shards(*arrays):
    if (lax.axis_size("dp"), lax.axis_size("sp")) == (4, 8):
        return line_shards(*arrays)
    return any_shards(*arrays)


def solution(mesh):
    tokens = P("dp", "sp", None)
    split = P(("dp", "sp"))
    matrix = P(("dp", "sp"), None)
    return jax.shard_map(
        shards,
        mesh=mesh,
        in_specs=(
            tokens,
            P("dp", "sp"),
            tokens,
            split,
            split,
            matrix,
            split,
            matrix,
            split,
            split,
            split,
            matrix,
            split,
            matrix,
            split,
        ),
        out_specs=(
            tokens,
            tokens,
            split,
            split,
            matrix,
            split,
            matrix,
            split,
            split,
            split,
            matrix,
            split,
            matrix,
            split,
        ),
        check_vma=False,
    )
```
